512 devices in a mesh: seq: 64 (over z, y), head: 8 (over x, core).
Axes of the slice: x: 4, y: 4, z: 16, core: 2. Of those that a mesh axis runs over, the one named last changes fastest.
Arguments:
- grad_full: bfloat16 [65536, 8192], P('seq', 'head'), may hold values from -6 to 6
- keep: int32 [512, 16], P('seq'), may hold values from 0 to 127, as said below
- router_score: float32 [8192], P('seq'), may hold values from 0.2 to 1
- x_in: bfloat16 [8192, 8192], P('seq', 'head'), may hold values from -6 to 6
- z_in: bfloat16 [8192, 8192], P('seq', 'head'), may hold values from -6 to 6
- b_in: bfloat16 [8192, 128], P('seq'), may hold values from -4 to 4
- c_in: bfloat16 [8192, 128], P('seq'), may hold values from -4 to 4
- dt_raw: float32 [8192, 64], P('seq', 'head'), may hold values from -3 to 3
- dt_bias: float32 [64], P('head'), may hold values from -2.8 to -2.2
- a_log: float32 [64], P('head')
- d_skip: float32 [64], P('head'), may hold values from 0.5 to 1.5
- norm_gain: float32 [8192], P('head'), may hold values from 0.5 to 1.5
- state_in: float32 [64, 128, 128], P('head'), may hold values from -12 to 12
Outputs:
- grad_x: bfloat16 [8192, 8192], P('seq', 'head')
- grad_z: bfloat16 [8192, 8192], P('seq', 'head')
- grad_b: float32 [8192, 128], P('seq')
- grad_c: float32 [8192, 128], P('seq')
- grad_dt: float32 [8192, 64], P('seq', 'head')
- grad_router: float32 [8192], P('seq')
- grad_gain: float32 [8192], P('head')
- grad_alog: float32 [64], P('head')
- grad_skip: float32 [64], P('head')
The draws below stay inside these ranges and needn't reach their ends.
Inputs may be any that keep to these rules, and one draw needn't show every extreme that they name: `keep`: each row lists 16 different positions of its routing block in increasing order.
All inputs are finite; a program needn't handle non-finite values.
Results may differ from the reference program's by a relative error of at most 0.002.
Values sent between devices are 32-bit elements; how exact they have to be, the bound alone decides.
No kernel may reach another device: no remote copies, remote signals or barrier semaphores. Data moves between devices by JAX's collectives and lax.ppermute only.
A program may use at most 128 MiB of HBM per device.

```python
import jax
import jax.numpy as jnp
from jax import lax

HEADS = 64
P_SIZE = 128
N = 128
BLOCK = 128
KEEP = 16
KEPT_DEV = 128
TOKENS = 65536
KEPT = 8192
BLOCKS = 512
CH = 8192


def draw_keep(key, part):
    key = jax.random.fold_in(key, 3)
    scores = jax.random.randint(key, (BLOCKS, BLOCK), 0, 2 ** 20)
    scores = scores * BLOCK + jnp.arange(BLOCK, dtype=jnp.int32)[None, :]
    order = jnp.argsort(scores, axis=1)[:, :KEEP]
    return jnp.sort(order, axis=1).astype(jnp.int32)


def draw_a_log(key, part):
    key = jax.random.fold_in(key, 5)
    first, second = jax.random.split(key)
    share = 0.5
    slow = jax.random.uniform(first, (HEADS,), jnp.float32) < share
    spread = jax.random.uniform(second, (HEADS,), jnp.float32)
    slow_rate = jnp.exp(jnp.log(0.3 / KEPT) + spread * jnp.log(6.0))
    fast_rate = jnp.exp(jnp.log(1.0 / 50.0) + spread * jnp.log(50.0 / 30.0))
    rate = jnp.where(slow, slow_rate, fast_rate)
    return (jnp.log(rate) + jnp.log(12.5)).astype(jnp.float32)


def steps_of(rng, dims, cuts, smallest, top_value):
    loudness, own = 1.0, jax.random.fold_in(rng, 6)
    for dim, blocks in cuts:
        steps = jnp.exp(jax.random.uniform(jax.random.fold_in(own, dim), (blocks,), jnp.float32, smallest / len(cuts), top_value / len(cuts)))
        loudness = loudness * jnp.repeat(steps, dims[dim] // blocks).reshape([-1 if axis == dim else 1 for axis in range(len(dims))])
    return loudness


def noise(rng, extent, width, limit, cuts=(), kind=jnp.bfloat16):
    entries = jax.random.normal(rng, extent, jnp.float32) * width
    if len(cuts) > 0:
        entries = steps_of(rng, extent, cuts, -0.22, 0.18) * entries
    return jnp.clip(entries, min=-limit, max=limit).astype(kind)


def setup_inputs(seed: int = 0) -> dict:
    seeds = jax.random.split(jax.random.key(seed), 14)
    return {
        "grad_full": noise(seeds[0], (TOKENS, CH), 1.0, 6.0, ((0, 64), (1, 8))),
        "keep": draw_keep(jax.random.fold_in(seeds[13], 71), 0),
        "router_score": jnp.clip(0.2 + 0.8 * jax.random.uniform(seeds[2], (KEPT,), jnp.float32) ** steps_of(seeds[2], (KEPT,), ((0, 64),), -0.2, 0.2), 0.2, 1.0),
        "x_in": noise(seeds[3], (KEPT, CH), 1.0, 6.0, ((0, 64), (1, 8))),
        "z_in": noise(seeds[4], (KEPT, CH), 1.0, 6.0, ((0, 64), (1, 8))),
        "b_in": noise(seeds[5], (KEPT, N), (N ** -0.25), 4.0, ((0, 64),)),
        "c_in": noise(seeds[6], (KEPT, N), (N ** -0.25), 4.0, ((0, 64),)),
        "dt_raw": noise(seeds[7], (KEPT, HEADS), 0.7, 3.0, ((0, 64), (1, 8)), jnp.float32),
        "dt_bias": jnp.clip(-2.8 + 0.5999999 * jax.random.uniform(seeds[8], (HEADS,), jnp.float32) ** steps_of(seeds[8], (HEADS,), ((0, 8),), -0.2, 0.2), -2.8, -2.2),
        "a_log": draw_a_log(jax.random.fold_in(seeds[13], 71), 0),
        "d_skip": jnp.clip(0.5 + 1.0 * jax.random.uniform(seeds[10], (HEADS,), jnp.float32) ** steps_of(seeds[10], (HEADS,), ((0, 8),), -0.2, 0.2), 0.5, 1.5),
        "norm_gain": jnp.clip(1.0 + 0.1 * jax.random.normal(seeds[11], (CH,), jnp.float32), 0.5, 1.5),
        "state_in": noise(seeds[12], (HEADS, P_SIZE, N), 2.0, 12.0, ((0, 8),), jnp.float32),
    }


EPS = 1e-05
HIGH = lax.Precision.HIGHEST

def group_pass(state, pieces, skip, rate):
    x_rows, b_rows, c_rows, step = pieces
    logs = jnp.cumsum(step * rate[None, :], axis=0)
    count = step.shape[0]
    lower = (jnp.arange(count)[:, None] >= jnp.arange(count)[None, :])[:, :, None]
    diff = logs[:, None, :] - logs[None, :, :]
    weights = jnp.where(lower, jnp.exp(jnp.where(lower, diff, 0.0)), 0.0)
    scores = jnp.dot(c_rows, b_rows.T, precision=HIGH)
    mixed = weights * scores[:, :, None] * step[None, :, :]
    inner = jnp.einsum('tsh,shp->thp', mixed, x_rows, precision=HIGH)
    carried = jnp.einsum('hpn,tn->thp', state, c_rows, precision=HIGH) * jnp.exp(logs)[:, :, None]
    y_rows = inner + carried + skip[None, :, None] * x_rows
    tail = jnp.exp(logs[-1][None, :] - logs) * step
    scaled_rows = tail[:, :, None] * x_rows
    leaving = jnp.exp(logs[-1])[:, None, None] * state + jnp.einsum('thp,tn->hpn', scaled_rows, b_rows, precision=HIGH)
    return (leaving, y_rows)

def mix_norm(y_all, z_rows, gain, router):
    gated = y_all * z_rows * jax.nn.sigmoid(z_rows)
    rstd = lax.rsqrt(lax.optimization_barrier(jnp.mean(gated * gated, axis=1, keepdims=True)) + EPS)
    return router[:, None] * gated * rstd * gain[None, :]

def reference(grad_full, keep, router_score, x_in, z_in, b_in, c_in, dt_raw, dt_bias, a_log, d_skip, norm_gain, state_in):
    rows = (jnp.arange(BLOCKS, dtype=jnp.int32)[:, None] * BLOCK + keep).reshape(-1).astype(jnp.int32)
    upstream = jnp.take(grad_full, rows, axis=0).astype(jnp.float32)
    pieces_count = KEPT // KEPT_DEV

    def forward(x_rows, z_rows, b_rows, c_rows, raw, alog, skip, gain, router):
        step = jax.nn.softplus(raw + dt_bias[None, :])
        rate = -jnp.exp(alog)
        pieces = (x_rows.reshape(pieces_count, KEPT_DEV, HEADS, P_SIZE), b_rows.reshape(pieces_count, KEPT_DEV, N), c_rows.reshape(pieces_count, KEPT_DEV, N), step.reshape(pieces_count, KEPT_DEV, HEADS))

        def advance(state, piece):
            return group_pass(state, piece, skip, rate)
        _, ys = lax.scan(jax.checkpoint(advance), state_in, pieces)
        return mix_norm(ys.reshape(KEPT, CH), z_rows, gain, router)
    primals = (x_in.astype(jnp.float32).reshape(KEPT, HEADS, P_SIZE), z_in.astype(jnp.float32), b_in.astype(jnp.float32), c_in.astype(jnp.float32), dt_raw, a_log, d_skip, norm_gain, router_score)
    _, pullback = jax.vjp(forward, *primals)
    gx, gz, gb, gc, graw, galog, gskip, ggain, grouter = pullback(upstream)
    return (gx.reshape(KEPT, CH).astype(jnp.bfloat16), gz.astype(jnp.bfloat16), gb, gc, graw, grouter, ggain, galog, gskip)
```

```python
import functools

import jax
import jax.numpy as jnp
import numpy as np
from jax import lax
from jax.experimental import pallas as pl
from jax.experimental.pallas import tpu as pltpu
from jax.sharding import Mesh
from jax.sharding import PartitionSpec as P

EPS = 1e-05
GROUP = 4
CHUNK = 128
HP = 2
PC = 128
NS = 128
WIDE = HP * PC
F32 = jnp.float32
BF16 = jnp.bfloat16
NN = ((1,), (0,))
NT = ((1,), (1,))

X_B, X_C, X_S, ROWS_X = CHUNK, CHUNK + CHUNK // 2, 2 * CHUNK, 2 * CHUNK + 8
ROWS_Y = CHUNK + 8
HOME_S, HOME_B, HOME_C = CHUNK, CHUNK + 8, CHUNK + 8 + CHUNK // 2
ROWS_HOME = 2 * CHUNK + 8

VMEM = pl.BlockSpec(memory_space=pltpu.VMEM)
SMEM = pl.BlockSpec(memory_space=pltpu.SMEM)
ANY = pl.BlockSpec(memory_space=pl.ANY)
LIMIT = 24 * 2**20
FULL = 56 * 2**20


def mm(a, b, dims=NN):
    return lax.dot_general(a, b, (dims, ((), ())), preferred_element_type=F32)


def split(a):
    high = a.astype(BF16)
    return high, (a - high.astype(F32)).astype(BF16)


def mm_left(a, exact, dims=NN):
    high, low = split(a)
    return mm(high, exact, dims) + mm(low, exact, dims)


def mm_right(exact, b, dims=NN):
    high, low = split(b)
    return mm(exact, high, dims) + mm(exact, low, dims)


def mm_both(a, b, dims=NN):
    ah, al = split(a)
    bh, bl = split(b)
    return mm(ah, bh, dims) + (mm(ah, bl, dims) + mm(al, bh, dims))


def iota(shape, dim):
    return lax.broadcasted_iota(jnp.int32, shape, dim)


def softplus(v):
    return jnp.maximum(v, 0.0) + jnp.log1p(jnp.exp(-jnp.abs(v)))


def sigmoid(v):
    return 1.0 / (1.0 + jnp.exp(-v))


def own_heads():
    return lax.axis_index("y") * HP


def two_rows(x, row):
    odd = iota((GROUP * HP, PC), 0) % HP == 1
    at = slice(X_S + row, X_S + row + 1)
    return jnp.where(odd, x[0, at, PC:], x[0, at, :PC])


def halves(ref, k, at, count=CHUNK):
    return jnp.concatenate([ref[k, at : at + count // 2, :PC], ref[k, at : at + count // 2, PC:]], axis=0)


def token_rows(x):
    raw = jnp.concatenate(
        [x[k, X_S : X_S + 1, h * PC : (h + 1) * PC] for k in range(GROUP) for h in range(HP)], axis=0
    )
    raw = raw + two_rows(x, 1)
    step = softplus(raw)
    rate = -jnp.exp(two_rows(x, 2))
    la = step * rate
    upper = (iota((CHUNK, CHUNK), 0) <= iota((CHUNK, CHUNK), 1)).astype(F32)
    logs = jnp.dot(la, upper, precision=lax.Precision.HIGHEST, preferred_element_type=F32)
    return raw, step, rate, la, logs, logs[:, CHUNK - 1 :]


def columns(*rows):
    count = sum(r.shape[0] for r in rows)
    return jnp.concatenate(rows + (jnp.zeros((CHUNK - count, CHUNK), F32),), axis=0).T


def rows_of(cols):
    pad = jnp.zeros((CHUNK, CHUNK - len(cols)), F32)
    return jnp.concatenate(list(cols) + [pad], axis=1).T[: len(cols)]


def pair(a, b, rows):
    return jnp.concatenate(
        [jnp.broadcast_to(a, (rows, PC)), jnp.broadcast_to(b, (rows, PC))], axis=1
    )


def lanes_of(values):
    return [pair(values[k * HP : k * HP + 1], values[k * HP + 1 : k * HP + 2], 1) for k in range(GROUP)]


def pair_cols(cols, k, at=0):
    c = at + k * HP
    return pair(cols[:, c : c + 1], cols[:, c + 1 : c + 2], CHUNK)


def head_sums(a):
    return [jnp.sum(a[:, h * PC : (h + 1) * PC], axis=1, keepdims=True) for h in range(HP)]


def pack_body(x_hbm, b_hbm, c_hbm, dt_hbm, bias_hbm, alog_hbm, skip_hbm, xs, x, b, c, dt_t, bias, alog, skip, sem):
    copies = [
        pltpu.make_async_copy(src, dst, sem.at[i])
        for i, (src, dst) in enumerate(
            [(x_hbm, x), (b_hbm, b), (c_hbm, c), (dt_hbm, dt_t), (bias_hbm, bias), (alog_hbm, alog), (skip_hbm, skip)]
        )
    ]
    for copy in copies:
        copy.start()
    for copy in copies:
        copy.wait()
    half = CHUNK // 2
    odd = iota((1, WIDE), 1) >= PC
    for q in range(GROUP):
        xs[q, :CHUNK, :] = x[:, q * WIDE : (q + 1) * WIDE].astype(F32)
        for at, ref in ((X_B, b), (X_C, c)):
            xs[q, at : at + half, :PC] = ref[:half].astype(F32)
            xs[q, at : at + half, PC:] = ref[half:].astype(F32)
        row = q * HP
        tile = [jnp.concatenate([dt_t[row : row + 1, :], dt_t[row + 1 : row + 2, :]], axis=1)]
        tile += [jnp.where(odd, ref[row + 1], ref[row]) for ref in (bias, alog, skip)]
        tile += [jnp.zeros((4, WIDE), F32)]
        xs[q, X_S:, :] = jnp.concatenate(tile, axis=0)


def upstream_body(block_len, after, grad_full, keep, out):
    blocks, kept = keep.shape
    for i in range(blocks):
        pick = (iota((kept, block_len), 1) == keep[i : i + 1, :].T).astype(BF16)
        out[i * kept : (i + 1) * kept, :] = mm(pick, grad_full[i * block_len : (i + 1) * block_len, :])


def to_slices(out, at, state, rows):
    for lap in range(NS // rows):
        for h in range(HP):
            out[lap, at + h * rows : at + (h + 1) * rows, :] = state[
                lap * rows : (lap + 1) * rows, h * PC : (h + 1) * PC
            ]


def from_slices(ref, rows):
    return jnp.concatenate(
        [ref[:, h * rows : (h + 1) * rows, :].reshape(NS, PC) for h in range(HP)], axis=1
    )


def group_log(total):
    out = total[:HP]
    for k in range(1, GROUP):
        out = out + total[k * HP : (k + 1) * HP]
    return out


def own_state_body(rows, x, part, send):
    _, step, _, _, logs, total = token_rows(x)
    cols = columns(jnp.exp(total - logs) * step)
    decay = lanes_of(jnp.exp(total))
    state = jnp.zeros((NS, WIDE), F32)
    for k in range(GROUP):
        b_t = halves(x, k, X_B).T.astype(BF16)
        state = decay[k] * state + mm_right(b_t, x[k, :CHUNK, :] * pair_cols(cols, k))
        part[k] = state
    to_slices(send, 0, state, rows)
    whole = jnp.exp(group_log(total))
    extra = jnp.where(iota((8, PC), 0) == 0, whole[:1], whole[1:])
    for lap in range(NS // rows):
        send[lap, HP * rows :, :] = extra


def scan_body(rows, got, first, out, decay):
    state = [first[h * rows : (h + 1) * rows, :] for h in range(HP)]
    for lap in range(got.shape[0]):
        for h in range(HP):
            at = slice(h * rows, (h + 1) * rows)
            out[lap, at, :] = state[h]
            state[h] = got[lap, HP * rows + h : HP * rows + h + 1, :] * state[h] + got[lap, at, :]
        decay[lap] = got[lap, HP * rows :, :]


def scan_back_body(rows, got, decay, out, done):
    laps = got.shape[0]
    wide = HP * rows
    state = [jnp.zeros((rows, PC), F32) for _ in range(HP)]
    cross = [jnp.zeros((rows, PC), F32) for _ in range(HP)]
    total = jnp.zeros((8, PC), F32)
    for lap in reversed(range(laps)):
        for h in range(HP):
            at = slice(h * rows, (h + 1) * rows)
            out[lap, at, :] = state[h]
            cross[h] = cross[h] + state[h] * got[lap, wide + h * rows : wide + (h + 1) * rows, :]
            state[h] = decay[lap, h : h + 1, :] * state[h] + got[lap, at, :]
        total = total + got[lap, 2 * wide :, :]
    done[...] = total
    row = iota((8, PC), 0)
    extra = jnp.zeros((8, PC), F32)
    for h in range(HP):
        extra = extra + jnp.where(row == h, jnp.sum(cross[h], axis=0, keepdims=True), 0.0)
    for lap in range(laps):
        out[lap, wide:, :] = extra


def first_body(rows, after, state_in, out, flat):
    base = own_heads()
    for h in range(HP):
        flat[...] = state_in[base + h].T
        out[h * rows : (h + 1) * rows, :] = flat[
            pl.ds(pl.multiple_of(lax.axis_index("z") * rows, rows), rows), :
        ]


def group_states(part, enter, total):
    out, log = [enter], jnp.zeros((HP, 1), F32)
    for k in range(GROUP):
        log = log + total[k * HP : (k + 1) * HP]
        out.append(part[k] + pair(jnp.exp(log[:1]), jnp.exp(log[1:]), 1) * enter)
    return out


def rest_logs(total):
    out, log = [None] * GROUP, jnp.zeros((HP, 1), F32)
    for k in reversed(range(GROUP)):
        out[k] = log
        log = log + total[k * HP : (k + 1) * HP]
    return jnp.concatenate(out, axis=0)


def decays(logs, cols, k, h, lower):
    r = k * HP + h
    diff = cols[:, r : r + 1] - logs[r : r + 1]
    return jnp.where(lower, jnp.exp(jnp.where(lower, diff, 0.0)), 0.0)


def output_body(rows, x, part, got, y_out):
    _, step, _, _, logs, total = token_rows(x)
    cols = columns(logs, jnp.exp(logs))
    lower = iota((CHUNK, CHUNK), 0) >= iota((CHUNK, CHUNK), 1)
    states = group_states(part, from_slices(got, rows), total)
    d = x[0, X_S + 3 : X_S + 4, :]
    for k in range(GROUP):
        b = halves(x, k, X_B).astype(BF16)
        c = halves(x, k, X_C).astype(BF16)
        xk = x[k, :CHUNK, :]
        scores = mm(c, b, NT)
        inner = []
        for h in range(HP):
            r = k * HP + h
            mixed = decays(logs, cols, k, h, lower) * scores * step[r : r + 1]
            inner.append(mm_left(mixed, xk[:, h * PC : (h + 1) * PC].astype(BF16)))
        carried = mm_right(c, states[k]) * pair_cols(cols, k, GROUP * HP)
        y_out[k] = jnp.concatenate(inner, axis=1) + carried + d * xk


def norm_body(y, z, up, gain, stats):
    squares = jnp.zeros((CHUNK, 1), F32)
    crosses = jnp.zeros((CHUNK, 1), F32)
    for q in range(GROUP):
        at = slice(q * WIDE, (q + 1) * WIDE)
        zq = z[:, at].astype(F32)
        gated = y[q] * zq * sigmoid(zq)
        squares = squares + jnp.sum(gated * gated, axis=1, keepdims=True)
        crosses = crosses + jnp.sum(up[:, at] * gated * gain[:, at], axis=1, keepdims=True)
    both = rows_of([squares, crosses])
    tile = jnp.concatenate([both, jnp.zeros((6, CHUNK), F32)], axis=0)
    stats[...] = jnp.broadcast_to(tile[None], stats.shape)


def norm_back_body(total_width, stats, y, z, up, gain, router, gz, gy, router_grad):
    sums = stats[0, :2, :]
    for q in range(1, stats.shape[0]):
        sums = sums + stats[q, :2, :]
    rstd = lax.rsqrt(sums[:1] / total_width + EPS)
    cross = sums[1:]
    router_grad[...] = rstd * cross
    cols = columns(rstd * router[...], rstd * rstd * rstd * (router[...] * cross / total_width))
    for q in range(GROUP):
        at = slice(q * WIDE, (q + 1) * WIDE)
        zq = z[:, at].astype(F32)
        sig = sigmoid(zq)
        gate = zq * sig
        gated = y[q] * gate
        scaled = cols[:, :1] * up[:, at]
        gg = scaled * gain[:, at] - gated * cols[:, 1:2]
        gz[:, at] = (gg * y[q] * sig * (1.0 + zq * (1.0 - sig))).astype(BF16)
        gy[q, :CHUNK, :] = gg * gate
        gy[q, CHUNK:, :] = jnp.broadcast_to(jnp.sum(scaled * gated, axis=0, keepdims=True), (8, WIDE))


def sum_body(got, out):
    total = got[0]
    for q in range(1, got.shape[0]):
        total = total + got[q]
    out[...] = jnp.broadcast_to(total[None], out.shape)


def tangent_body(rows, after, x, part, got, out):
    _, step, _, _, logs, total = token_rows(x)
    rest = rest_logs(total)
    cols = columns(jnp.exp(total - logs + rest) * step * logs)
    near = lanes_of(jnp.exp(rest) * total)
    states = group_states(part, from_slices(got, rows), total)
    tangent = jnp.zeros((NS, WIDE), F32)
    for k in range(GROUP):
        b_t = halves(x, k, X_B).T.astype(BF16)
        scaled = x[k, :CHUNK, :] * pair_cols(cols, k)
        tangent = tangent + near[k] * states[k + 1] - mm_right(b_t, scaled)
    to_slices(out, 0, tangent, rows)


def output_back_body(rows, x, gy_in, y_in, part, got, tangent, gx_out, db_out, dc_out, send, small):
    raw, step, rate, la, logs, total = token_rows(x)
    cols = columns(logs, jnp.exp(logs), jnp.exp(total - logs), step)
    n = GROUP * HP
    lower = iota((CHUNK, CHUNK), 0) >= iota((CHUNK, CHUNK), 1)
    upper = iota((CHUNK, CHUNK), 0) <= iota((CHUNK, CHUNK), 1)
    states = group_states(part, from_slices(got, rows), total)
    d = x[0, X_S + 3 : X_S + 4, :]
    decay = lanes_of(jnp.exp(total))
    gain_part = jnp.zeros((1, WIDE), F32)
    skip_part = jnp.zeros((1, WIDE), F32)
    dots, xv, ends = [None] * n, [None] * n, [None] * n
    own = jnp.zeros((NS, WIDE), F32)
    for k in reversed(range(GROUP)):
        b = halves(x, k, X_B).astype(BF16)
        c32 = halves(x, k, X_C)
        c = c32.astype(BF16)
        xk, y, gy = x[k, :CHUNK, :], y_in[k], gy_in[k, :CHUNK, :]
        gain_part = gain_part + gy_in[k, CHUNK : CHUNK + 1, :]
        skip_part = skip_part + jnp.sum(gy * xk, axis=0, keepdims=True)
        dots[k * HP : (k + 1) * HP] = head_sums(gy * (y - d * xk))
        scores_t = mm(b, c, NT)
        dscores = jnp.zeros((CHUNK, CHUNK), F32)
        inner = []
        for h in range(HP):
            r = k * HP + h
            sl = slice(h * PC, (h + 1) * PC)
            gh, gl = split(gy[:, sl])
            xh = xk[:, sl].astype(BF16)
            dmixed = mm(gh, xh, NT) + mm(gl, xh, NT)
            dscores = dscores + decays(logs, cols, k, h, lower) * dmixed * step[r : r + 1]
            diff = logs[r : r + 1] - cols[:, r : r + 1]
            mixed_t = jnp.where(upper, jnp.exp(jnp.where(upper, diff, 0.0)), 0.0) * scores_t
            mh, ml = split(mixed_t)
            inner.append(mm(mh, gh) + (mm(mh, gl) + mm(ml, gh)))
        tail = pair_cols(cols, k, 2 * n)
        stepc = pair_cols(cols, k, 3 * n)
        oh, ol = split(own)
        v = jnp.concatenate(inner, axis=1) + tail * (mm(b, oh) + mm(b, ol))
        gx_out[k] = stepc * v + d * gy
        xv[k * HP : (k + 1) * HP] = head_sums(xk * v)
        ends[k * HP : (k + 1) * HP] = [
            jnp.sum(e, axis=0, keepdims=True) for e in head_sums(own * states[k + 1])
        ]
        sh, sl = split(tail * stepc * xk)
        db_out[k] = mm_left(dscores.T, c) + (mm(sh, oh, NT) + (mm(sh, ol, NT) + mm(sl, oh, NT)))
        eg = pair_cols(cols, k, n) * gy
        dc_out[k] = mm_left(dscores, b) + mm_both(eg, states[k], NT)
        own = decay[k] * own + mm_right(c32.T.astype(BF16), eg)
    xv = rows_of(xv)
    after = (iota((CHUNK, CHUNK), 0) >= iota((CHUNK, CHUNK), 1)).astype(F32)
    dla = jnp.dot(rows_of(dots) - step * xv, after, precision=lax.Precision.HIGHEST, preferred_element_type=F32)
    dla = dla + jnp.concatenate(ends, axis=0)
    small[:n] = dla
    small[n:] = xv
    to_slices(send, 0, own, rows)
    send[:, HP * rows : 2 * HP * rows, :] = tangent[...]
    decayed = dla * la
    odd = iota((n, 1), 0) % HP
    extra = jnp.concatenate(
        [gain_part[:, :PC], gain_part[:, PC:], skip_part[:, :PC], skip_part[:, PC:]]
        + [jnp.sum(jnp.where(odd == h, decayed, 0.0), axis=0, keepdims=True) for h in range(HP)]
        + [jnp.zeros((2, PC), F32)], axis=0,
    )
    for lap in range(NS // rows):
        send[lap, 2 * HP * rows :, :] = extra


def input_back_body(rows, x, gx_in, part, got, late, done, small, db_in, dc_in, home):
    raw, step, rate, la, logs, total = token_rows(x)
    n = GROUP * HP
    rest = rest_logs(total)
    cols = columns(jnp.exp(total - logs + rest), step)
    states = group_states(part, from_slices(got, rows), total)
    reach = lanes_of(jnp.exp(rest))
    grad = from_slices(late, rows)
    gh, gl = split(grad)
    ends, xv = [], []
    half = CHUNK // 2
    for k in range(GROUP):
        b = halves(x, k, X_B).astype(BF16)
        xk = x[k, :CHUNK, :]
        tail = pair_cols(cols, k)
        stepc = pair_cols(cols, k, n)
        v = tail * (mm(b, gh) + mm(b, gl))
        home[k, :CHUNK, :] = gx_in[k] + stepc * v
        sh, sl = split(tail * stepc * xk)
        db = db_in[k] + (mm(sh, gh, NT) + (mm(sh, gl, NT) + mm(sl, gh, NT)))
        for at, grad_map in ((HOME_B, db), (HOME_C, dc_in[k])):
            home[k, at : at + half, :PC] = grad_map[:half]
            home[k, at : at + half, PC:] = grad_map[half:]
        xv += head_sums(xk * v)
        ends += [jnp.sum(e, axis=0, keepdims=True) for e in head_sums(reach[k] * grad * states[k + 1])]
    xv = rows_of(xv)
    after = (iota((CHUNK, CHUNK), 0) >= iota((CHUNK, CHUNK), 1)).astype(F32)
    dla = jnp.dot(-step * xv, after, precision=lax.Precision.HIGHEST, preferred_element_type=F32)
    dla = small[:n] + dla + jnp.concatenate(ends, axis=0)
    ddt = (dla * rate + small[n:] + xv) * sigmoid(raw)
    alog_rows = done[4:6, :]
    for lap in range(late.shape[0]):
        alog_rows = alog_rows + late[lap, HP * rows : HP * rows + HP, :]
    shared = jnp.concatenate(
        [jnp.concatenate([done[i : i + 1, :], done[i + 1 : i + 2, :]], axis=1) for i in (0, 2)]
        + [jnp.concatenate([alog_rows[:1], alog_rows[1:]], axis=1), jnp.zeros((4, WIDE), F32)], axis=0,
    )
    for k in range(GROUP):
        own = jnp.concatenate([ddt[k * HP : k * HP + 1], ddt[k * HP + 1 : k * HP + 2]], axis=1)
        home[k, HOME_S:HOME_B, :] = jnp.concatenate([own, shared], axis=0)


def summed(block, lo, hi):
    got = block[0, lo:hi, :]
    for q in range(1, GROUP):
        got = got + block[q, lo:hi, :]
    return got


def home_body(block, gx, ddt, gain, alog, skip, send):
    lane = iota((1, GROUP * HP), 1)
    a = jnp.zeros((1, GROUP * HP), F32)
    s = jnp.zeros((1, GROUP * HP), F32)
    for q in range(GROUP):
        gx[:, q * WIDE : (q + 1) * WIDE] = block[q, :CHUNK, :].astype(BF16)
        gain[:, q * WIDE : (q + 1) * WIDE] = block[q, HOME_S + 1 : HOME_S + 2, :]
        for h in range(HP):
            sl = slice(h * PC, (h + 1) * PC)
            ddt[q * HP + h : q * HP + h + 1, :] = block[q, HOME_S : HOME_S + 1, sl]
            here = lane == q * HP + h
            s = s + jnp.where(here, jnp.sum(block[q, HOME_S + 2 : HOME_S + 3, sl], axis=1, keepdims=True), 0.0)
            a = a + jnp.where(here, jnp.sum(block[q, HOME_S + 3 : HOME_S + 4, sl], axis=1, keepdims=True), 0.0)
    alog[...] = a
    skip[...] = s
    ranks = send.shape[0]
    rows = CHUNK // ranks
    for i, at in enumerate((HOME_B, HOME_C)):
        got = summed(block, at, at + CHUNK // 2)
        both = jnp.concatenate([got[:, :PC], got[:, PC:]], axis=0)
        for j in range(ranks):
            send[j, i * rows : (i + 1) * rows, :] = both[j * rows : (j + 1) * rows]


def maps_body(got, db, dc):
    ranks = got.shape[0]
    rows = CHUNK // ranks
    for i in range(ranks):
        db[i * rows : (i + 1) * rows, :] = got[i, :rows, :]
        dc[i * rows : (i + 1) * rows, :] = got[i, rows:, :]


def call(body, ins, outs, scratch=(), limit=LIMIT):
    out = pl.pallas_call(
        body,
        in_specs=ins,
        out_specs=[VMEM] * len(outs),
        out_shape=[jax.ShapeDtypeStruct(s, t) for s, t in outs],
        scratch_shapes=scratch,
        compiler_params=pltpu.CompilerParams(vmem_limit_bytes=limit),
    )
    return out


def swap(a, axis):
    return lax.all_to_all(a, axis, 0, 0, tiled=True)


def shards(
    grad_full, keep, router_score, x_in, z_in, b_in, c_in, dt_raw, dt_bias, a_log, d_skip, norm_gain, state_in,
):
    laps = lax.axis_size("z")
    ranks = lax.axis_size("head")
    heads = dt_raw.shape[1]
    width = x_in.shape[1]
    total_width = width * ranks
    block_len = grad_full.shape[0] // keep.shape[0]
    big = ((GROUP, CHUNK, WIDE), F32)
    states = ((GROUP, NS, WIDE), F32)
    rows = NS // laps
    wide = HP * rows
    bind = functools.partial
    dma = pltpu.SemaphoreType.DMA

    router = router_score.reshape(1, CHUNK)
    gain = norm_gain.reshape(1, width)
    (xs,) = call(
        pack_body, [ANY] * 7, [((GROUP, ROWS_X, WIDE), F32)],
        [
            pltpu.VMEM((CHUNK, width), BF16), pltpu.VMEM((CHUNK, NS), BF16), pltpu.VMEM((CHUNK, NS), BF16),
            pltpu.VMEM((heads, CHUNK), F32), pltpu.SMEM((heads,), F32), pltpu.SMEM((heads,), F32),
            pltpu.SMEM((heads,), F32), dma((7,)),
        ], FULL,
    )(x_in, b_in, c_in, dt_raw.T, dt_bias, a_log, d_skip)
    x = swap(xs, "y")
    (up,) = call(bind(upstream_body, block_len), [ANY] + [VMEM] * 2, [((CHUNK, width), F32)])(xs, grad_full, keep)
    (first,) = call(bind(first_body, rows), [ANY, VMEM], [((wide, PC), F32)], [pltpu.VMEM((NS, PC), F32)])(
        xs, state_in
    )

    part, send = call(bind(own_state_body, rows), [VMEM], [states, ((laps, wide + 8, PC), F32)])(x)
    got = swap(send, "z")
    send, decay = call(bind(scan_body, rows), [VMEM] * 2, [((laps, wide, PC), F32), ((laps, 8, PC), F32)])(got, first)
    enter = swap(send, "z")

    (y,) = call(bind(output_body, rows), [VMEM] * 3, [big])(x, part, enter)
    y_home = swap(y, "y")
    (stats,) = call(norm_body, [VMEM] * 4, [((ranks, 8, CHUNK), F32)])(y_home, z_in, up, gain)
    (tangent,) = call(bind(tangent_body, rows), [ANY] + [VMEM] * 3, [((laps, wide, PC), F32)])(stats, x, part, enter)
    stats = swap(stats, "head")
    grad_z, gy, router_grad = call(
        bind(norm_back_body, total_width), [VMEM] * 6,
        [((CHUNK, width), BF16), ((GROUP, ROWS_Y, WIDE), F32), ((1, CHUNK), F32)],
    )(stats, y_home, z_in, up, gain, router)
    gx, db, dc, send, small = call(
        bind(output_back_body, rows), [VMEM] * 6,
        [
            big, ((GROUP, CHUNK, NS), F32), ((GROUP, CHUNK, NS), F32), ((laps, 2 * wide + 8, PC), F32),
            ((2 * GROUP * HP, CHUNK), F32),
        ],
    )(x, swap(gy, "y"), y, part, enter, tangent)
    got = swap(send, "z")
    send, done = call(bind(scan_back_body, rows), [VMEM] * 2, [((laps, wide + 8, PC), F32), ((8, PC), F32)])(got, decay)
    late = swap(send, "z")

    (home,) = call(bind(input_back_body, rows), [VMEM] * 9, [((GROUP, ROWS_HOME, WIDE), F32)])(
        x, gx, part, enter, late, done, small, db, dc
    )
    piece = ((ranks, 2 * CHUNK // ranks, NS), F32)
    grad_x, ddt, grad_gain, grad_alog, grad_skip, send = call(
        home_body, [VMEM],
        [
            ((CHUNK, width), BF16), ((heads, CHUNK), F32), ((1, width), F32), ((1, heads), F32),
            ((1, heads), F32), piece,
        ],
    )(swap(home, "y"))
    (send,) = call(sum_body, [VMEM], [piece])(swap(send, "head"))
    grad_b, grad_c = call(maps_body, [VMEM], [((CHUNK, NS), F32)] * 2)(swap(send, "head"))
    return (
        grad_x,
        grad_z,
        grad_b,
        grad_c,
        ddt.T,
        router_grad.reshape(CHUNK),
        grad_gain.reshape(width),
        grad_alog.reshape(heads),
        grad_skip.reshape(heads),
    )


def solution(mesh):
    count, heads = mesh.devices.shape
    inner = Mesh(mesh.devices.reshape(count // GROUP, GROUP, heads), ("z", "y", "head"))
    seq = ("z", "y")
    in_specs = (
        P(seq, "head"),
        P(seq, None),
        P(seq),
        P(seq, "head"),
        P(seq, "head"),
        P(seq, None),
        P(seq, None),
        P(seq, "head"),
        P("head"),
        P("head"),
        P("head"),
        P("head"),
        P("head", None, None),
    )
    out_specs = (
        P(seq, "head"),
        P(seq, "head"),
        P(seq, None),
        P(seq, None),
        P(seq, "head"),
        P(seq),
        P("head"),
        P("head"),
        P("head"),
    )
    return jax.shard_map(shards, mesh=inner, in_specs=in_specs, out_specs=out_specs, check_vma=False)
```

```python
import functools

import jax
import jax.numpy as jnp
import numpy as np
from jax import lax
from jax.experimental import pallas as pl
from jax.experimental.pallas import tpu as pltpu
from jax.sharding import Mesh
from jax.sharding import PartitionSpec as P

EPS = 1e-05
GROUP = 4
CHUNK = 128
HP = 2
PC = 128
NS = 128
WIDE = HP * PC
F32 = jnp.float32
BF16 = jnp.bfloat16
NN = ((1,), (0,))
NT = ((1,), (1,))

X_B, X_C, X_S, ROWS_X = CHUNK, CHUNK + CHUNK // 2, 2 * CHUNK, 2 * CHUNK + 8
ROWS_Y = CHUNK + 8
HOME_S, HOME_B, HOME_C = CHUNK, CHUNK + 8, CHUNK + 8 + CHUNK // 2
ROWS_HOME = 2 * CHUNK + 8

VMEM = pl.BlockSpec(memory_space=pltpu.VMEM)
SMEM = pl.BlockSpec(memory_space=pltpu.SMEM)
ANY = pl.BlockSpec(memory_space=pl.ANY)
LIMIT = 24 * 2**20
FULL = 56 * 2**20


def mm(a, b, dims=NN):
    return lax.dot_general(a, b, (dims, ((), ())), preferred_element_type=F32)


def split(a):
    high = a.astype(BF16)
    return high, (a - high.astype(F32)).astype(BF16)


def mm_left(a, exact, dims=NN):
    high, low = split(a)
    return mm(high, exact, dims) + mm(low, exact, dims)


def mm_right(exact, b, dims=NN):
    high, low = split(b)
    return mm(exact, high, dims) + mm(exact, low, dims)


def mm_both(a, b, dims=NN):
    ah, al = split(a)
    bh, bl = split(b)
    return mm(ah, bh, dims) + (mm(ah, bl, dims) + mm(al, bh, dims))


def iota(shape, dim):
    return lax.broadcasted_iota(jnp.int32, shape, dim)


def softplus(v):
    return jnp.maximum(v, 0.0) + jnp.log1p(jnp.exp(-jnp.abs(v)))


def sigmoid(v):
    return 1.0 / (1.0 + jnp.exp(-v))


def own_heads():
    return lax.axis_index("y") * HP


def two_rows(x, row):
    odd = iota((GROUP * HP, PC), 0) % HP == 1
    at = slice(X_S + row, X_S + row + 1)
    return jnp.where(odd, x[0, at, PC:], x[0, at, :PC])


def halves(ref, k, at, count=CHUNK):
    return jnp.concatenate([ref[k, at : at + count // 2, :PC], ref[k, at : at + count // 2, PC:]], axis=0)


def token_rows(x):
    raw = jnp.concatenate(
        [x[k, X_S : X_S + 1, h * PC : (h + 1) * PC] for k in range(GROUP) for h in range(HP)], axis=0
    )
    raw = raw + two_rows(x, 1)
    step = softplus(raw)
    rate = -jnp.exp(two_rows(x, 2))
    la = step * rate
    upper = (iota((CHUNK, CHUNK), 0) <= iota((CHUNK, CHUNK), 1)).astype(F32)
    logs = jnp.dot(la, upper, precision=lax.Precision.HIGHEST, preferred_element_type=F32)
    return raw, step, rate, la, logs, logs[:, CHUNK - 1 :]


def columns(*rows):
    count = sum(r.shape[0] for r in rows)
    return jnp.concatenate(rows + (jnp.zeros((CHUNK - count, CHUNK), F32),), axis=0).T


def rows_of(cols):
    pad = jnp.zeros((CHUNK, CHUNK - len(cols)), F32)
    return jnp.concatenate(list(cols) + [pad], axis=1).T[: len(cols)]


def pair(a, b, rows):
    return jnp.concatenate(
        [jnp.broadcast_to(a, (rows, PC)), jnp.broadcast_to(b, (rows, PC))], axis=1
    )


def lanes_of(values):
    return [pair(values[k * HP : k * HP + 1], values[k * HP + 1 : k * HP + 2], 1) for k in range(GROUP)]


def pair_cols(cols, k, at=0):
    c = at + k * HP
    return pair(cols[:, c : c + 1], cols[:, c + 1 : c + 2], CHUNK)


def head_sums(a):
    return [jnp.sum(a[:, h * PC : (h + 1) * PC], axis=1, keepdims=True) for h in range(HP)]


def pack_body(x_hbm, b_hbm, c_hbm, dt_hbm, bias_hbm, alog_hbm, skip_hbm, xs, x, b, c, dt_t, bias, alog, skip, sem):
    copies = [
        pltpu.make_async_copy(src, dst, sem.at[i])
        for i, (src, dst) in enumerate(
            [(x_hbm, x), (b_hbm, b), (c_hbm, c), (dt_hbm, dt_t), (bias_hbm, bias), (alog_hbm, alog), (skip_hbm, skip)]
        )
    ]
    for copy in copies:
        copy.start()
    for copy in copies:
        copy.wait()
    half = CHUNK // 2
    odd = iota((1, WIDE), 1) >= PC
    for q in range(GROUP):
        xs[q, :CHUNK, :] = x[:, q * WIDE : (q + 1) * WIDE].astype(F32)
        for at, ref in ((X_B, b), (X_C, c)):
            xs[q, at : at + half, :PC] = ref[:half].astype(F32)
            xs[q, at : at + half, PC:] = ref[half:].astype(F32)
        row = q * HP
        tile = [jnp.concatenate([dt_t[row : row + 1, :], dt_t[row + 1 : row + 2, :]], axis=1)]
        tile += [jnp.where(odd, ref[row + 1], ref[row]) for ref in (bias, alog, skip)]
        tile += [jnp.zeros((4, WIDE), F32)]
        xs[q, X_S:, :] = jnp.concatenate(tile, axis=0)


def to_slices(out, at, state):
    rows = NS // out.shape[0]
    for n in range(NS):
        tile = slice((at + n % rows) * PC, (at + n % rows + 1) * PC)
        out[n // rows, :, tile] = jnp.concatenate([state[n : n + 1, :PC], state[n : n + 1, PC:]], axis=0)


def from_slices(ref, out):
    rows = NS // ref.shape[0]
    for n in range(NS):
        tile = slice(n % rows * PC, (n % rows + 1) * PC)
        for h in range(HP):
            out[n : n + 1, h * PC : (h + 1) * PC] = ref[n // rows, h : h + 1, tile]


def group_log(total):
    out = total[:HP]
    for k in range(1, GROUP):
        out = out + total[k * HP : (k + 1) * HP]
    return out


def own_state_body(block_len, x, grad_full, keep, part, send, up):
    _, step, _, _, logs, total = token_rows(x)
    cols = columns(jnp.exp(total - logs) * step)
    decay = lanes_of(jnp.exp(total))
    state = jnp.zeros((NS, WIDE), F32)
    for k in range(GROUP):
        b_t = halves(x, k, X_B).T.astype(BF16)
        state = decay[k] * state + mm_right(b_t, x[k, :CHUNK, :] * pair_cols(cols, k))
        part[k] = state
    to_slices(send, 0, state)
    whole = jnp.broadcast_to(jnp.exp(group_log(total)), (HP, PC))
    for lap in range(send.shape[0]):
        send[lap, :, send.shape[2] - PC :] = whole
    blocks, kept = keep.shape
    for i in range(blocks):
        pick = (iota((kept, block_len), 1) == keep[i : i + 1, :].T).astype(BF16)
        up[i * kept : (i + 1) * kept, :] = mm(pick, grad_full[i * block_len : (i + 1) * block_len, :])


def spread(row, count):
    return jnp.concatenate([row] * count, axis=1)


def scan_body(got, state_in, out, decay, flat, first):
    laps, _, lanes = out.shape
    rows = lanes // PC
    base = own_heads()
    for h in range(HP):
        flat[...] = state_in[base + h].T
        for j in range(rows):
            first[h : h + 1, j * PC : (j + 1) * PC] = flat[pl.ds(lax.axis_index("z") * rows + j, 1), :]
    state = first[...]
    for lap in range(laps):
        out[lap] = state
        factor = got[lap, :, lanes:]
        decay[lap] = factor
        state = spread(factor, rows) * state + got[lap, :, :lanes]


def scan_back_body(got, decay, out, done):
    laps = got.shape[0]
    lanes = out.shape[2] - PC
    rows = lanes // PC
    state = jnp.zeros((HP, lanes), F32)
    cross = jnp.zeros((HP, lanes), F32)
    total = jnp.zeros((HP, 3 * PC), F32)
    for lap in reversed(range(laps)):
        out[lap, :, :lanes] = state
        cross = cross + state * got[lap, :, lanes : 2 * lanes]
        state = spread(decay[lap], rows) * state + got[lap, :, :lanes]
        total = total + got[lap, :, 2 * lanes :]
    done[...] = total
    extra = cross[:, :PC]
    for j in range(1, rows):
        extra = extra + cross[:, j * PC : (j + 1) * PC]
    for lap in range(laps):
        out[lap, :, lanes:] = extra


def group_states(part, enter, total):
    out, log = [enter], jnp.zeros((HP, 1), F32)
    for k in range(GROUP):
        log = log + total[k * HP : (k + 1) * HP]
        out.append(part[k] + pair(jnp.exp(log[:1]), jnp.exp(log[1:]), 1) * enter)
    return out


def rest_logs(total):
    out, log = [None] * GROUP, jnp.zeros((HP, 1), F32)
    for k in reversed(range(GROUP)):
        out[k] = log
        log = log + total[k * HP : (k + 1) * HP]
    return jnp.concatenate(out, axis=0)


def decays(logs, cols, k, h, lower):
    r = k * HP + h
    diff = cols[:, r : r + 1] - logs[r : r + 1]
    return jnp.where(lower, jnp.exp(jnp.where(lower, diff, 0.0)), 0.0)


def output_body(x, part, got, y_out, enter):
    from_slices(got, enter)
    _, step, _, _, logs, total = token_rows(x)
    cols = columns(logs, jnp.exp(logs))
    lower = iota((CHUNK, CHUNK), 0) >= iota((CHUNK, CHUNK), 1)
    states = group_states(part, enter[...], total)
    d = x[0, X_S + 3 : X_S + 4, :]
    for k in range(GROUP):
        b = halves(x, k, X_B).astype(BF16)
        c = halves(x, k, X_C).astype(BF16)
        xk = x[k, :CHUNK, :]
        scores = mm(c, b, NT)
        inner = []
        for h in range(HP):
            r = k * HP + h
            mixed = decays(logs, cols, k, h, lower) * scores * step[r : r + 1]
            inner.append(mm_left(mixed, xk[:, h * PC : (h + 1) * PC].astype(BF16)))
        carried = mm_right(c, states[k]) * pair_cols(cols, k, GROUP * HP)
        y_out[k] = jnp.concatenate(inner, axis=1) + carried + d * xk


def norm_body(y, z, up, gain, stats):
    squares = jnp.zeros((CHUNK, 1), F32)
    crosses = jnp.zeros((CHUNK, 1), F32)
    for q in range(GROUP):
        at = slice(q * WIDE, (q + 1) * WIDE)
        zq = z[:, at].astype(F32)
        gated = y[q] * zq * sigmoid(zq)
        squares = squares + jnp.sum(gated * gated, axis=1, keepdims=True)
        crosses = crosses + jnp.sum(up[:, at] * gated * gain[:, at], axis=1, keepdims=True)
    both = rows_of([squares, crosses])
    tile = jnp.concatenate([both, jnp.zeros((6, CHUNK), F32)], axis=0)
    stats[...] = jnp.broadcast_to(tile[None], stats.shape)


def norm_back_body(total_width, stats, y, z, up, gain, router, gz, gy, router_grad):
    sums = stats[0, :2, :]
    for q in range(1, stats.shape[0]):
        sums = sums + stats[q, :2, :]
    rstd = lax.rsqrt(sums[:1] / total_width + EPS)
    cross = sums[1:]
    router_grad[...] = rstd * cross
    cols = columns(rstd * router[...], rstd * rstd * rstd * (router[...] * cross / total_width))
    for q in range(GROUP):
        at = slice(q * WIDE, (q + 1) * WIDE)
        zq = z[:, at].astype(F32)
        sig = sigmoid(zq)
        gate = zq * sig
        gated = y[q] * gate
        scaled = cols[:, :1] * up[:, at]
        gg = scaled * gain[:, at] - gated * cols[:, 1:2]
        gz[:, at] = (gg * y[q] * sig * (1.0 + zq * (1.0 - sig))).astype(BF16)
        gy[q, :CHUNK, :] = gg * gate
        gy[q, CHUNK:, :] = jnp.broadcast_to(jnp.sum(scaled * gated, axis=0, keepdims=True), (8, WIDE))


def sum_body(got, out):
    total = got[0]
    for q in range(1, got.shape[0]):
        total = total + got[q]
    out[...] = jnp.broadcast_to(total[None], out.shape)


def output_back_body(x, gy_in, y_in, part, enter, gx_out, db_out, dc_out, send, small):
    raw, step, rate, la, logs, total = token_rows(x)
    rest = rest_logs(total)
    cols = columns(
        logs, jnp.exp(logs), jnp.exp(total - logs), step, jnp.exp(total - logs + rest) * step * logs
    )
    near = lanes_of(jnp.exp(rest) * total)
    n = GROUP * HP
    lower = iota((CHUNK, CHUNK), 0) >= iota((CHUNK, CHUNK), 1)
    upper = iota((CHUNK, CHUNK), 0) <= iota((CHUNK, CHUNK), 1)
    states = group_states(part, enter[...], total)
    d = x[0, X_S + 3 : X_S + 4, :]
    decay = lanes_of(jnp.exp(total))
    gain_part = jnp.zeros((1, WIDE), F32)
    skip_part = jnp.zeros((1, WIDE), F32)
    dots, xv, ends = [None] * n, [None] * n, [None] * n
    own = jnp.zeros((NS, WIDE), F32)
    tangent = jnp.zeros((NS, WIDE), F32)
    for k in reversed(range(GROUP)):
        b = halves(x, k, X_B).astype(BF16)
        c32 = halves(x, k, X_C)
        c = c32.astype(BF16)
        xk, y, gy = x[k, :CHUNK, :], y_in[k], gy_in[k, :CHUNK, :]
        gain_part = gain_part + gy_in[k, CHUNK : CHUNK + 1, :]
        skip_part = skip_part + jnp.sum(gy * xk, axis=0, keepdims=True)
        dots[k * HP : (k + 1) * HP] = head_sums(gy * (y - d * xk))
        scores_t = mm(b, c, NT)
        dscores = jnp.zeros((CHUNK, CHUNK), F32)
        inner = []
        for h in range(HP):
            r = k * HP + h
            sl = slice(h * PC, (h + 1) * PC)
            gh, gl = split(gy[:, sl])
            xh = xk[:, sl].astype(BF16)
            dmixed = mm(gh, xh, NT) + mm(gl, xh, NT)
            dscores = dscores + decays(logs, cols, k, h, lower) * dmixed * step[r : r + 1]
            diff = logs[r : r + 1] - cols[:, r : r + 1]
            mixed_t = jnp.where(upper, jnp.exp(jnp.where(upper, diff, 0.0)), 0.0) * scores_t
            mh, ml = split(mixed_t)
            inner.append(mm(mh, gh) + (mm(mh, gl) + mm(ml, gh)))
        tail = pair_cols(cols, k, 2 * n)
        stepc = pair_cols(cols, k, 3 * n)
        oh, ol = split(own)
        v = jnp.concatenate(inner, axis=1) + tail * (mm(b, oh) + mm(b, ol))
        gx_out[k] = stepc * v + d * gy
        xv[k * HP : (k + 1) * HP] = head_sums(xk * v)
        ends[k * HP : (k + 1) * HP] = [
            jnp.sum(e, axis=0, keepdims=True) for e in head_sums(own * states[k + 1])
        ]
        sh, sl = split(tail * stepc * xk)
        db_out[k] = mm_left(dscores.T, c) + (mm(sh, oh, NT) + (mm(sh, ol, NT) + mm(sl, oh, NT)))
        b_t = halves(x, k, X_B).T.astype(BF16)
        tangent = tangent + near[k] * states[k + 1] - mm_right(b_t, xk * pair_cols(cols, k, 4 * n))
        eg = pair_cols(cols, k, n) * gy
        dc_out[k] = mm_left(dscores, b) + mm_both(eg, states[k], NT)
        own = decay[k] * own + mm_right(c32.T.astype(BF16), eg)
    xv = rows_of(xv)
    after = (iota((CHUNK, CHUNK), 0) >= iota((CHUNK, CHUNK), 1)).astype(F32)
    dla = jnp.dot(rows_of(dots) - step * xv, after, precision=lax.Precision.HIGHEST, preferred_element_type=F32)
    dla = dla + jnp.concatenate(ends, axis=0)
    small[:n] = dla
    small[n:] = xv
    laps = send.shape[0]
    rows = NS // laps
    to_slices(send, 0, own)
    to_slices(send, rows, tangent)
    decayed = dla * la
    odd = iota((n, 1), 0) % HP
    extra = jnp.concatenate(
        [jnp.concatenate([a[:, :PC], a[:, PC:]], axis=0) for a in (gain_part, skip_part)]
        + [
            jnp.concatenate(
                [jnp.sum(jnp.where(odd == h, decayed, 0.0), axis=0, keepdims=True) for h in range(HP)], axis=0
            )
        ], axis=1,
    )
    for lap in range(laps):
        send[lap, :, 2 * rows * PC :] = extra


def input_back_body(x, gx_in, part, enter, late, done, small, db_in, dc_in, home, grad_out):
    from_slices(late, grad_out)
    raw, step, rate, la, logs, total = token_rows(x)
    n = GROUP * HP
    rest = rest_logs(total)
    cols = columns(jnp.exp(total - logs + rest), step)
    states = group_states(part, enter[...], total)
    reach = lanes_of(jnp.exp(rest))
    grad = grad_out[...]
    gh, gl = split(grad)
    ends, xv = [], []
    half = CHUNK // 2
    for k in range(GROUP):
        b = halves(x, k, X_B).astype(BF16)
        xk = x[k, :CHUNK, :]
        tail = pair_cols(cols, k)
        stepc = pair_cols(cols, k, n)
        v = tail * (mm(b, gh) + mm(b, gl))
        home[k, :CHUNK, :] = gx_in[k] + stepc * v
        sh, sl = split(tail * stepc * xk)
        db = db_in[k] + (mm(sh, gh, NT) + (mm(sh, gl, NT) + mm(sl, gh, NT)))
        for at, grad_map in ((HOME_B, db), (HOME_C, dc_in[k])):
            home[k, at : at + half, :PC] = grad_map[:half]
            home[k, at : at + half, PC:] = grad_map[half:]
        xv += head_sums(xk * v)
        ends += [jnp.sum(e, axis=0, keepdims=True) for e in head_sums(reach[k] * grad * states[k + 1])]
    xv = rows_of(xv)
    after = (iota((CHUNK, CHUNK), 0) >= iota((CHUNK, CHUNK), 1)).astype(F32)
    dla = jnp.dot(-step * xv, after, precision=lax.Precision.HIGHEST, preferred_element_type=F32)
    dla = small[:n] + dla + jnp.concatenate(ends, axis=0)
    ddt = (dla * rate + small[n:] + xv) * sigmoid(raw)
    alog_rows = done[:, 2 * PC :]
    lanes = late.shape[2] - PC
    for lap in range(late.shape[0]):
        alog_rows = alog_rows + late[lap, :, lanes:]
    shared = jnp.concatenate(
        [jnp.concatenate([a[:1], a[1:]], axis=1) for a in (done[:, :PC], done[:, PC : 2 * PC], alog_rows)]
        + [jnp.zeros((4, WIDE), F32)], axis=0,
    )
    for k in range(GROUP):
        own = jnp.concatenate([ddt[k * HP : k * HP + 1], ddt[k * HP + 1 : k * HP + 2]], axis=1)
        home[k, HOME_S:HOME_B, :] = jnp.concatenate([own, shared], axis=0)


def summed(block, lo, hi):
    got = block[0, lo:hi, :]
    for q in range(1, GROUP):
        got = got + block[q, lo:hi, :]
    return got


def home_body(block, gx, ddt, gain, alog, skip, send):
    lane = iota((1, GROUP * HP), 1)
    a = jnp.zeros((1, GROUP * HP), F32)
    s = jnp.zeros((1, GROUP * HP), F32)
    for q in range(GROUP):
        gx[:, q * WIDE : (q + 1) * WIDE] = block[q, :CHUNK, :].astype(BF16)
        gain[:, q * WIDE : (q + 1) * WIDE] = block[q, HOME_S + 1 : HOME_S + 2, :]
        for h in range(HP):
            sl = slice(h * PC, (h + 1) * PC)
            ddt[q * HP + h : q * HP + h + 1, :] = block[q, HOME_S : HOME_S + 1, sl]
            here = lane == q * HP + h
            s = s + jnp.where(here, jnp.sum(block[q, HOME_S + 2 : HOME_S + 3, sl], axis=1, keepdims=True), 0.0)
            a = a + jnp.where(here, jnp.sum(block[q, HOME_S + 3 : HOME_S + 4, sl], axis=1, keepdims=True), 0.0)
    alog[...] = a
    skip[...] = s
    ranks = send.shape[0]
    rows = CHUNK // ranks
    for i, at in enumerate((HOME_B, HOME_C)):
        got = summed(block, at, at + CHUNK // 2)
        both = jnp.concatenate([got[:, :PC], got[:, PC:]], axis=0)
        for j in range(ranks):
            send[j, i * rows : (i + 1) * rows, :] = both[j * rows : (j + 1) * rows]


def maps_body(got, db, dc):
    ranks = got.shape[0]
    rows = CHUNK // ranks
    for i in range(ranks):
        db[i * rows : (i + 1) * rows, :] = got[i, :rows, :]
        dc[i * rows : (i + 1) * rows, :] = got[i, rows:, :]


def call(body, ins, outs, scratch=(), limit=LIMIT):
    out = pl.pallas_call(
        body,
        in_specs=ins,
        out_specs=[VMEM] * len(outs),
        out_shape=[jax.ShapeDtypeStruct(s, t) for s, t in outs],
        scratch_shapes=scratch,
        compiler_params=pltpu.CompilerParams(vmem_limit_bytes=limit),
    )
    return out


def swap(a, axis):
    return lax.all_to_all(a, axis, 0, 0, tiled=True)


def shards(
    grad_full, keep, router_score, x_in, z_in, b_in, c_in, dt_raw, dt_bias, a_log, d_skip, norm_gain, state_in,
):
    laps = lax.axis_size("z")
    ranks = lax.axis_size("head")
    heads = dt_raw.shape[1]
    width = x_in.shape[1]
    total_width = width * ranks
    block_len = grad_full.shape[0] // keep.shape[0]
    big = ((GROUP, CHUNK, WIDE), F32)
    states = ((GROUP, NS, WIDE), F32)
    lanes = NS // laps * PC
    bind = functools.partial
    dma = pltpu.SemaphoreType.DMA

    router = router_score.reshape(1, CHUNK)
    gain = norm_gain.reshape(1, width)
    (xs,) = call(
        pack_body, [ANY] * 7, [((GROUP, ROWS_X, WIDE), F32)],
        [
            pltpu.VMEM((CHUNK, width), BF16), pltpu.VMEM((CHUNK, NS), BF16), pltpu.VMEM((CHUNK, NS), BF16),
            pltpu.VMEM((heads, CHUNK), F32), pltpu.SMEM((heads,), F32), pltpu.SMEM((heads,), F32),
            pltpu.SMEM((heads,), F32), dma((7,)),
        ], FULL,
    )(x_in, b_in, c_in, dt_raw.T, dt_bias, a_log, d_skip)
    x = swap(xs, "y")
    part, send, up = call(
        bind(own_state_body, block_len), [VMEM] * 3,
        [states, ((laps, HP, lanes + PC), F32), ((CHUNK, width), F32)],
    )(x, grad_full, keep)
    send, decay = call(
        scan_body, [VMEM] * 2, [((laps, HP, lanes), F32), ((laps, HP, PC), F32)],
        [pltpu.VMEM((NS, PC), F32), pltpu.VMEM((HP, lanes), F32)],
    )(swap(send, "z"), state_in)

    y, enter = call(output_body, [VMEM] * 3, [big, ((NS, WIDE), F32)])(x, part, swap(send, "z"))
    y_home = swap(y, "y")
    (stats,) = call(norm_body, [VMEM] * 4, [((ranks, 8, CHUNK), F32)])(y_home, z_in, up, gain)
    grad_z, gy, router_grad = call(
        bind(norm_back_body, total_width), [VMEM] * 6,
        [((CHUNK, width), BF16), ((GROUP, ROWS_Y, WIDE), F32), ((1, CHUNK), F32)],
    )(swap(stats, "head"), y_home, z_in, up, gain, router)
    gx, db, dc, send, small = call(
        output_back_body, [VMEM] * 5,
        [
            big, ((GROUP, CHUNK, NS), F32), ((GROUP, CHUNK, NS), F32), ((laps, HP, 2 * lanes + 3 * PC), F32),
            ((2 * GROUP * HP, CHUNK), F32),
        ],
    )(x, swap(gy, "y"), y, part, enter)
    send, done = call(scan_back_body, [VMEM] * 2, [((laps, HP, lanes + PC), F32), ((HP, 3 * PC), F32)])(
        swap(send, "z"), decay
    )

    (home,) = call(
        input_back_body, [VMEM] * 9, [((GROUP, ROWS_HOME, WIDE), F32)], [pltpu.VMEM((NS, WIDE), F32)]
    )(x, gx, part, enter, swap(send, "z"), done, small, db, dc)
    piece = ((ranks, 2 * CHUNK // ranks, NS), F32)
    grad_x, ddt, grad_gain, grad_alog, grad_skip, send = call(
        home_body, [VMEM],
        [
            ((CHUNK, width), BF16), ((heads, CHUNK), F32), ((1, width), F32), ((1, heads), F32),
            ((1, heads), F32), piece,
        ],
    )(swap(home, "y"))
    (send,) = call(sum_body, [VMEM], [piece])(swap(send, "head"))
    grad_b, grad_c = call(maps_body, [VMEM], [((CHUNK, NS), F32)] * 2)(swap(send, "head"))
    return (
        grad_x,
        grad_z,
        grad_b,
        grad_c,
        ddt.T,
        router_grad.reshape(CHUNK),
        grad_gain.reshape(width),
        grad_alog.reshape(heads),
        grad_skip.reshape(heads),
    )


def solution(mesh):
    count, heads = mesh.devices.shape
    inner = Mesh(mesh.devices.reshape(count // GROUP, GROUP, heads), ("z", "y", "head"))
    seq = ("z", "y")
    in_specs = (
        P(seq, "head"),
        P(seq, None),
        P(seq),
        P(seq, "head"),
        P(seq, "head"),
        P(seq, None),
        P(seq, None),
        P(seq, "head"),
        P("head"),
        P("head"),
        P("head"),
        P("head"),
        P("head", None, None),
    )
    out_specs = (
        P(seq, "head"),
        P(seq, "head"),
        P(seq, None),
        P(seq, None),
        P(seq, "head"),
        P(seq),
        P("head"),
        P("head"),
        P("head"),
    )
    return jax.shard_map(shards, mesh=inner, in_specs=in_specs, out_specs=out_specs, check_vma=False)
```

```python
import functools

import jax
import jax.numpy as jnp
import numpy as np
from jax import lax
from jax.experimental import pallas as pl
from jax.experimental.pallas import tpu as pltpu
from jax.sharding import Mesh
from jax.sharding import PartitionSpec as P

EPS = 1e-05
GROUP = 4
CHUNK = 128
HP = 2
PC = 128
NS = 128
WIDE = HP * PC
F32 = jnp.float32
BF16 = jnp.bfloat16
NN = ((1,), (0,))
NT = ((1,), (1,))

HD = GROUP * HP
ROWS_S = NS + 8
ROWS_G = 2 * NS + 8

VMEM = pl.BlockSpec(memory_space=pltpu.VMEM)
SMEM = pl.BlockSpec(memory_space=pltpu.SMEM)
ANY = pl.BlockSpec(memory_space=pl.ANY)
LIMIT = 24 * 2**20
FULL = 56 * 2**20


def mm(a, b, dims=NN):
    return lax.dot_general(a, b, (dims, ((), ())), preferred_element_type=F32)


def split(a):
    high = a.astype(BF16)
    return high, (a - high.astype(F32)).astype(BF16)


def mm_left(a, exact, dims=NN):
    high, low = split(a)
    return mm(high, exact, dims) + mm(low, exact, dims)


def mm_right(exact, b, dims=NN):
    high, low = split(b)
    return mm(exact, high, dims) + mm(exact, low, dims)


def mm_both(a, b, dims=NN):
    ah, al = split(a)
    bh, bl = split(b)
    return mm(ah, bh, dims) + (mm(ah, bl, dims) + mm(al, bh, dims))


def iota(shape, dim):
    return lax.broadcasted_iota(jnp.int32, shape, dim)


def softplus(v):
    return jnp.maximum(v, 0.0) + jnp.log1p(jnp.exp(-jnp.abs(v)))


def sigmoid(v):
    return 1.0 / (1.0 + jnp.exp(-v))


def own_heads():
    return lax.axis_index("y") * HP


def head_col(ref):
    row = iota((HD, 1), 0)
    out = jnp.zeros((HD, 1), F32)
    for h in range(HD):
        out = jnp.where(row == h, ref[h], out)
    return out


T_RAW, T_STEP, T_LA, T_LOGS, T_RATE, T_SKIP, ROWS_T = (HD * i for i in range(7))


def table(tok, at):
    return tok[at : at + HD, :]


def last(rows):
    return rows[:, CHUNK - 1 :]


def columns(*rows):
    count = sum(r.shape[0] for r in rows)
    return jnp.concatenate(rows + (jnp.zeros((CHUNK - count, CHUNK), F32),), axis=0).T


def rows_of(cols):
    pad = jnp.zeros((CHUNK, CHUNK - len(cols)), F32)
    return jnp.concatenate(list(cols) + [pad], axis=1).T[: len(cols)]


def pair(a, b, rows):
    return jnp.concatenate(
        [jnp.broadcast_to(a, (rows, PC)), jnp.broadcast_to(b, (rows, PC))], axis=1
    )


def lanes_of(values):
    return [pair(values[q * HP : q * HP + 1], values[q * HP + 1 : q * HP + 2], 1) for q in range(GROUP)]


def pair_cols(cols, q, at=0):
    c = at + q * HP
    return pair(cols[:, c : c + 1], cols[:, c + 1 : c + 2], CHUNK)


def head_sums(a):
    return [jnp.sum(a[:, h * PC : (h + 1) * PC], axis=1, keepdims=True) for h in range(HP)]


def two(row):
    return jnp.concatenate([row[:, :PC], row[:, PC:]], axis=0)


def one(rows):
    return jnp.concatenate([rows[:1], rows[1:]], axis=1)


def lanes(q):
    return slice(q * WIDE, (q + 1) * WIDE)


def own_state_body(
    x_hbm, b_hbm, dt_hbm, bias_hbm, alog_hbm, skip_hbm, send, tok, x, b, dt_t, bias, alog, skip, sem
):
    copies = [
        pltpu.make_async_copy(src, dst, sem.at[i])
        for i, (src, dst) in enumerate(
            [(dt_hbm, dt_t), (bias_hbm, bias), (alog_hbm, alog), (skip_hbm, skip), (b_hbm, b), (x_hbm, x)]
        )
    ]
    for copy in copies:
        copy.start()
    for copy in copies:
        copy.wait()
    raw = dt_t[...] + head_col(bias)
    step = softplus(raw)
    rate = -jnp.exp(head_col(alog))
    la = step * rate
    upper = (iota((CHUNK, CHUNK), 0) <= iota((CHUNK, CHUNK), 1)).astype(F32)
    logs = jnp.dot(la, upper, precision=lax.Precision.HIGHEST, preferred_element_type=F32)
    for at, value in (
        (T_RAW, raw), (T_STEP, step), (T_LA, la), (T_LOGS, logs), (T_RATE, rate), (T_SKIP, head_col(skip))
    ):
        tok[at : at + HD, :] = jnp.broadcast_to(value, (HD, CHUNK))
    cols = columns(jnp.exp(last(logs) - logs) * step)
    decay = lanes_of(jnp.exp(last(logs)))
    b_t = b[...].astype(F32).T.astype(BF16)
    for q in range(GROUP):
        send[q, :NS, :] = mm_right(b_t, x[:, lanes(q)].astype(F32) * pair_cols(cols, q))
        send[q, NS:, :] = jnp.broadcast_to(decay[q], (8, WIDE))


def to_slices(out, at, state):
    rows = NS // out.shape[0]
    for n in range(NS):
        tile = slice((at + n % rows) * PC, (at + n % rows + 1) * PC)
        out[n // rows, :, tile] = jnp.concatenate([state[n : n + 1, :PC], state[n : n + 1, PC:]], axis=0)


def from_slices(ref, out):
    rows = NS // ref.shape[0]
    for n in range(NS):
        tile = slice(n % rows * PC, (n % rows + 1) * PC)
        for h in range(HP):
            out[n : n + 1, h * PC : (h + 1) * PC] = ref[n // rows, h : h + 1, tile]


def group_state_body(block_len, got, grad_full, keep, part, send, up):
    state = got[0, :NS, :]
    whole = got[0, NS : NS + 1, :]
    part[0] = state
    for k in range(1, GROUP):
        decay = got[k, NS : NS + 1, :]
        state = decay * state + got[k, :NS, :]
        whole = whole * decay
        part[k] = state
    to_slices(send, 0, state)
    for lap in range(send.shape[0]):
        send[lap, :, send.shape[2] - PC :] = two(whole)
    blocks, kept = keep.shape
    for i in range(blocks):
        pick = (iota((kept, block_len), 1) == keep[i : i + 1, :].T).astype(BF16)
        up[i * kept : (i + 1) * kept, :] = mm(pick, grad_full[i * block_len : (i + 1) * block_len, :])


def spread(row, count):
    return jnp.concatenate([row] * count, axis=1)


def scan_body(got, state_in, out, decay, flat, first):
    laps, _, lanes = out.shape
    rows = lanes // PC
    base = own_heads()
    for h in range(HP):
        flat[...] = state_in[base + h].T
        for j in range(rows):
            first[h : h + 1, j * PC : (j + 1) * PC] = flat[pl.ds(lax.axis_index("z") * rows + j, 1), :]
    state = first[...]
    for lap in range(laps):
        out[lap] = state
        factor = got[lap, :, lanes:]
        decay[lap] = factor
        state = spread(factor, rows) * state + got[lap, :, :lanes]


def scan_back_body(got, decay, out, done):
    laps = got.shape[0]
    lanes = out.shape[2] - PC
    rows = lanes // PC
    state = jnp.zeros((HP, lanes), F32)
    cross = jnp.zeros((HP, lanes), F32)
    total = jnp.zeros((HP, 3 * PC), F32)
    for lap in reversed(range(laps)):
        out[lap, :, :lanes] = state
        cross = cross + state * got[lap, :, lanes : 2 * lanes]
        state = spread(decay[lap], rows) * state + got[lap, :, :lanes]
        total = total + got[lap, :, 2 * lanes :]
    done[...] = total
    extra = cross[:, :PC]
    for j in range(1, rows):
        extra = extra + cross[:, j * PC : (j + 1) * PC]
    for lap in range(laps):
        out[lap, :, lanes:] = extra


def enter_body(got, own, part, send, flat):
    from_slices(got, flat)
    state = flat[...]
    send[0] = state
    reach = own[0, NS : NS + 1, :]
    for k in range(1, GROUP):
        send[k] = part[k - 1] + reach * state
        reach = reach * own[k, NS : NS + 1, :]


def decays(logs, cols, r, lower):
    diff = cols[:, r : r + 1] - logs[r : r + 1]
    return jnp.where(lower, jnp.exp(jnp.where(lower, diff, 0.0)), 0.0)


def output_body(x, b, c, z, up, gain, tok, enter, y_out, stats):
    logs, step = table(tok, T_LOGS), table(tok, T_STEP)
    cols = columns(logs, jnp.exp(logs))
    lower = iota((CHUNK, CHUNK), 0) >= iota((CHUNK, CHUNK), 1)
    d = lanes_of(last(table(tok, T_SKIP)))
    scores = mm(c[...], b[...], NT)
    squares = jnp.zeros((CHUNK, 1), F32)
    crosses = jnp.zeros((CHUNK, 1), F32)
    for q in range(GROUP):
        inner = []
        for h in range(HP):
            r = q * HP + h
            mixed = decays(logs, cols, r, lower) * scores * step[r : r + 1]
            inner.append(mm_left(mixed, x[:, r * PC : (r + 1) * PC]))
        carried = mm_right(c[...], enter[q]) * pair_cols(cols, q, HD)
        y = jnp.concatenate(inner, axis=1) + carried + d[q] * x[:, lanes(q)].astype(F32)
        y_out[:, lanes(q)] = y
        zq = z[:, lanes(q)].astype(F32)
        gated = y * zq * sigmoid(zq)
        squares = squares + jnp.sum(gated * gated, axis=1, keepdims=True)
        crosses = crosses + jnp.sum(up[:, lanes(q)] * gated * gain[:, lanes(q)], axis=1, keepdims=True)
    tile = jnp.concatenate([rows_of([squares, crosses]), jnp.zeros((6, CHUNK), F32)], axis=0)
    stats[...] = jnp.broadcast_to(tile[None], stats.shape)


def output_back_body(
    total_width, stats, x, b, c, z, up, gain, router, tok, enter, own, y_in,
    gz, gx_out, send, small, maps, router_grad,
):
    sums = stats[0, :2, :]
    for i in range(1, stats.shape[0]):
        sums = sums + stats[i, :2, :]
    rstd = lax.rsqrt(sums[:1] / total_width + EPS)
    cross = sums[1:]
    router_grad[...] = rstd * cross
    logs, step, la = table(tok, T_LOGS), table(tok, T_STEP), table(tok, T_LA)
    total = last(logs)
    tail = jnp.exp(total - logs)
    cols = columns(
        logs, jnp.exp(logs), step, tail * step * logs,
        rstd * router[...], rstd * rstd * rstd * (router[...] * cross / total_width),
    )
    at_a = 4 * HD
    lower = iota((CHUNK, CHUNK), 0) >= iota((CHUNK, CHUNK), 1)
    upper = iota((CHUNK, CHUNK), 0) <= iota((CHUNK, CHUNK), 1)
    d = lanes_of(last(table(tok, T_SKIP)))
    decay = lanes_of(jnp.exp(total))
    near = lanes_of(total)
    scores_t = mm(b[...], c[...], NT)
    b_t = b[...].astype(F32).T.astype(BF16)
    c_t = c[...].astype(F32).T.astype(BF16)
    dscores = jnp.zeros((CHUNK, CHUNK), F32)
    dc = jnp.zeros((CHUNK, NS), F32)
    dots, xv, shared = [], [], []
    for q in range(GROUP):
        xb = x[:, lanes(q)]
        xq, zq, u, y = xb.astype(F32), z[:, lanes(q)].astype(F32), up[:, lanes(q)], y_in[:, lanes(q)]
        sig = sigmoid(zq)
        gate = zq * sig
        gated = y * gate
        scaled = cols[:, at_a : at_a + 1] * u
        gg = scaled * gain[:, lanes(q)] - gated * cols[:, at_a + 1 : at_a + 2]
        gz[:, lanes(q)] = (gg * y * sig * (1.0 + zq * (1.0 - sig))).astype(BF16)
        gy = gg * gate
        shared.append(
            [jnp.sum(scaled * gated, axis=0, keepdims=True), jnp.sum(gy * xq, axis=0, keepdims=True)]
        )
        dots += head_sums(gy * (y - d[q] * xq))
        gh, gl = split(gy)
        inner = []
        for h in range(HP):
            r = q * HP + h
            sl = slice(h * PC, (h + 1) * PC)
            dmixed = mm(gh[:, sl], xb[:, sl], NT) + mm(gl[:, sl], xb[:, sl], NT)
            dscores = dscores + decays(logs, cols, r, lower) * dmixed * step[r : r + 1]
            diff = logs[r : r + 1] - cols[:, r : r + 1]
            mixed_t = jnp.where(upper, jnp.exp(jnp.where(upper, diff, 0.0)), 0.0) * scores_t
            mh, ml = split(mixed_t)
            inner.append(mm(mh, gh[:, sl]) + (mm(mh, gl[:, sl]) + mm(ml, gh[:, sl])))
        v = jnp.concatenate(inner, axis=1)
        gx_out[:, lanes(q)] = pair_cols(cols, q, 2 * HD) * v + d[q] * gy
        xv += head_sums(xq * v)
        eg = pair_cols(cols, q, HD) * gy
        dc = dc + mm_both(eg, enter[q], NT)
        send[q, :NS, :] = mm_right(c_t, eg)
        leaving = decay[q] * enter[q] + own[q, :NS, :]
        send[q, NS : 2 * NS, :] = near[q] * leaving - mm_right(b_t, xq * pair_cols(cols, q, 3 * HD))
    maps[0] = mm_left(dscores.T, c[...])
    maps[1] = dc + mm_left(dscores, b[...])
    xv = rows_of(xv)
    after = (iota((CHUNK, CHUNK), 0) >= iota((CHUNK, CHUNK), 1)).astype(F32)
    dla = jnp.dot(rows_of(dots) - step * xv, after, precision=lax.Precision.HIGHEST, preferred_element_type=F32)
    small[:HD] = dla
    small[HD:] = xv
    decayed = dla * la
    for q in range(GROUP):
        rows = shared[q] + [one(decayed[q * HP : (q + 1) * HP]), jnp.zeros((5, WIDE), F32)]
        send[q, 2 * NS :, :] = jnp.concatenate(rows, axis=0)


def group_back_body(got, own, back, send):
    grad = got[GROUP - 1, :NS, :]
    tangent = got[GROUP - 1, NS : 2 * NS, :]
    reach = own[GROUP - 1, NS : NS + 1, :]
    back[GROUP - 1] = jnp.zeros((NS, WIDE), F32)
    extra = got[GROUP - 1, 2 * NS : 2 * NS + 3, :]
    cross = jnp.zeros((1, WIDE), F32)
    for k in reversed(range(GROUP - 1)):
        q = got[k, NS : 2 * NS, :]
        back[k] = grad
        cross = cross + jnp.sum(grad * q, axis=0, keepdims=True)
        tangent = tangent + reach * q
        extra = extra + got[k, 2 * NS : 2 * NS + 3, :]
        decay = own[k, NS : NS + 1, :]
        reach = reach * decay
        grad = decay * grad + got[k, :NS, :]
    laps = send.shape[0]
    rows = NS // laps
    to_slices(send, 0, grad)
    to_slices(send, rows, tangent)
    tail = jnp.concatenate([two(extra[:1]), two(extra[1:2]), two(extra[2:] + cross)], axis=1)
    for lap in range(laps):
        send[lap, :, 2 * rows * PC :] = tail


def leave_body(late, done, back, own, send, flat):
    from_slices(late, flat)
    grad = flat[...]
    alog = done[:, 2 * PC :]
    at = late.shape[2] - PC
    for lap in range(late.shape[0]):
        alog = alog + late[lap, :, at:]
    extra = jnp.concatenate(
        [one(done[:, :PC]), one(done[:, PC : 2 * PC]), one(alog), jnp.zeros((5, WIDE), F32)], axis=0
    )
    reach = jnp.ones((1, WIDE), F32)
    for k in reversed(range(GROUP)):
        send[k, :NS, :] = back[k] + reach * grad
        send[k, NS:, :] = extra
        reach = reach * own[k, NS : NS + 1, :]


def input_back_body(x, b, tok, gx_in, small, maps, enter, own, late, gx, ddt, gain, alog, skip, send):
    raw, step, rate = table(tok, T_RAW), table(tok, T_STEP), table(tok, T_RATE)
    logs = table(tok, T_LOGS)
    total = last(logs)
    cols = columns(jnp.exp(total - logs), step)
    decay = lanes_of(jnp.exp(total))
    db = maps[0]
    ends, xv = [], []
    lane = iota((1, HD), 1)
    a = jnp.zeros((1, HD), F32)
    s = jnp.zeros((1, HD), F32)
    for q in range(GROUP):
        grad = late[q, :NS, :]
        xq = x[:, lanes(q)].astype(F32)
        tail = pair_cols(cols, q)
        stepc = pair_cols(cols, q, HD)
        gh, gl = split(grad)
        v = tail * (mm(b[...], gh) + mm(b[...], gl))
        gx[:, lanes(q)] = (gx_in[:, lanes(q)] + stepc * v).astype(BF16)
        sh, sl = split(tail * stepc * xq)
        db = db + (mm(sh, gh, NT) + (mm(sh, gl, NT) + mm(sl, gh, NT)))
        xv += head_sums(xq * v)
        leaving = decay[q] * enter[q] + own[q, :NS, :]
        ends += [jnp.sum(e, axis=0, keepdims=True) for e in head_sums(grad * leaving)]
        gain[:, lanes(q)] = late[q, NS : NS + 1, :]
        for h in range(HP):
            here = lane == q * HP + h
            sl = slice(h * PC, (h + 1) * PC)
            s = s + jnp.where(here, jnp.sum(late[q, NS + 1 : NS + 2, sl], axis=1, keepdims=True), 0.0)
            a = a + jnp.where(here, jnp.sum(late[q, NS + 2 : NS + 3, sl], axis=1, keepdims=True), 0.0)
    alog[...] = a
    skip[...] = s
    xv = rows_of(xv)
    after = (iota((CHUNK, CHUNK), 0) >= iota((CHUNK, CHUNK), 1)).astype(F32)
    dla = jnp.dot(-step * xv, after, precision=lax.Precision.HIGHEST, preferred_element_type=F32)
    dla = small[:HD] + dla + jnp.concatenate(ends, axis=0)
    ddt[...] = (dla * rate + small[HD:] + xv) * sigmoid(raw)
    ranks = send.shape[0]
    rows = CHUNK // ranks
    for j in range(ranks):
        send[j, :rows, :] = db[j * rows : (j + 1) * rows]
        send[j, rows:, :] = maps[1, j * rows : (j + 1) * rows, :]


def sum_body(got, out):
    total = got[0]
    for q in range(1, got.shape[0]):
        total = total + got[q]
    out[...] = jnp.broadcast_to(total[None], out.shape)


def maps_body(got, db, dc):
    ranks = got.shape[0]
    rows = CHUNK // ranks
    for i in range(ranks):
        db[i * rows : (i + 1) * rows, :] = got[i, :rows, :]
        dc[i * rows : (i + 1) * rows, :] = got[i, rows:, :]


def call(body, ins, outs, scratch=(), limit=LIMIT):
    out = pl.pallas_call(
        body,
        in_specs=ins,
        out_specs=[VMEM] * len(outs),
        out_shape=[jax.ShapeDtypeStruct(s, t) for s, t in outs],
        scratch_shapes=scratch,
        compiler_params=pltpu.CompilerParams(vmem_limit_bytes=limit),
    )
    return out


def swap(a, axis):
    return lax.all_to_all(a, axis, 0, 0, tiled=True)


def shards(
    grad_full, keep, router_score, x_in, z_in, b_in, c_in, dt_raw, dt_bias, a_log, d_skip, norm_gain, state_in,
):
    laps = lax.axis_size("z")
    ranks = lax.axis_size("head")
    heads = dt_raw.shape[1]
    width = x_in.shape[1]
    total_width = width * ranks
    block_len = grad_full.shape[0] // keep.shape[0]
    states = ((GROUP, NS, WIDE), F32)
    slab = ((CHUNK, width), F32)
    tile = NS // laps * PC
    bind = functools.partial
    dma = pltpu.SemaphoreType.DMA
    router = router_score.reshape(1, CHUNK)
    gain = norm_gain.reshape(1, width)
    flat = pltpu.VMEM((NS, WIDE), F32)

    own, tok = call(
        own_state_body, [ANY] * 6, [((GROUP, ROWS_S, WIDE), F32), ((ROWS_T, CHUNK), F32)],
        [
            pltpu.VMEM((CHUNK, width), BF16), pltpu.VMEM((CHUNK, NS), BF16), pltpu.VMEM((heads, CHUNK), F32),
            pltpu.SMEM((heads,), F32), pltpu.SMEM((heads,), F32), pltpu.SMEM((heads,), F32), dma((6,)),
        ], FULL,
    )(x_in, b_in, dt_raw.T, dt_bias, a_log, d_skip)
    group = swap(own, "y")
    part, send, up = call(
        bind(group_state_body, block_len), [VMEM] * 3, [states, ((laps, HP, tile + PC), F32), slab]
    )(group, grad_full, keep)
    send, decay = call(
        scan_body, [VMEM] * 2, [((laps, HP, tile), F32), ((laps, HP, PC), F32)],
        [pltpu.VMEM((NS, PC), F32), pltpu.VMEM((HP, tile), F32)],
    )(swap(send, "z"), state_in)
    (enter,) = call(enter_body, [VMEM] * 3, [states], [flat])(swap(send, "z"), group, part)
    enter = swap(enter, "y")

    y, stats = call(output_body, [VMEM] * 8, [slab, ((ranks, 8, CHUNK), F32)])(
        x_in, b_in, c_in, z_in, up, gain, tok, enter
    )
    grad_z, gx, send, small, maps, router_grad = call(
        bind(output_back_body, total_width), [VMEM] * 12,
        [
            ((CHUNK, width), BF16), slab, ((GROUP, ROWS_G, WIDE), F32), ((2 * HD, CHUNK), F32),
            ((2, CHUNK, NS), F32), ((1, CHUNK), F32),
        ],
    )(swap(stats, "head"), x_in, b_in, c_in, z_in, up, gain, router, tok, enter, own, y)
    back, send = call(group_back_body, [VMEM] * 2, [states, ((laps, HP, 2 * tile + 3 * PC), F32)])(
        swap(send, "y"), group
    )
    send, done = call(scan_back_body, [VMEM] * 2, [((laps, HP, tile + PC), F32), ((HP, 3 * PC), F32)])(
        swap(send, "z"), decay
    )
    (late,) = call(leave_body, [VMEM] * 4, [((GROUP, ROWS_S, WIDE), F32)], [flat])(
        swap(send, "z"), done, back, group
    )
    piece = ((ranks, 2 * CHUNK // ranks, NS), F32)
    grad_x, ddt, grad_gain, grad_alog, grad_skip, send = call(
        input_back_body, [VMEM] * 9,
        [
            ((CHUNK, width), BF16), ((heads, CHUNK), F32), ((1, width), F32), ((1, heads), F32),
            ((1, heads), F32), piece,
        ],
    )(x_in, b_in, tok, gx, small, maps, enter, own, swap(late, "y"))
    (send,) = call(sum_body, [VMEM], [piece])(swap(send, "head"))
    grad_b, grad_c = call(maps_body, [VMEM], [((CHUNK, NS), F32)] * 2)(swap(send, "head"))
    return (
        grad_x,
        grad_z,
        grad_b,
        grad_c,
        ddt.T,
        router_grad.reshape(CHUNK),
        grad_gain.reshape(width),
        grad_alog.reshape(heads),
        grad_skip.reshape(heads),
    )


def solution(mesh):
    count, heads = mesh.devices.shape
    inner = Mesh(mesh.devices.reshape(count // GROUP, GROUP, heads), ("z", "y", "head"))
    seq = ("z", "y")
    in_specs = (
        P(seq, "head"),
        P(seq, None),
        P(seq),
        P(seq, "head"),
        P(seq, "head"),
        P(seq, None),
        P(seq, None),
        P(seq, "head"),
        P("head"),
        P("head"),
        P("head"),
        P("head"),
        P("head", None, None),
    )
    out_specs = (
        P(seq, "head"),
        P(seq, "head"),
        P(seq, None),
        P(seq, None),
        P(seq, "head"),
        P(seq),
        P("head"),
        P("head"),
        P("head"),
    )
    return jax.shard_map(shards, mesh=inner, in_specs=in_specs, out_specs=out_specs, check_vma=False)
```

```python
import functools

import jax
import jax.numpy as jnp
import numpy as np
from jax import lax
from jax.experimental import pallas as pl
from jax.experimental.pallas import tpu as pltpu
from jax.sharding import Mesh
from jax.sharding import PartitionSpec as P

EPS = 1e-05
GROUP = 4
CHUNK = 128
HP = 2
PC = 128
NS = 128
WIDE = HP * PC
F32 = jnp.float32
BF16 = jnp.bfloat16
NN = ((1,), (0,))
NT = ((1,), (1,))

HD = GROUP * HP
ROWS_S = NS + 8
ROWS_G = 2 * NS + 8

VMEM = pl.BlockSpec(memory_space=pltpu.VMEM)
SMEM = pl.BlockSpec(memory_space=pltpu.SMEM)
ANY = pl.BlockSpec(memory_space=pl.ANY)
LIMIT = 24 * 2**20
FULL = 56 * 2**20


def mm(a, b, dims=NN):
    return lax.dot_general(a, b, (dims, ((), ())), preferred_element_type=F32)


def split(a):
    high = a.astype(BF16)
    return high, (a - high.astype(F32)).astype(BF16)


def mm_left(a, exact, dims=NN):
    high, low = split(a)
    return mm(high, exact, dims) + mm(low, exact, dims)


def mm_right(exact, b, dims=NN):
    high, low = split(b)
    return mm(exact, high, dims) + mm(exact, low, dims)


def mm_both(a, b, dims=NN):
    ah, al = split(a)
    bh, bl = split(b)
    return mm(ah, bh, dims) + (mm(ah, bl, dims) + mm(al, bh, dims))


def iota(shape, dim):
    return lax.broadcasted_iota(jnp.int32, shape, dim)


def softplus(v):
    return jnp.maximum(v, 0.0) + jnp.log1p(jnp.exp(-jnp.abs(v)))


def sigmoid(v):
    return 1.0 / (1.0 + jnp.exp(-v))


def own_heads():
    return lax.axis_index("y") * HP


def head_col(ref):
    row = iota((HD, 1), 0)
    out = jnp.zeros((HD, 1), F32)
    for h in range(HD):
        out = jnp.where(row == h, ref[h], out)
    return out


T_RAW, T_STEP, T_LA, T_LOGS, T_RATE, T_SKIP, ROWS_T = (HD * i for i in range(7))


def table(tok, at):
    return tok[at : at + HD, :]


def last(rows):
    return rows[:, CHUNK - 1 :]


def columns(*rows):
    count = sum(r.shape[0] for r in rows)
    return jnp.concatenate(rows + (jnp.zeros((CHUNK - count, CHUNK), F32),), axis=0).T


def rows_of(cols):
    pad = jnp.zeros((CHUNK, CHUNK - len(cols)), F32)
    return jnp.concatenate(list(cols) + [pad], axis=1).T[: len(cols)]


def pair(a, b, rows):
    return jnp.concatenate(
        [jnp.broadcast_to(a, (rows, PC)), jnp.broadcast_to(b, (rows, PC))], axis=1
    )


def lanes_of(values):
    return [pair(values[q * HP : q * HP + 1], values[q * HP + 1 : q * HP + 2], 1) for q in range(GROUP)]


def pair_cols(cols, q, at=0):
    c = at + q * HP
    return pair(cols[:, c : c + 1], cols[:, c + 1 : c + 2], CHUNK)


def head_sums(a):
    return [jnp.sum(a[:, h * PC : (h + 1) * PC], axis=1, keepdims=True) for h in range(HP)]


def whole_sums(a):
    return [jnp.sum(s, axis=0, keepdims=True) for s in head_sums(a)]


def halved(a, b):
    return jnp.where(iota((1, WIDE), 1) % PC < PC // 2, a, b)


def two(row):
    return jnp.concatenate([row[:, :PC], row[:, PC:]], axis=0)


def one(rows):
    return jnp.concatenate([rows[:1], rows[1:]], axis=1)


def lanes(q):
    return slice(q * WIDE, (q + 1) * WIDE)


def own_state_body(
    x_hbm, b_hbm, dt_hbm, bias_hbm, alog_hbm, skip_hbm, send_hbm, tok, x, b, dt_t, bias, alog, skip, send, sem, quarter
):
    copies = [
        pltpu.make_async_copy(src, dst, sem.at[i])
        for i, (src, dst) in enumerate(
            [(dt_hbm, dt_t), (bias_hbm, bias), (alog_hbm, alog), (skip_hbm, skip), (b_hbm, b)]
        )
    ]
    loads = [pltpu.make_async_copy(x_hbm.at[:, lanes(q)], x.at[:, lanes(q)], quarter.at[0, q]) for q in range(GROUP)]
    stores = [pltpu.make_async_copy(send.at[q], send_hbm.at[q], quarter.at[1, q]) for q in range(GROUP)]
    for copy in copies + loads:
        copy.start()
    for copy in copies:
        copy.wait()
    raw = dt_t[...] + head_col(bias)
    step = softplus(raw)
    rate = -jnp.exp(head_col(alog))
    la = step * rate
    upper = (iota((CHUNK, CHUNK), 0) <= iota((CHUNK, CHUNK), 1)).astype(F32)
    logs = jnp.dot(la, upper, precision=lax.Precision.HIGHEST, preferred_element_type=F32)
    for at, value in (
        (T_RAW, raw), (T_STEP, step), (T_LA, la), (T_LOGS, logs), (T_RATE, rate), (T_SKIP, head_col(skip))
    ):
        tok[at : at + HD, :] = jnp.broadcast_to(value, (HD, CHUNK))
    cols = columns(jnp.exp(last(logs) - logs) * step)
    decay = lanes_of(jnp.exp(last(logs)))
    b_t = b[...].astype(F32).T.astype(BF16)
    for q in range(GROUP):
        loads[q].wait()
        send[q, :NS, :] = mm_right(b_t, x[:, lanes(q)].astype(F32) * pair_cols(cols, q))
        send[q, NS:, :] = jnp.broadcast_to(decay[q], (8, WIDE))
        stores[q].start()
    for q in range(GROUP):
        stores[q].wait()


def to_slices(out, at, state):
    rows = NS // out.shape[0]
    for n in range(NS):
        tile = slice((at + n % rows) * PC, (at + n % rows + 1) * PC)
        out[n // rows, :, tile] = jnp.concatenate([state[n : n + 1, :PC], state[n : n + 1, PC:]], axis=0)


def from_slices(ref, out):
    rows = NS // ref.shape[0]
    for n in range(NS):
        tile = slice(n % rows * PC, (n % rows + 1) * PC)
        for h in range(HP):
            out[n : n + 1, h * PC : (h + 1) * PC] = ref[n // rows, h : h + 1, tile]


def group_state_body(got, part, send):
    state = got[0, :NS, :]
    whole = got[0, NS : NS + 1, :]
    part[0] = state
    for k in range(1, GROUP):
        decay = got[k, NS : NS + 1, :]
        state = decay * state + got[k, :NS, :]
        whole = whole * decay
        part[k] = state
    to_slices(send, 0, state)
    for lap in range(send.shape[0]):
        send[lap, :, send.shape[2] - PC :] = two(whole)
def spread(row, count):
    return jnp.concatenate([row] * count, axis=1)


def scan_body(got, state_in, out, decay, flat, first):
    laps, _, lanes = out.shape
    rows = lanes // PC
    base = own_heads()
    for h in range(HP):
        flat[...] = state_in[base + h].T
        for j in range(rows):
            first[h : h + 1, j * PC : (j + 1) * PC] = flat[pl.ds(lax.axis_index("z") * rows + j, 1), :]
    state = first[...]
    for lap in range(laps):
        out[lap] = state
        factor = got[lap, :, lanes:]
        decay[lap] = factor
        state = spread(factor, rows) * state + got[lap, :, :lanes]


def scan_back_body(got, decay, out, done):
    laps = got.shape[0]
    lanes = out.shape[2] - PC
    rows = lanes // PC
    state = jnp.zeros((HP, lanes), F32)
    cross = jnp.zeros((HP, lanes), F32)
    total = jnp.zeros((HP, 2 * PC), F32)
    for lap in reversed(range(laps)):
        out[lap, :, :lanes] = state
        cross = cross + state * got[lap, :, lanes : 2 * lanes]
        state = spread(decay[lap], rows) * state + got[lap, :, :lanes]
        total = total + got[lap, :, 2 * lanes :]
    done[...] = total
    extra = cross[:, :PC]
    for j in range(1, rows):
        extra = extra + cross[:, j * PC : (j + 1) * PC]
    for lap in range(laps):
        out[lap, :, lanes:] = extra


def enter_body(got, own, part, send, flat):
    from_slices(got, flat)
    state = flat[...]
    send[0] = state
    reach = own[0, NS : NS + 1, :]
    for k in range(1, GROUP):
        send[k] = part[k - 1] + reach * state
        reach = reach * own[k, NS : NS + 1, :]


def decays(logs, cols, r, lower):
    diff = cols[:, r : r + 1] - logs[r : r + 1]
    return jnp.where(lower, jnp.exp(jnp.where(lower, diff, 0.0)), 0.0)


def output_body(block_len, x, b, c, z, grad_full, keep, gain, tok, enter, y_out, up, stats):
    blocks, kept = keep.shape
    for i in range(blocks):
        pick = (iota((kept, block_len), 1) == keep[i : i + 1, :].T).astype(BF16)
        up[i * kept : (i + 1) * kept, :] = mm(pick, grad_full[i * block_len : (i + 1) * block_len, :])
    logs, step = table(tok, T_LOGS), table(tok, T_STEP)
    cols = columns(logs, jnp.exp(logs))
    lower = iota((CHUNK, CHUNK), 0) >= iota((CHUNK, CHUNK), 1)
    d = lanes_of(last(table(tok, T_SKIP)))
    scores = mm(c[...], b[...], NT)
    squares = jnp.zeros((CHUNK, 1), F32)
    crosses = jnp.zeros((CHUNK, 1), F32)
    for q in range(GROUP):
        inner = []
        for h in range(HP):
            r = q * HP + h
            mixed = decays(logs, cols, r, lower) * scores * step[r : r + 1]
            inner.append(mm_left(mixed, x[:, r * PC : (r + 1) * PC]))
        carried = mm_right(c[...], enter[q]) * pair_cols(cols, q, HD)
        y = jnp.concatenate(inner, axis=1) + carried + d[q] * x[:, lanes(q)].astype(F32)
        y_out[:, lanes(q)] = y
        zq = z[:, lanes(q)].astype(F32)
        gated = y * zq * sigmoid(zq)
        squares = squares + jnp.sum(gated * gated, axis=1, keepdims=True)
        crosses = crosses + jnp.sum(up[:, lanes(q)] * gated * gain[:, lanes(q)], axis=1, keepdims=True)
    stats[...] = jnp.broadcast_to(rows_of([squares, crosses])[None], stats.shape)


def output_back_body(
    total_width, stats, x, b, c, z, up, gain, router, tok, enter, own, y_in,
    gz, gx_out, send, small, maps, router_grad,
):
    sums = stats[0]
    for i in range(1, stats.shape[0]):
        sums = sums + stats[i]
    rstd = lax.rsqrt(sums[:1] / total_width + EPS)
    cross = sums[1:]
    router_grad[...] = rstd * cross
    logs, step, la = table(tok, T_LOGS), table(tok, T_STEP), table(tok, T_LA)
    total = last(logs)
    tail = jnp.exp(total - logs)
    cols = columns(
        logs, jnp.exp(logs), step, tail * step * logs,
        rstd * router[...], rstd * rstd * rstd * (router[...] * cross / total_width),
    )
    at_a = 4 * HD
    lower = iota((CHUNK, CHUNK), 0) >= iota((CHUNK, CHUNK), 1)
    upper = iota((CHUNK, CHUNK), 0) <= iota((CHUNK, CHUNK), 1)
    d = lanes_of(last(table(tok, T_SKIP)))
    decay = lanes_of(jnp.exp(total))
    near = lanes_of(total)
    scores_t = mm(b[...], c[...], NT)
    b_t = b[...].astype(F32).T.astype(BF16)
    c_t = c[...].astype(F32).T.astype(BF16)
    dscores = jnp.zeros((CHUNK, CHUNK), F32)
    dc = jnp.zeros((CHUNK, NS), F32)
    dots, xv, shared, skips = [], [], [], []
    for q in range(GROUP):
        xb = x[:, lanes(q)]
        xq, zq, u, y = xb.astype(F32), z[:, lanes(q)].astype(F32), up[:, lanes(q)], y_in[:, lanes(q)]
        sig = sigmoid(zq)
        gate = zq * sig
        gated = y * gate
        scaled = cols[:, at_a : at_a + 1] * u
        gg = scaled * gain[:, lanes(q)] - gated * cols[:, at_a + 1 : at_a + 2]
        gz[:, lanes(q)] = (gg * y * sig * (1.0 + zq * (1.0 - sig))).astype(BF16)
        gy = gg * gate
        shared.append(jnp.sum(scaled * gated, axis=0, keepdims=True))
        skips += whole_sums(gy * xq)
        dots += head_sums(gy * (y - d[q] * xq))
        gh, gl = split(gy)
        inner = []
        for h in range(HP):
            r = q * HP + h
            sl = slice(h * PC, (h + 1) * PC)
            dmixed = mm(gh[:, sl], xb[:, sl], NT) + mm(gl[:, sl], xb[:, sl], NT)
            dscores = dscores + decays(logs, cols, r, lower) * dmixed * step[r : r + 1]
            diff = logs[r : r + 1] - cols[:, r : r + 1]
            mixed_t = jnp.where(upper, jnp.exp(jnp.where(upper, diff, 0.0)), 0.0) * scores_t
            mh, ml = split(mixed_t)
            inner.append(mm(mh, gh[:, sl]) + (mm(mh, gl[:, sl]) + mm(ml, gh[:, sl])))
        v = jnp.concatenate(inner, axis=1)
        gx_out[:, lanes(q)] = pair_cols(cols, q, 2 * HD) * v + d[q] * gy
        xv += head_sums(xq * v)
        eg = pair_cols(cols, q, HD) * gy
        dc = dc + mm_both(eg, enter[q], NT)
        send[q, :NS, :] = mm_right(c_t, eg)
        leaving = decay[q] * enter[q] + own[q, :NS, :]
        send[q, NS : 2 * NS, :] = near[q] * leaving - mm_right(b_t, xq * pair_cols(cols, q, 3 * HD))
    maps[0] = mm_left(dscores.T, c[...])
    maps[1] = dc + mm_left(dscores, b[...])
    xv = rows_of(xv)
    after = (iota((CHUNK, CHUNK), 0) >= iota((CHUNK, CHUNK), 1)).astype(F32)
    dla = jnp.dot(rows_of(dots) - step * xv, after, precision=lax.Precision.HIGHEST, preferred_element_type=F32)
    small[:HD] = dla
    small[HD:] = xv
    alogs = jnp.sum(dla * la, axis=1, keepdims=True)
    for q in range(GROUP):
        r = q * HP
        row = halved(pair(skips[r], skips[r + 1], 1), pair(alogs[r : r + 1], alogs[r + 1 : r + 2], 1))
        send[q, 2 * NS :, :] = jnp.concatenate([shared[q], row, jnp.zeros((6, WIDE), F32)], axis=0)


def group_back_body(got, own, back, send):
    grad = got[GROUP - 1, :NS, :]
    tangent = got[GROUP - 1, NS : 2 * NS, :]
    reach = own[GROUP - 1, NS : NS + 1, :]
    back[GROUP - 1] = jnp.zeros((NS, WIDE), F32)
    extra = got[GROUP - 1, 2 * NS : 2 * NS + 2, :]
    cross = jnp.zeros((1, WIDE), F32)
    for k in reversed(range(GROUP - 1)):
        q = got[k, NS : 2 * NS, :]
        back[k] = grad
        cross = cross + jnp.sum(grad * q, axis=0, keepdims=True)
        tangent = tangent + reach * q
        extra = extra + got[k, 2 * NS : 2 * NS + 2, :]
        decay = own[k, NS : NS + 1, :]
        reach = reach * decay
        grad = decay * grad + got[k, :NS, :]
    laps = send.shape[0]
    rows = NS // laps
    to_slices(send, 0, grad)
    to_slices(send, rows, tangent)
    cross = head_sums(cross)
    scalars = extra[1:] + halved(jnp.zeros((1, WIDE), F32), pair(cross[0], cross[1], 1))
    tail = jnp.concatenate([two(extra[:1]), two(scalars)], axis=1)
    for lap in range(laps):
        send[lap, :, 2 * rows * PC :] = tail


def leave_body(late, done, back, own, send, flat):
    from_slices(late, flat)
    grad = flat[...]
    at = late.shape[2] - PC
    alog = late[0, :, at:]
    for lap in range(1, late.shape[0]):
        alog = alog + late[lap, :, at:]
    alog = jnp.sum(alog, axis=1, keepdims=True) + done[:, 2 * PC - 1 :]
    skip = done[:, PC : PC + 1]
    extra = jnp.concatenate(
        [one(done[:, :PC]), pair(skip[:1], skip[1:], 1), pair(alog[:1], alog[1:], 1), jnp.zeros((5, WIDE), F32)],
        axis=0,
    )
    reach = jnp.ones((1, WIDE), F32)
    for k in reversed(range(GROUP)):
        send[k, :NS, :] = back[k] + reach * grad
        send[k, NS:, :] = extra
        reach = reach * own[k, NS : NS + 1, :]


def input_back_body(x, b, tok, gx_in, small, maps, enter, own, late, gx, ddt, gain, alog, skip, send):
    raw, step, rate = table(tok, T_RAW), table(tok, T_STEP), table(tok, T_RATE)
    logs = table(tok, T_LOGS)
    total = last(logs)
    cols = columns(jnp.exp(total - logs), step)
    decay = lanes_of(jnp.exp(total))
    db = maps[0]
    ends, xv = [], []
    lane = iota((1, HD), 1)
    a = jnp.zeros((1, HD), F32)
    s = jnp.zeros((1, HD), F32)
    for q in range(GROUP):
        grad = late[q, :NS, :]
        xq = x[:, lanes(q)].astype(F32)
        tail = pair_cols(cols, q)
        stepc = pair_cols(cols, q, HD)
        gh, gl = split(grad)
        v = tail * (mm(b[...], gh) + mm(b[...], gl))
        gx[:, lanes(q)] = (gx_in[:, lanes(q)] + stepc * v).astype(BF16)
        sh, sl = split(tail * stepc * xq)
        db = db + (mm(sh, gh, NT) + (mm(sh, gl, NT) + mm(sl, gh, NT)))
        xv += head_sums(xq * v)
        leaving = decay[q] * enter[q] + own[q, :NS, :]
        ends += whole_sums(grad * leaving)
        gain[:, lanes(q)] = late[q, NS : NS + 1, :]
        for h in range(HP):
            here = lane == q * HP + h
            s = jnp.where(here, late[q, NS + 1 : NS + 2, h * PC : h * PC + 1], s)
            a = jnp.where(here, late[q, NS + 2 : NS + 3, h * PC : h * PC + 1], a)
    alog[...] = a
    skip[...] = s
    xv = rows_of(xv)
    after = (iota((CHUNK, CHUNK), 0) >= iota((CHUNK, CHUNK), 1)).astype(F32)
    dla = jnp.dot(-step * xv, after, precision=lax.Precision.HIGHEST, preferred_element_type=F32)
    dla = small[:HD] + dla + jnp.concatenate(ends, axis=0)
    ddt[...] = (dla * rate + small[HD:] + xv) * sigmoid(raw)
    ranks = send.shape[0]
    rows = CHUNK // ranks
    for j in range(ranks):
        send[j, :rows, :] = db[j * rows : (j + 1) * rows]
        send[j, rows:, :] = maps[1, j * rows : (j + 1) * rows, :]


def sum_body(got, out):
    total = got[0]
    for q in range(1, got.shape[0]):
        total = total + got[q]
    out[...] = jnp.broadcast_to(total[None], out.shape)


def maps_body(got, db, dc):
    ranks = got.shape[0]
    rows = CHUNK // ranks
    for i in range(ranks):
        db[i * rows : (i + 1) * rows, :] = got[i, :rows, :]
        dc[i * rows : (i + 1) * rows, :] = got[i, rows:, :]


def call(body, ins, outs, scratch=(), limit=LIMIT, places=None):
    out = pl.pallas_call(
        body,
        in_specs=ins,
        out_specs=places or [VMEM] * len(outs),
        out_shape=[jax.ShapeDtypeStruct(s, t) for s, t in outs],
        scratch_shapes=scratch,
        compiler_params=pltpu.CompilerParams(vmem_limit_bytes=limit),
    )
    return out


def swap(a, axis):
    return lax.all_to_all(a, axis, 0, 0, tiled=True)


def shards(
    grad_full, keep, router_score, x_in, z_in, b_in, c_in, dt_raw, dt_bias, a_log, d_skip, norm_gain, state_in,
):
    laps = lax.axis_size("z")
    ranks = lax.axis_size("head")
    heads = dt_raw.shape[1]
    width = x_in.shape[1]
    total_width = width * ranks
    block_len = grad_full.shape[0] // keep.shape[0]
    states = ((GROUP, NS, WIDE), F32)
    slab = ((CHUNK, width), F32)
    tile = NS // laps * PC
    bind = functools.partial
    dma = pltpu.SemaphoreType.DMA
    router = router_score.reshape(1, CHUNK)
    gain = norm_gain.reshape(1, width)
    flat = pltpu.VMEM((NS, WIDE), F32)

    own, tok = call(
        own_state_body, [ANY] * 6, [((GROUP, ROWS_S, WIDE), F32), ((ROWS_T, CHUNK), F32)],
        [
            pltpu.VMEM((CHUNK, width), BF16), pltpu.VMEM((CHUNK, NS), BF16), pltpu.VMEM((heads, CHUNK), F32),
            pltpu.SMEM((heads,), F32), pltpu.SMEM((heads,), F32), pltpu.SMEM((heads,), F32),
            pltpu.VMEM((GROUP, ROWS_S, WIDE), F32), dma((5,)), dma((2, GROUP)),
        ], FULL, [ANY, VMEM],
    )(x_in, b_in, dt_raw.T, dt_bias, a_log, d_skip)
    group = swap(own, "y")
    part, send = call(group_state_body, [VMEM], [states, ((laps, HP, tile + PC), F32)])(group)
    send, decay = call(
        scan_body, [VMEM] * 2, [((laps, HP, tile), F32), ((laps, HP, PC), F32)],
        [pltpu.VMEM((NS, PC), F32), pltpu.VMEM((HP, tile), F32)],
    )(swap(send, "z"), state_in)
    (enter,) = call(enter_body, [VMEM] * 3, [states], [flat])(swap(send, "z"), group, part)
    enter = swap(enter, "y")

    y, up, stats = call(bind(output_body, block_len), [VMEM] * 9, [slab, slab, ((ranks, 2, CHUNK), F32)])(
        x_in, b_in, c_in, z_in, grad_full, keep, gain, tok, enter
    )
    grad_z, gx, send, small, maps, router_grad = call(
        bind(output_back_body, total_width), [VMEM] * 12,
        [
            ((CHUNK, width), BF16), slab, ((GROUP, ROWS_G, WIDE), F32), ((2 * HD, CHUNK), F32),
            ((2, CHUNK, NS), F32), ((1, CHUNK), F32),
        ],
    )(swap(stats, "head"), x_in, b_in, c_in, z_in, up, gain, router, tok, enter, own, y)
    back, send = call(group_back_body, [VMEM] * 2, [states, ((laps, HP, 2 * tile + 2 * PC), F32)])(
        swap(send, "y"), group
    )
    send, done = call(scan_back_body, [VMEM] * 2, [((laps, HP, tile + PC), F32), ((HP, 2 * PC), F32)])(
        swap(send, "z"), decay
    )
    (late,) = call(leave_body, [VMEM] * 4, [((GROUP, ROWS_S, WIDE), F32)], [flat])(
        swap(send, "z"), done, back, group
    )
    piece = ((ranks, 2 * CHUNK // ranks, NS), F32)
    grad_x, ddt, grad_gain, grad_alog, grad_skip, send = call(
        input_back_body, [VMEM] * 9,
        [
            ((CHUNK, width), BF16), ((heads, CHUNK), F32), ((1, width), F32), ((1, heads), F32),
            ((1, heads), F32), piece,
        ],
    )(x_in, b_in, tok, gx, small, maps, enter, own, swap(late, "y"))
    (send,) = call(sum_body, [VMEM], [piece])(swap(send, "head"))
    grad_b, grad_c = call(maps_body, [VMEM], [((CHUNK, NS), F32)] * 2)(swap(send, "head"))
    return (
        grad_x,
        grad_z,
        grad_b,
        grad_c,
        ddt.T,
        router_grad.reshape(CHUNK),
        grad_gain.reshape(width),
        grad_alog.reshape(heads),
        grad_skip.reshape(heads),
    )


def solution(mesh):
    count, heads = mesh.devices.shape
    inner = Mesh(mesh.devices.reshape(count // GROUP, GROUP, heads), ("z", "y", "head"))
    seq = ("z", "y")
    in_specs = (
        P(seq, "head"),
        P(seq, None),
        P(seq),
        P(seq, "head"),
        P(seq, "head"),
        P(seq, None),
        P(seq, None),
        P(seq, "head"),
        P("head"),
        P("head"),
        P("head"),
        P("head"),
        P("head", None, None),
    )
    out_specs = (
        P(seq, "head"),
        P(seq, "head"),
        P(seq, None),
        P(seq, None),
        P(seq, "head"),
        P(seq),
        P("head"),
        P("head"),
        P("head"),
    )
    return jax.shard_map(shards, mesh=inner, in_specs=in_specs, out_specs=out_specs, check_vma=False)
```

```python
import functools

import jax
import jax.numpy as jnp
import numpy as np
from jax import lax
from jax.experimental import pallas as pl
from jax.experimental.pallas import tpu as pltpu
from jax.sharding import Mesh
from jax.sharding import PartitionSpec as P

EPS = 1e-05
GROUP = 4
CHUNK = 128
HP = 2
PC = 128
NS = 128
WIDE = HP * PC
F32 = jnp.float32
BF16 = jnp.bfloat16
NN = ((1,), (0,))
NT = ((1,), (1,))

HD = GROUP * HP
ROWS_S = NS + 8
ROWS_G = 2 * NS + 8

VMEM = pl.BlockSpec(memory_space=pltpu.VMEM)
SMEM = pl.BlockSpec(memory_space=pltpu.SMEM)
ANY = pl.BlockSpec(memory_space=pl.ANY)
LIMIT = 24 * 2**20
FULL = 56 * 2**20


def mm(a, b, dims=NN):
    return lax.dot_general(a, b, (dims, ((), ())), preferred_element_type=F32)


def split(a):
    high = a.astype(BF16)
    return high, (a - high.astype(F32)).astype(BF16)


def stack(parts, dim):
    return jnp.concatenate(parts, axis=dim)


def mm_left(a, exact, dims=NN):
    return mm(stack(split(a), 1), stack([exact, exact], dims[1][0]), dims)


def mm_right(exact, b, dims=NN):
    return mm(stack([exact, exact], 1), stack(split(b), dims[1][0]), dims)


def mm_halves(a, b, dims=NN):
    (ah, al), (bh, bl) = a, b
    return mm(stack([ah, al], 1), stack([bh, bh], dims[1][0]), dims) + mm(ah, bl, dims)


def mm_both(a, b, dims=NN):
    return mm_halves(split(a), split(b), dims)


def iota(shape, dim):
    return lax.broadcasted_iota(jnp.int32, shape, dim)


def softplus(v):
    return jnp.maximum(v, 0.0) + jnp.log1p(jnp.exp(-jnp.abs(v)))


def sigmoid(v):
    return 1.0 / (1.0 + jnp.exp(-v))


def own_heads():
    return lax.axis_index("y") * HP


def head_col(ref):
    row = iota((HD, 1), 0)
    out = jnp.zeros((HD, 1), F32)
    for h in range(HD):
        out = jnp.where(row == h, ref[h], out)
    return out


T_RAW, T_STEP, T_LA, T_LOGS, T_RATE, T_SKIP, ROWS_T = (HD * i for i in range(7))


def table(tok, at):
    return tok[at : at + HD, :]


def last(rows):
    return rows[:, CHUNK - 1 :]


def columns(*rows):
    count = sum(r.shape[0] for r in rows)
    return jnp.concatenate(rows + (jnp.zeros((CHUNK - count, CHUNK), F32),), axis=0).T


def rows_of(cols):
    pad = jnp.zeros((CHUNK, CHUNK - len(cols)), F32)
    return jnp.concatenate(list(cols) + [pad], axis=1).T[: len(cols)]


def pair(a, b, rows):
    return jnp.concatenate(
        [jnp.broadcast_to(a, (rows, PC)), jnp.broadcast_to(b, (rows, PC))], axis=1
    )


def lanes_of(values):
    return [pair(values[q * HP : q * HP + 1], values[q * HP + 1 : q * HP + 2], 1) for q in range(GROUP)]


def pair_cols(cols, q, at=0):
    c = at + q * HP
    return pair(cols[:, c : c + 1], cols[:, c + 1 : c + 2], CHUNK)


def head_sums(a):
    return [jnp.sum(a[:, h * PC : (h + 1) * PC], axis=1, keepdims=True) for h in range(HP)]


def whole_sums(a):
    return head_sums(jnp.sum(a, axis=0, keepdims=True))


def halved(a, b):
    return jnp.where(iota((1, WIDE), 1) % PC < PC // 2, a, b)


def two(row):
    return jnp.concatenate([row[:, :PC], row[:, PC:]], axis=0)


def one(rows):
    return jnp.concatenate([rows[:1], rows[1:]], axis=1)


def lanes(q):
    return slice(q * WIDE, (q + 1) * WIDE)


def own_state_body(
    x_hbm, b_hbm, dt_hbm, bias_hbm, alog_hbm, skip_hbm, send_hbm, tok, x, b, dt_t, bias, alog, skip, send, sem, quarter
):
    copies = [
        pltpu.make_async_copy(src, dst, sem.at[i])
        for i, (src, dst) in enumerate(
            [(dt_hbm, dt_t), (bias_hbm, bias), (alog_hbm, alog), (skip_hbm, skip), (b_hbm, b), (x_hbm, x)]
        )
    ]
    stores = [pltpu.make_async_copy(send.at[q], send_hbm.at[q], quarter.at[q]) for q in range(GROUP)]
    for copy in copies:
        copy.start()
    for copy in copies:
        copy.wait()
    raw = dt_t[...] + head_col(bias)
    step = softplus(raw)
    rate = -jnp.exp(head_col(alog))
    la = step * rate
    upper = (iota((CHUNK, CHUNK), 0) <= iota((CHUNK, CHUNK), 1)).astype(F32)
    logs = jnp.dot(la, upper, precision=lax.Precision.HIGHEST, preferred_element_type=F32)
    for at, value in (
        (T_RAW, raw), (T_STEP, step), (T_LA, la), (T_LOGS, logs), (T_RATE, rate), (T_SKIP, head_col(skip))
    ):
        tok[at : at + HD, :] = jnp.broadcast_to(value, (HD, CHUNK))
    cols = columns(jnp.exp(last(logs) - logs) * step)
    decay = lanes_of(jnp.exp(last(logs)))
    b_t = b[...].astype(F32).T.astype(BF16)
    for q in range(GROUP):
        send[q, :NS, :] = mm_right(b_t, x[:, lanes(q)].astype(F32) * pair_cols(cols, q))
        send[q, NS:, :] = jnp.broadcast_to(decay[q], (8, WIDE))
        stores[q].start()
    for q in range(GROUP):
        stores[q].wait()


def to_slices(out, at, state):
    rows = NS // out.shape[0]
    for n in range(NS):
        tile = slice((at + n % rows) * PC, (at + n % rows + 1) * PC)
        out[n // rows, :, tile] = jnp.concatenate([state[n : n + 1, :PC], state[n : n + 1, PC:]], axis=0)


def from_slices(ref, out):
    rows = NS // ref.shape[0]
    for n in range(NS):
        tile = slice(n % rows * PC, (n % rows + 1) * PC)
        for h in range(HP):
            out[n : n + 1, h * PC : (h + 1) * PC] = ref[n // rows, h : h + 1, tile]


def group_state_body(got, part, send):
    state = got[0, :NS, :]
    whole = got[0, NS : NS + 1, :]
    part[0] = state
    for k in range(1, GROUP):
        decay = got[k, NS : NS + 1, :]
        state = decay * state + got[k, :NS, :]
        whole = whole * decay
        part[k] = state
    to_slices(send, 0, state)
    for lap in range(send.shape[0]):
        send[lap, :, send.shape[2] - PC :] = two(whole)
def spread(row, count):
    return jnp.concatenate([row] * count, axis=1)


def scan_body(got, state_in, out, decay, flat, first):
    laps, _, lanes = out.shape
    rows = lanes // PC
    base = own_heads()
    for h in range(HP):
        flat[...] = state_in[base + h].T
        for j in range(rows):
            first[h : h + 1, j * PC : (j + 1) * PC] = flat[pl.ds(lax.axis_index("z") * rows + j, 1), :]
    state = first[...]
    for lap in range(laps):
        out[lap] = state
        factor = got[lap, :, lanes:]
        decay[lap] = factor
        state = spread(factor, rows) * state + got[lap, :, :lanes]


def scan_back_body(got, decay, out, done):
    laps = got.shape[0]
    lanes = out.shape[2] - PC
    rows = lanes // PC
    state = jnp.zeros((HP, lanes), F32)
    cross = jnp.zeros((HP, lanes), F32)
    total = jnp.zeros((HP, 2 * PC), F32)
    for lap in reversed(range(laps)):
        out[lap, :, :lanes] = state
        cross = cross + state * got[lap, :, lanes : 2 * lanes]
        state = spread(decay[lap], rows) * state + got[lap, :, :lanes]
        total = total + got[lap, :, 2 * lanes :]
    done[...] = total
    extra = cross[:, :PC]
    for j in range(1, rows):
        extra = extra + cross[:, j * PC : (j + 1) * PC]
    for lap in range(laps):
        out[lap, :, lanes:] = extra


def enter_body(got, own, part, send, flat):
    from_slices(got, flat)
    state = flat[...]
    send[0] = state
    reach = own[0, NS : NS + 1, :]
    for k in range(1, GROUP):
        send[k] = part[k - 1] + reach * state
        reach = reach * own[k, NS : NS + 1, :]


def decays(logs, cols, r, lower):
    diff = cols[:, r : r + 1] - logs[r : r + 1]
    return jnp.where(lower, jnp.exp(jnp.where(lower, diff, 0.0)), 0.0)


def output_body(block_len, x, b, c, z, grad_full, keep, gain, tok, enter, y_out, up, stats):
    blocks, kept = keep.shape
    for i in range(blocks):
        pick = (iota((kept, block_len), 1) == keep[i : i + 1, :].T).astype(BF16)
        up[i * kept : (i + 1) * kept, :] = mm(pick, grad_full[i * block_len : (i + 1) * block_len, :])
    logs, step = table(tok, T_LOGS), table(tok, T_STEP)
    cols = columns(logs, jnp.exp(logs))
    lower = iota((CHUNK, CHUNK), 0) >= iota((CHUNK, CHUNK), 1)
    d = lanes_of(last(table(tok, T_SKIP)))
    scores = mm(c[...], b[...], NT)
    squares = jnp.zeros((CHUNK, 1), F32)
    crosses = jnp.zeros((CHUNK, 1), F32)
    for q in range(GROUP):
        inner = []
        for h in range(HP):
            r = q * HP + h
            mixed = decays(logs, cols, r, lower) * scores * step[r : r + 1]
            inner.append(mm_left(mixed, x[:, r * PC : (r + 1) * PC]))
        carried = mm_right(c[...], enter[q]) * pair_cols(cols, q, HD)
        y = jnp.concatenate(inner, axis=1) + carried + d[q] * x[:, lanes(q)].astype(F32)
        y_out[:, lanes(q)] = y
        zq = z[:, lanes(q)].astype(F32)
        gated = y * zq * sigmoid(zq)
        squares = squares + jnp.sum(gated * gated, axis=1, keepdims=True)
        crosses = crosses + jnp.sum(up[:, lanes(q)] * gated * gain[:, lanes(q)], axis=1, keepdims=True)
    stats[...] = jnp.broadcast_to(rows_of([squares, crosses])[None], stats.shape)


def output_back_body(
    total_width, stats, x, b, c, z, up, gain, router, tok, enter, own, y_in,
    gz, gx_out, send, small, maps, router_grad,
):
    sums = stats[0]
    for i in range(1, stats.shape[0]):
        sums = sums + stats[i]
    rstd = lax.rsqrt(sums[:1] / total_width + EPS)
    cross = sums[1:]
    router_grad[...] = rstd * cross
    logs, step, la = table(tok, T_LOGS), table(tok, T_STEP), table(tok, T_LA)
    total = last(logs)
    tail = jnp.exp(total - logs)
    cols = columns(
        logs, jnp.exp(logs), step, tail * step * logs,
        rstd * router[...], rstd * rstd * rstd * (router[...] * cross / total_width),
    )
    at_a = 4 * HD
    lower = iota((CHUNK, CHUNK), 0) >= iota((CHUNK, CHUNK), 1)
    upper = iota((CHUNK, CHUNK), 0) <= iota((CHUNK, CHUNK), 1)
    d = lanes_of(last(table(tok, T_SKIP)))
    decay = lanes_of(jnp.exp(total))
    near = lanes_of(total)
    scores_t = mm(b[...], c[...], NT)
    b_t = b[...].astype(F32).T.astype(BF16)
    c_t = c[...].astype(F32).T.astype(BF16)
    dscores = jnp.zeros((CHUNK, CHUNK), F32)
    dc = jnp.zeros((CHUNK, NS), F32)
    dots, xv, shared, skips = [], [], [], []
    for q in range(GROUP):
        xb = x[:, lanes(q)]
        xq, zq, u, y = xb.astype(F32), z[:, lanes(q)].astype(F32), up[:, lanes(q)], y_in[:, lanes(q)]
        sig = sigmoid(zq)
        gate = zq * sig
        gated = y * gate
        scaled = cols[:, at_a : at_a + 1] * u
        gg = scaled * gain[:, lanes(q)] - gated * cols[:, at_a + 1 : at_a + 2]
        gz[:, lanes(q)] = (gg * y * sig * (1.0 + zq * (1.0 - sig))).astype(BF16)
        gy = gg * gate
        shared.append(jnp.sum(scaled * gated, axis=0, keepdims=True))
        skips += whole_sums(gy * xq)
        dots += head_sums(gy * (y - d[q] * xq))
        gh, gl = split(gy)
        inner = []
        for h in range(HP):
            r = q * HP + h
            sl = slice(h * PC, (h + 1) * PC)
            dmixed = mm(stack([gh[:, sl], gl[:, sl]], 1), stack([xb[:, sl], xb[:, sl]], 1), NT)
            dscores = dscores + decays(logs, cols, r, lower) * dmixed * step[r : r + 1]
            diff = logs[r : r + 1] - cols[:, r : r + 1]
            mixed_t = jnp.where(upper, jnp.exp(jnp.where(upper, diff, 0.0)), 0.0) * scores_t
            inner.append(mm_halves(split(mixed_t), (gh[:, sl], gl[:, sl])))
        v = jnp.concatenate(inner, axis=1)
        gx_out[:, lanes(q)] = pair_cols(cols, q, 2 * HD) * v + d[q] * gy
        xv += head_sums(xq * v)
        eg = pair_cols(cols, q, HD) * gy
        dc = dc + mm_both(eg, enter[q], NT)
        send[q, :NS, :] = mm_right(c_t, eg)
        leaving = decay[q] * enter[q] + own[q, :NS, :]
        send[q, NS : 2 * NS, :] = near[q] * leaving - mm_right(b_t, xq * pair_cols(cols, q, 3 * HD))
    maps[0] = mm_left(dscores.T, c[...])
    maps[1] = dc + mm_left(dscores, b[...])
    xv = rows_of(xv)
    after = (iota((CHUNK, CHUNK), 0) >= iota((CHUNK, CHUNK), 1)).astype(F32)
    dla = jnp.dot(rows_of(dots) - step * xv, after, precision=lax.Precision.HIGHEST, preferred_element_type=F32)
    small[:HD] = dla
    small[HD:] = xv
    alogs = jnp.sum(dla * la, axis=1, keepdims=True)
    for q in range(GROUP):
        r = q * HP
        row = halved(pair(skips[r], skips[r + 1], 1), pair(alogs[r : r + 1], alogs[r + 1 : r + 2], 1))
        send[q, 2 * NS :, :] = jnp.concatenate([shared[q], row, jnp.zeros((6, WIDE), F32)], axis=0)


def group_back_body(got, own, back, send):
    grad = got[GROUP - 1, :NS, :]
    tangent = got[GROUP - 1, NS : 2 * NS, :]
    reach = own[GROUP - 1, NS : NS + 1, :]
    back[GROUP - 1] = jnp.zeros((NS, WIDE), F32)
    extra = got[GROUP - 1, 2 * NS : 2 * NS + 2, :]
    cross = jnp.zeros((1, WIDE), F32)
    for k in reversed(range(GROUP - 1)):
        q = got[k, NS : 2 * NS, :]
        back[k] = grad
        cross = cross + jnp.sum(grad * q, axis=0, keepdims=True)
        tangent = tangent + reach * q
        extra = extra + got[k, 2 * NS : 2 * NS + 2, :]
        decay = own[k, NS : NS + 1, :]
        reach = reach * decay
        grad = decay * grad + got[k, :NS, :]
    laps = send.shape[0]
    rows = NS // laps
    to_slices(send, 0, grad)
    to_slices(send, rows, tangent)
    cross = head_sums(cross)
    scalars = extra[1:] + halved(jnp.zeros((1, WIDE), F32), pair(cross[0], cross[1], 1))
    tail = jnp.concatenate([two(extra[:1]), two(scalars)], axis=1)
    for lap in range(laps):
        send[lap, :, 2 * rows * PC :] = tail


def leave_body(late, done, back, own, send, flat):
    from_slices(late, flat)
    grad = flat[...]
    at = late.shape[2] - PC
    alog = late[0, :, at:]
    for lap in range(1, late.shape[0]):
        alog = alog + late[lap, :, at:]
    alog = jnp.sum(alog, axis=1, keepdims=True) + done[:, 2 * PC - 1 :]
    skip = done[:, PC : PC + 1]
    extra = jnp.concatenate(
        [one(done[:, :PC]), pair(skip[:1], skip[1:], 1), pair(alog[:1], alog[1:], 1), jnp.zeros((5, WIDE), F32)],
        axis=0,
    )
    reach = jnp.ones((1, WIDE), F32)
    for k in reversed(range(GROUP)):
        send[k, :NS, :] = back[k] + reach * grad
        send[k, NS:, :] = extra
        reach = reach * own[k, NS : NS + 1, :]


def input_back_body(x, b, tok, gx_in, small, maps, enter, own, late, gx, ddt, gain, alog, skip, send):
    raw, step, rate = table(tok, T_RAW), table(tok, T_STEP), table(tok, T_RATE)
    logs = table(tok, T_LOGS)
    total = last(logs)
    cols = columns(jnp.exp(total - logs), step)
    decay = lanes_of(jnp.exp(total))
    db = maps[0]
    ends, xv = [], []
    lane = iota((1, HD), 1)
    a = jnp.zeros((1, HD), F32)
    s = jnp.zeros((1, HD), F32)
    for q in range(GROUP):
        grad = late[q, :NS, :]
        xq = x[:, lanes(q)].astype(F32)
        tail = pair_cols(cols, q)
        stepc = pair_cols(cols, q, HD)
        v = tail * mm_right(b[...], grad)
        gx[:, lanes(q)] = (gx_in[:, lanes(q)] + stepc * v).astype(BF16)
        db = db + mm_both(tail * stepc * xq, grad, NT)
        xv += head_sums(xq * v)
        leaving = decay[q] * enter[q] + own[q, :NS, :]
        ends += whole_sums(grad * leaving)
        gain[:, lanes(q)] = late[q, NS : NS + 1, :]
        for h in range(HP):
            here = lane == q * HP + h
            s = jnp.where(here, late[q, NS + 1 : NS + 2, h * PC : h * PC + 1], s)
            a = jnp.where(here, late[q, NS + 2 : NS + 3, h * PC : h * PC + 1], a)
    alog[...] = a
    skip[...] = s
    xv = rows_of(xv)
    after = (iota((CHUNK, CHUNK), 0) >= iota((CHUNK, CHUNK), 1)).astype(F32)
    dla = jnp.dot(-step * xv, after, precision=lax.Precision.HIGHEST, preferred_element_type=F32)
    dla = small[:HD] + dla + jnp.concatenate(ends, axis=0)
    ddt[...] = (dla * rate + small[HD:] + xv) * sigmoid(raw)
    ranks = send.shape[0]
    rows = CHUNK // ranks
    for j in range(ranks):
        send[j, :rows, :] = db[j * rows : (j + 1) * rows]
        send[j, rows:, :] = maps[1, j * rows : (j + 1) * rows, :]


def sum_body(got, out):
    total = got[0]
    for q in range(1, got.shape[0]):
        total = total + got[q]
    out[...] = jnp.broadcast_to(total[None], out.shape)


def maps_body(got, db, dc):
    ranks = got.shape[0]
    rows = CHUNK // ranks
    for i in range(ranks):
        db[i * rows : (i + 1) * rows, :] = got[i, :rows, :]
        dc[i * rows : (i + 1) * rows, :] = got[i, rows:, :]


def call(body, ins, outs, scratch=(), limit=LIMIT, places=None):
    out = pl.pallas_call(
        body,
        in_specs=ins,
        out_specs=places or [VMEM] * len(outs),
        out_shape=[jax.ShapeDtypeStruct(s, t) for s, t in outs],
        scratch_shapes=scratch,
        compiler_params=pltpu.CompilerParams(vmem_limit_bytes=limit),
    )
    return out


def swap(a, axis):
    return lax.all_to_all(a, axis, 0, 0, tiled=True)


def shards(
    grad_full, keep, router_score, x_in, z_in, b_in, c_in, dt_raw, dt_bias, a_log, d_skip, norm_gain, state_in,
):
    laps = lax.axis_size("z")
    ranks = lax.axis_size("head")
    heads = dt_raw.shape[1]
    width = x_in.shape[1]
    total_width = width * ranks
    block_len = grad_full.shape[0] // keep.shape[0]
    states = ((GROUP, NS, WIDE), F32)
    slab = ((CHUNK, width), F32)
    tile = NS // laps * PC
    bind = functools.partial
    dma = pltpu.SemaphoreType.DMA
    router = router_score.reshape(1, CHUNK)
    gain = norm_gain.reshape(1, width)
    flat = pltpu.VMEM((NS, WIDE), F32)

    own, tok = call(
        own_state_body, [ANY] * 6, [((GROUP, ROWS_S, WIDE), F32), ((ROWS_T, CHUNK), F32)],
        [
            pltpu.VMEM((CHUNK, width), BF16), pltpu.VMEM((CHUNK, NS), BF16), pltpu.VMEM((heads, CHUNK), F32),
            pltpu.SMEM((heads,), F32), pltpu.SMEM((heads,), F32), pltpu.SMEM((heads,), F32),
            pltpu.VMEM((GROUP, ROWS_S, WIDE), F32), dma((6,)), dma((GROUP,)),
        ], FULL, [ANY, VMEM],
    )(x_in, b_in, dt_raw.T, dt_bias, a_log, d_skip)
    group = swap(own, "y")
    part, send = call(group_state_body, [VMEM], [states, ((laps, HP, tile + PC), F32)])(group)
    send, decay = call(
        scan_body, [VMEM] * 2, [((laps, HP, tile), F32), ((laps, HP, PC), F32)],
        [pltpu.VMEM((NS, PC), F32), pltpu.VMEM((HP, tile), F32)],
    )(swap(send, "z"), state_in)
    (enter,) = call(enter_body, [VMEM] * 3, [states], [flat])(swap(send, "z"), group, part)
    enter = swap(enter, "y")

    y, up, stats = call(bind(output_body, block_len), [VMEM] * 9, [slab, slab, ((ranks, 2, CHUNK), F32)])(
        x_in, b_in, c_in, z_in, grad_full, keep, gain, tok, enter
    )
    grad_z, gx, send, small, maps, router_grad = call(
        bind(output_back_body, total_width), [VMEM] * 12,
        [
            ((CHUNK, width), BF16), slab, ((GROUP, ROWS_G, WIDE), F32), ((2 * HD, CHUNK), F32),
            ((2, CHUNK, NS), F32), ((1, CHUNK), F32),
        ],
    )(swap(stats, "head"), x_in, b_in, c_in, z_in, up, gain, router, tok, enter, own, y)
    back, send = call(group_back_body, [VMEM] * 2, [states, ((laps, HP, 2 * tile + 2 * PC), F32)])(
        swap(send, "y"), group
    )
    send, done = call(scan_back_body, [VMEM] * 2, [((laps, HP, tile + PC), F32), ((HP, 2 * PC), F32)])(
        swap(send, "z"), decay
    )
    (late,) = call(leave_body, [VMEM] * 4, [((GROUP, ROWS_S, WIDE), F32)], [flat])(
        swap(send, "z"), done, back, group
    )
    piece = ((ranks, 2 * CHUNK // ranks, NS), F32)
    grad_x, ddt, grad_gain, grad_alog, grad_skip, send = call(
        input_back_body, [VMEM] * 9,
        [
            ((CHUNK, width), BF16), ((heads, CHUNK), F32), ((1, width), F32), ((1, heads), F32),
            ((1, heads), F32), piece,
        ],
    )(x_in, b_in, tok, gx, small, maps, enter, own, swap(late, "y"))
    (send,) = call(sum_body, [VMEM], [piece])(swap(send, "head"))
    grad_b, grad_c = call(maps_body, [VMEM], [((CHUNK, NS), F32)] * 2)(swap(send, "head"))
    return (
        grad_x,
        grad_z,
        grad_b,
        grad_c,
        ddt.T,
        router_grad.reshape(CHUNK),
        grad_gain.reshape(width),
        grad_alog.reshape(heads),
        grad_skip.reshape(heads),
    )


def solution(mesh):
    count, heads = mesh.devices.shape
    inner = Mesh(mesh.devices.reshape(count // GROUP, GROUP, heads), ("z", "y", "head"))
    seq = ("z", "y")
    in_specs = (
        P(seq, "head"),
        P(seq, None),
        P(seq),
        P(seq, "head"),
        P(seq, "head"),
        P(seq, None),
        P(seq, None),
        P(seq, "head"),
        P("head"),
        P("head"),
        P("head"),
        P("head"),
        P("head", None, None),
    )
    out_specs = (
        P(seq, "head"),
        P(seq, "head"),
        P(seq, None),
        P(seq, None),
        P(seq, "head"),
        P(seq),
        P("head"),
        P("head"),
        P("head"),
    )
    return jax.shard_map(shards, mesh=inner, in_specs=in_specs, out_specs=out_specs, check_vma=False)
```

```python
import functools

import jax
import jax.numpy as jnp
import numpy as np
from jax import lax
from jax.experimental import pallas as pl
from jax.experimental.pallas import tpu as pltpu
from jax.sharding import Mesh
from jax.sharding import PartitionSpec as P

EPS = 1e-05
GROUP = 8
CHUNK = 128
HP = 1
SUB = 2
PC = 128
NS = 128
WIDE = HP * PC
F32 = jnp.float32
BF16 = jnp.bfloat16
NN = ((1,), (0,))
NT = ((1,), (1,))

HD = GROUP * HP
ROWS_S = NS + 8
ROWS_G = 2 * NS + 8

VMEM = pl.BlockSpec(memory_space=pltpu.VMEM)
SMEM = pl.BlockSpec(memory_space=pltpu.SMEM)
ANY = pl.BlockSpec(memory_space=pl.ANY)
LIMIT = 24 * 2**20
FULL = 56 * 2**20


def mm(a, b, dims=NN):
    return lax.dot_general(a, b, (dims, ((), ())), preferred_element_type=F32)


def split(a):
    high = a.astype(BF16)
    return high, (a - high.astype(F32)).astype(BF16)


def stack(parts, dim):
    return jnp.concatenate(parts, axis=dim)


def mm_left(a, exact, dims=NN):
    return mm(stack(split(a), 1), stack([exact, exact], dims[1][0]), dims)


def mm_right(exact, b, dims=NN):
    return mm(stack([exact, exact], 1), stack(split(b), dims[1][0]), dims)


def mm_halves(a, b, dims=NN):
    (ah, al), (bh, bl) = a, b
    return mm(stack([ah, al], 1), stack([bh, bh], dims[1][0]), dims) + mm(ah, bl, dims)


def mm_both(a, b, dims=NN):
    return mm_halves(split(a), split(b), dims)


def iota(shape, dim):
    return lax.broadcasted_iota(jnp.int32, shape, dim)


def softplus(v):
    return jnp.maximum(v, 0.0) + jnp.log1p(jnp.exp(-jnp.abs(v)))


def sigmoid(v):
    return 1.0 / (1.0 + jnp.exp(-v))


def head_col(ref):
    row = iota((HD, 1), 0)
    out = jnp.zeros((HD, 1), F32)
    for h in range(HD):
        out = jnp.where(row == h, ref[h], out)
    return out


T_RAW, T_STEP, T_LA, T_LOGS, T_RATE, T_SKIP, ROWS_T = (HD * i for i in range(7))


def table(tok, at):
    return tok[at : at + HD, :]


def last(rows):
    return rows[:, CHUNK - 1 :]


def columns(*rows):
    count = sum(r.shape[0] for r in rows)
    return jnp.concatenate(rows + (jnp.zeros((CHUNK - count, CHUNK), F32),), axis=0).T


def rows_of(cols):
    pad = jnp.zeros((CHUNK, CHUNK - len(cols)), F32)
    return jnp.concatenate(list(cols) + [pad], axis=1).T[: len(cols)]


def over(value, rows=1):
    return jnp.broadcast_to(value, (rows, WIDE))


def lanes_of(values):
    return [over(values[q : q + 1]) for q in range(GROUP)]


def head_cols(cols, q, at=0):
    return over(cols[:, at + q : at + q + 1], CHUNK)


def head_sums(a):
    return [jnp.sum(a[:, h * PC : (h + 1) * PC], axis=1, keepdims=True) for h in range(HP)]


def whole_sums(a):
    return head_sums(jnp.sum(a, axis=0, keepdims=True))


def halved(a, b):
    return jnp.where(iota((1, WIDE), 1) % PC < PC // 2, a, b)


def lanes(q):
    return slice(q * WIDE, (q + 1) * WIDE)


def own_state_body(
    x_hbm, b_hbm, dt_hbm, bias_hbm, alog_hbm, skip_hbm, send, tok, x, b, dt_t, bias, alog, skip, sem
):
    copies = [
        pltpu.make_async_copy(src, dst, sem.at[i])
        for i, (src, dst) in enumerate(
            [(dt_hbm, dt_t), (bias_hbm, bias), (alog_hbm, alog), (skip_hbm, skip), (b_hbm, b), (x_hbm, x)]
        )
    ]
    for copy in copies:
        copy.start()
    for copy in copies:
        copy.wait()
    raw = dt_t[...] + head_col(bias)
    step = softplus(raw)
    rate = -jnp.exp(head_col(alog))
    la = step * rate
    upper = (iota((CHUNK, CHUNK), 0) <= iota((CHUNK, CHUNK), 1)).astype(F32)
    logs = jnp.dot(la, upper, precision=lax.Precision.HIGHEST, preferred_element_type=F32)
    for at, value in (
        (T_RAW, raw), (T_STEP, step), (T_LA, la), (T_LOGS, logs), (T_RATE, rate), (T_SKIP, head_col(skip))
    ):
        tok[at : at + HD, :] = jnp.broadcast_to(value, (HD, CHUNK))
    cols = columns(jnp.exp(last(logs) - logs) * step)
    decay = lanes_of(jnp.exp(last(logs)))
    b_t = b[...].astype(F32).T.astype(BF16)
    for q in range(GROUP):
        send[q, :NS, :] = mm_right(b_t, x[:, lanes(q)].astype(F32) * head_cols(cols, q))
        send[q, NS:, :] = jnp.broadcast_to(decay[q], (8, WIDE))


def to_slices(out, at, state):
    rows = NS // out.shape[0]
    for n in range(0, NS, SUB):
        tile = at + n % rows // SUB
        out[n // rows, :, tile * PC : (tile + 1) * PC] = state[n : n + SUB, :]


def from_slices(ref, out):
    rows = NS // ref.shape[0]
    for n in range(0, NS, SUB):
        tile = n % rows // SUB
        out[n : n + SUB, :] = ref[n // rows, :, tile * PC : (tile + 1) * PC]


def group_state_body(got, part, send):
    state = got[0, :NS, :]
    whole = got[0, NS : NS + 1, :]
    part[0] = state
    for k in range(1, GROUP):
        decay = got[k, NS : NS + 1, :]
        state = decay * state + got[k, :NS, :]
        whole = whole * decay
        part[k] = state
    to_slices(send, 0, state)
    for lap in range(send.shape[0]):
        send[lap, :, send.shape[2] - PC :] = jnp.broadcast_to(whole, (SUB, PC))
def spread(row, count):
    return jnp.concatenate([row] * count, axis=1)


def scan_body(got, state_in, out, decay, flat, first):
    laps, _, width = out.shape
    tiles = width // PC
    flat[...] = state_in[lax.axis_index("y")].T
    for j in range(tiles):
        for r in range(SUB):
            row = lax.axis_index("z") * (tiles * SUB) + (j * SUB + r)
            first[r : r + 1, j * PC : (j + 1) * PC] = flat[pl.ds(row, 1), :]
    state = first[...]
    for lap in range(laps):
        out[lap] = state
        factor = got[lap, :, width:]
        decay[lap] = factor
        state = spread(factor, tiles) * state + got[lap, :, :width]


def scan_back_body(got, decay, out, done):
    laps = got.shape[0]
    width = out.shape[2] - PC
    tiles = width // PC
    state = jnp.zeros((SUB, width), F32)
    cross = jnp.zeros((SUB, width), F32)
    total = jnp.zeros((SUB, PC), F32)
    for lap in reversed(range(laps)):
        out[lap, :, :width] = state
        cross = cross + state * got[lap, :, width : 2 * width]
        state = spread(decay[lap], tiles) * state + got[lap, :, :width]
        total = total + got[lap, :, 2 * width :]
    done[...] = total
    extra = cross[:, :PC]
    for j in range(1, tiles):
        extra = extra + cross[:, j * PC : (j + 1) * PC]
    for lap in range(laps):
        out[lap, :, width:] = extra


def enter_body(got, own, part, send, flat):
    from_slices(got, flat)
    state = flat[...]
    send[0] = state
    reach = own[0, NS : NS + 1, :]
    for k in range(1, GROUP):
        send[k] = part[k - 1] + reach * state
        reach = reach * own[k, NS : NS + 1, :]


def decays(logs, cols, r, lower):
    diff = cols[:, r : r + 1] - logs[r : r + 1]
    return jnp.where(lower, jnp.exp(jnp.where(lower, diff, 0.0)), 0.0)


def output_body(block_len, x, b, c, z, grad_full, keep, gain, tok, enter, y_out, up, stats):
    blocks, kept = keep.shape
    for i in range(blocks):
        pick = (iota((kept, block_len), 1) == keep[i : i + 1, :].T).astype(BF16)
        up[i * kept : (i + 1) * kept, :] = mm(pick, grad_full[i * block_len : (i + 1) * block_len, :])
    logs, step = table(tok, T_LOGS), table(tok, T_STEP)
    cols = columns(logs, jnp.exp(logs))
    lower = iota((CHUNK, CHUNK), 0) >= iota((CHUNK, CHUNK), 1)
    d = lanes_of(last(table(tok, T_SKIP)))
    scores = mm(c[...], b[...], NT)
    squares = jnp.zeros((CHUNK, 1), F32)
    crosses = jnp.zeros((CHUNK, 1), F32)
    for q in range(GROUP):
        inner = []
        for h in range(HP):
            r = q * HP + h
            mixed = decays(logs, cols, r, lower) * scores * step[r : r + 1]
            inner.append(mm_left(mixed, x[:, r * PC : (r + 1) * PC]))
        carried = mm_right(c[...], enter[q]) * head_cols(cols, q, HD)
        y = jnp.concatenate(inner, axis=1) + carried + d[q] * x[:, lanes(q)].astype(F32)
        y_out[:, lanes(q)] = y
        zq = z[:, lanes(q)].astype(F32)
        gated = y * zq * sigmoid(zq)
        squares = squares + jnp.sum(gated * gated, axis=1, keepdims=True)
        crosses = crosses + jnp.sum(up[:, lanes(q)] * gated * gain[:, lanes(q)], axis=1, keepdims=True)
    stats[...] = jnp.broadcast_to(rows_of([squares, crosses])[None], stats.shape)


def output_back_body(
    total_width, stats, x, b, c, z, up, gain, router, tok, enter, own, y_in,
    gz, gx_out, send, small, maps, router_grad,
):
    sums = stats[0]
    for i in range(1, stats.shape[0]):
        sums = sums + stats[i]
    rstd = lax.rsqrt(sums[:1] / total_width + EPS)
    cross = sums[1:]
    router_grad[...] = rstd * cross
    logs, step, la = table(tok, T_LOGS), table(tok, T_STEP), table(tok, T_LA)
    total = last(logs)
    tail = jnp.exp(total - logs)
    cols = columns(
        logs, jnp.exp(logs), step, tail * step * logs,
        rstd * router[...], rstd * rstd * rstd * (router[...] * cross / total_width),
    )
    at_a = 4 * HD
    lower = iota((CHUNK, CHUNK), 0) >= iota((CHUNK, CHUNK), 1)
    upper = iota((CHUNK, CHUNK), 0) <= iota((CHUNK, CHUNK), 1)
    d = lanes_of(last(table(tok, T_SKIP)))
    decay = lanes_of(jnp.exp(total))
    near = lanes_of(total)
    scores_t = mm(b[...], c[...], NT)
    b_t = b[...].astype(F32).T.astype(BF16)
    c_t = c[...].astype(F32).T.astype(BF16)
    dscores = jnp.zeros((CHUNK, CHUNK), F32)
    dc = jnp.zeros((CHUNK, NS), F32)
    dots, xv, shared, skips = [], [], [], []
    for q in range(GROUP):
        xb = x[:, lanes(q)]
        xq, zq, u, y = xb.astype(F32), z[:, lanes(q)].astype(F32), up[:, lanes(q)], y_in[:, lanes(q)]
        sig = sigmoid(zq)
        gate = zq * sig
        gated = y * gate
        scaled = cols[:, at_a : at_a + 1] * u
        gg = scaled * gain[:, lanes(q)] - gated * cols[:, at_a + 1 : at_a + 2]
        gz[:, lanes(q)] = (gg * y * sig * (1.0 + zq * (1.0 - sig))).astype(BF16)
        gy = gg * gate
        shared.append(jnp.sum(scaled * gated, axis=0, keepdims=True))
        skips += whole_sums(gy * xq)
        dots += head_sums(gy * (y - d[q] * xq))
        gh, gl = split(gy)
        inner = []
        for h in range(HP):
            r = q * HP + h
            sl = slice(h * PC, (h + 1) * PC)
            dmixed = mm(stack([gh[:, sl], gl[:, sl]], 1), stack([xb[:, sl], xb[:, sl]], 1), NT)
            dscores = dscores + decays(logs, cols, r, lower) * dmixed * step[r : r + 1]
            diff = logs[r : r + 1] - cols[:, r : r + 1]
            mixed_t = jnp.where(upper, jnp.exp(jnp.where(upper, diff, 0.0)), 0.0) * scores_t
            inner.append(mm_halves(split(mixed_t), (gh[:, sl], gl[:, sl])))
        v = jnp.concatenate(inner, axis=1)
        gx_out[:, lanes(q)] = head_cols(cols, q, 2 * HD) * v + d[q] * gy
        xv += head_sums(xq * v)
        eg = head_cols(cols, q, HD) * gy
        dc = dc + mm_both(eg, enter[q], NT)
        send[q, :NS, :] = mm_right(c_t, eg)
        leaving = decay[q] * enter[q] + own[q, :NS, :]
        send[q, NS : 2 * NS, :] = near[q] * leaving - mm_right(b_t, xq * head_cols(cols, q, 3 * HD))
    maps[0] = mm_left(dscores.T, c[...])
    maps[1] = dc + mm_left(dscores, b[...])
    xv = rows_of(xv)
    after = (iota((CHUNK, CHUNK), 0) >= iota((CHUNK, CHUNK), 1)).astype(F32)
    dla = jnp.dot(rows_of(dots) - step * xv, after, precision=lax.Precision.HIGHEST, preferred_element_type=F32)
    small[:HD] = dla
    small[HD:] = xv
    alogs = jnp.sum(dla * la, axis=1, keepdims=True)
    for q in range(GROUP):
        row = halved(over(skips[q]), over(alogs[q : q + 1]))
        send[q, 2 * NS :, :] = jnp.concatenate([shared[q], row, jnp.zeros((6, WIDE), F32)], axis=0)


def group_back_body(got, own, back, send):
    grad = got[GROUP - 1, :NS, :]
    tangent = got[GROUP - 1, NS : 2 * NS, :]
    reach = own[GROUP - 1, NS : NS + 1, :]
    back[GROUP - 1] = jnp.zeros((NS, WIDE), F32)
    extra = got[GROUP - 1, 2 * NS : 2 * NS + 2, :]
    cross = jnp.zeros((1, WIDE), F32)
    for k in reversed(range(GROUP - 1)):
        q = got[k, NS : 2 * NS, :]
        back[k] = grad
        cross = cross + jnp.sum(grad * q, axis=0, keepdims=True)
        tangent = tangent + reach * q
        extra = extra + got[k, 2 * NS : 2 * NS + 2, :]
        decay = own[k, NS : NS + 1, :]
        reach = reach * decay
        grad = decay * grad + got[k, :NS, :]
    laps = send.shape[0]
    tiles = NS // laps // SUB
    to_slices(send, 0, grad)
    to_slices(send, tiles, tangent)
    scalars = extra[1:] + halved(jnp.zeros((1, WIDE), F32), over(head_sums(cross)[0]))
    tail = jnp.concatenate([extra[:1], scalars], axis=0)
    for lap in range(laps):
        send[lap, :, 2 * tiles * PC :] = tail


def leave_body(late, done, back, own, send, flat):
    from_slices(late, flat)
    grad = flat[...]
    at = late.shape[2] - PC
    alog = late[0, :, at:]
    for lap in range(1, late.shape[0]):
        alog = alog + late[lap, :, at:]
    alog = jnp.sum(jnp.sum(alog, axis=0, keepdims=True), axis=1, keepdims=True) + done[1:, PC - 1 :]
    extra = jnp.concatenate([done[:1], over(done[1:, :1]), over(alog), jnp.zeros((5, WIDE), F32)], axis=0)
    reach = jnp.ones((1, WIDE), F32)
    for k in reversed(range(GROUP)):
        send[k, :NS, :] = back[k] + reach * grad
        send[k, NS:, :] = extra
        reach = reach * own[k, NS : NS + 1, :]


def input_back_body(x, b, tok, gx_in, small, maps, enter, own, late, gx, ddt, gain, alog, skip, send):
    raw, step, rate = table(tok, T_RAW), table(tok, T_STEP), table(tok, T_RATE)
    logs = table(tok, T_LOGS)
    total = last(logs)
    cols = columns(jnp.exp(total - logs), step)
    decay = lanes_of(jnp.exp(total))
    db = maps[0]
    ends, xv = [], []
    lane = iota((1, HD), 1)
    a = jnp.zeros((1, HD), F32)
    s = jnp.zeros((1, HD), F32)
    for q in range(GROUP):
        grad = late[q, :NS, :]
        xq = x[:, lanes(q)].astype(F32)
        tail = head_cols(cols, q)
        stepc = head_cols(cols, q, HD)
        v = tail * mm_right(b[...], grad)
        gx[:, lanes(q)] = (gx_in[:, lanes(q)] + stepc * v).astype(BF16)
        db = db + mm_both(tail * stepc * xq, grad, NT)
        xv += head_sums(xq * v)
        leaving = decay[q] * enter[q] + own[q, :NS, :]
        ends += whole_sums(grad * leaving)
        gain[:, lanes(q)] = late[q, NS : NS + 1, :]
        for h in range(HP):
            here = lane == q * HP + h
            s = jnp.where(here, late[q, NS + 1 : NS + 2, h * PC : h * PC + 1], s)
            a = jnp.where(here, late[q, NS + 2 : NS + 3, h * PC : h * PC + 1], a)
    alog[...] = a
    skip[...] = s
    xv = rows_of(xv)
    after = (iota((CHUNK, CHUNK), 0) >= iota((CHUNK, CHUNK), 1)).astype(F32)
    dla = jnp.dot(-step * xv, after, precision=lax.Precision.HIGHEST, preferred_element_type=F32)
    dla = small[:HD] + dla + jnp.concatenate(ends, axis=0)
    ddt[...] = (dla * rate + small[HD:] + xv) * sigmoid(raw)
    ranks = send.shape[0]
    rows = CHUNK // ranks
    for j in range(ranks):
        send[j, :rows, :] = db[j * rows : (j + 1) * rows]
        send[j, rows:, :] = maps[1, j * rows : (j + 1) * rows, :]


def sum_body(got, out):
    total = got[0]
    for q in range(1, got.shape[0]):
        total = total + got[q]
    out[...] = jnp.broadcast_to(total[None], out.shape)


def maps_body(got, db, dc):
    ranks = got.shape[0]
    rows = CHUNK // ranks
    for i in range(ranks):
        db[i * rows : (i + 1) * rows, :] = got[i, :rows, :]
        dc[i * rows : (i + 1) * rows, :] = got[i, rows:, :]


def call(body, ins, outs, scratch=(), limit=LIMIT):
    out = pl.pallas_call(
        body,
        in_specs=ins,
        out_specs=[VMEM] * len(outs),
        out_shape=[jax.ShapeDtypeStruct(s, t) for s, t in outs],
        scratch_shapes=scratch,
        compiler_params=pltpu.CompilerParams(vmem_limit_bytes=limit),
    )
    return out


def swap(a, axis):
    return lax.all_to_all(a, axis, 0, 0, tiled=True)


def shards(
    grad_full, keep, router_score, x_in, z_in, b_in, c_in, dt_raw, dt_bias, a_log, d_skip, norm_gain, state_in,
):
    laps = lax.axis_size("z")
    ranks = lax.axis_size("head")
    heads = dt_raw.shape[1]
    width = x_in.shape[1]
    total_width = width * ranks
    block_len = grad_full.shape[0] // keep.shape[0]
    states = ((GROUP, NS, WIDE), F32)
    slab = ((CHUNK, width), F32)
    tile = NS // laps // SUB * PC
    bind = functools.partial
    dma = pltpu.SemaphoreType.DMA
    router = router_score.reshape(1, CHUNK)
    gain = norm_gain.reshape(1, width)
    flat = pltpu.VMEM((NS, WIDE), F32)

    own, tok = call(
        own_state_body, [ANY] * 6, [((GROUP, ROWS_S, WIDE), F32), ((ROWS_T, CHUNK), F32)],
        [
            pltpu.VMEM((CHUNK, width), BF16), pltpu.VMEM((CHUNK, NS), BF16), pltpu.VMEM((heads, CHUNK), F32),
            pltpu.SMEM((heads,), F32), pltpu.SMEM((heads,), F32), pltpu.SMEM((heads,), F32),
            dma((6,)),
        ], FULL,
    )(x_in, b_in, dt_raw.T, dt_bias, a_log, d_skip)
    group = swap(own, "y")
    part, send = call(group_state_body, [VMEM], [states, ((laps, SUB, tile + PC), F32)])(group)
    send, decay = call(
        scan_body, [VMEM] * 2, [((laps, SUB, tile), F32), ((laps, SUB, PC), F32)],
        [pltpu.VMEM((NS, PC), F32), pltpu.VMEM((SUB, tile), F32)],
    )(swap(send, "z"), state_in)
    (enter,) = call(enter_body, [VMEM] * 3, [states], [flat])(swap(send, "z"), group, part)
    enter = swap(enter, "y")

    y, up, stats = call(bind(output_body, block_len), [VMEM] * 9, [slab, slab, ((ranks, 2, CHUNK), F32)])(
        x_in, b_in, c_in, z_in, grad_full, keep, gain, tok, enter
    )
    grad_z, gx, send, small, maps, router_grad = call(
        bind(output_back_body, total_width), [VMEM] * 12,
        [
            ((CHUNK, width), BF16), slab, ((GROUP, ROWS_G, WIDE), F32), ((2 * HD, CHUNK), F32),
            ((2, CHUNK, NS), F32), ((1, CHUNK), F32),
        ],
    )(swap(stats, "head"), x_in, b_in, c_in, z_in, up, gain, router, tok, enter, own, y)
    back, send = call(group_back_body, [VMEM] * 2, [states, ((laps, SUB, 2 * tile + PC), F32)])(
        swap(send, "y"), group
    )
    send, done = call(scan_back_body, [VMEM] * 2, [((laps, SUB, tile + PC), F32), ((SUB, PC), F32)])(
        swap(send, "z"), decay
    )
    (late,) = call(leave_body, [VMEM] * 4, [((GROUP, ROWS_S, WIDE), F32)], [flat])(
        swap(send, "z"), done, back, group
    )
    piece = ((ranks, 2 * CHUNK // ranks, NS), F32)
    grad_x, ddt, grad_gain, grad_alog, grad_skip, send = call(
        input_back_body, [VMEM] * 9,
        [
            ((CHUNK, width), BF16), ((heads, CHUNK), F32), ((1, width), F32), ((1, heads), F32),
            ((1, heads), F32), piece,
        ],
    )(x_in, b_in, tok, gx, small, maps, enter, own, swap(late, "y"))
    (send,) = call(sum_body, [VMEM], [piece])(swap(send, "head"))
    grad_b, grad_c = call(maps_body, [VMEM], [((CHUNK, NS), F32)] * 2)(swap(send, "head"))
    return (
        grad_x,
        grad_z,
        grad_b,
        grad_c,
        ddt.T,
        router_grad.reshape(CHUNK),
        grad_gain.reshape(width),
        grad_alog.reshape(heads),
        grad_skip.reshape(heads),
    )


def solution(mesh):
    count, heads = mesh.devices.shape
    inner = Mesh(mesh.devices.reshape(count // GROUP, GROUP, heads), ("z", "y", "head"))
    seq = ("z", "y")
    in_specs = (
        P(seq, "head"),
        P(seq, None),
        P(seq),
        P(seq, "head"),
        P(seq, "head"),
        P(seq, None),
        P(seq, None),
        P(seq, "head"),
        P("head"),
        P("head"),
        P("head"),
        P("head"),
        P("head", None, None),
    )
    out_specs = (
        P(seq, "head"),
        P(seq, "head"),
        P(seq, None),
        P(seq, None),
        P(seq, "head"),
        P(seq),
        P("head"),
        P("head"),
        P("head"),
    )
    return jax.shard_map(shards, mesh=inner, in_specs=in_specs, out_specs=out_specs, check_vma=False)
```

```python
import functools

import jax
import jax.numpy as jnp
import numpy as np
from jax import lax
from jax.experimental import pallas as pl
from jax.experimental.pallas import tpu as pltpu
from jax.sharding import Mesh
from jax.sharding import PartitionSpec as P

EPS = 1e-05
GROUP = 8
CHUNK = 128
HP = 1
PAIR = 2
SUB = 2
PC = 128
NS = 128
WIDE = HP * PC
F32 = jnp.float32
BF16 = jnp.bfloat16
NN = ((1,), (0,))
NT = ((1,), (1,))

HD = GROUP * HP
ROWS_S = NS + 8
ROWS_G = 2 * NS + 8

VMEM = pl.BlockSpec(memory_space=pltpu.VMEM)
SMEM = pl.BlockSpec(memory_space=pltpu.SMEM)
ANY = pl.BlockSpec(memory_space=pl.ANY)
LIMIT = 24 * 2**20
FULL = 56 * 2**20


def mm(a, b, dims=NN):
    return lax.dot_general(a, b, (dims, ((), ())), preferred_element_type=F32)


def split(a):
    high = a.astype(BF16)
    return high, (a - high.astype(F32)).astype(BF16)


def stack(parts, dim):
    return jnp.concatenate(parts, axis=dim)


def mm_left(a, exact, dims=NN):
    return mm(stack(split(a), 1), stack([exact, exact], dims[1][0]), dims)


def mm_right(exact, b, dims=NN):
    return mm(stack([exact, exact], 1), stack(split(b), dims[1][0]), dims)


def mm_halves(a, b, dims=NN):
    (ah, al), (bh, bl) = a, b
    return mm(stack([ah, al], 1), stack([bh, bh], dims[1][0]), dims) + mm(ah, bl, dims)


def mm_both(a, b, dims=NN):
    return mm_halves(split(a), split(b), dims)


def iota(shape, dim):
    return lax.broadcasted_iota(jnp.int32, shape, dim)


def softplus(v):
    return jnp.maximum(v, 0.0) + jnp.log1p(jnp.exp(-jnp.abs(v)))


def sigmoid(v):
    return 1.0 / (1.0 + jnp.exp(-v))


def head_col(ref):
    row = iota((HD, 1), 0)
    out = jnp.zeros((HD, 1), F32)
    for h in range(HD):
        out = jnp.where(row == h, ref[h], out)
    return out


T_RAW, T_STEP, T_LA, T_LOGS, T_RATE, T_SKIP, ROWS_T = (HD * i for i in range(7))


def table(tok, at):
    return tok[at : at + HD, :]


def last(rows):
    return rows[:, CHUNK - 1 :]


def columns(*rows):
    count = sum(r.shape[0] for r in rows)
    return jnp.concatenate(rows + (jnp.zeros((CHUNK - count, CHUNK), F32),), axis=0).T


def rows_of(cols):
    pad = jnp.zeros((CHUNK, CHUNK - len(cols)), F32)
    return jnp.concatenate(list(cols) + [pad], axis=1).T[: len(cols)]


def over(value, rows=1):
    return jnp.broadcast_to(value, (rows, WIDE))


def lanes_of(values):
    return [over(values[q : q + 1]) for q in range(GROUP)]


def head_cols(cols, q, at=0):
    return over(cols[:, at + q : at + q + 1], CHUNK)


def head_sums(a):
    return [jnp.sum(a[:, h * PC : (h + 1) * PC], axis=1, keepdims=True) for h in range(HP)]


def whole_sums(a):
    return pair_sums(jnp.sum(a, axis=0, keepdims=True))


def halved(a, b):
    return jnp.where(iota((1, WIDE), 1) % PC < PC // 2, a, b)


def pairs_of(values):
    return [jnp.concatenate([over(values[r : r + 1]), over(values[r + 1 : r + 2])], axis=1) for r in range(0, HD, PAIR)]


def both_cols(cols, q, at=0):
    c = at + q * PAIR
    return jnp.concatenate([over(cols[:, c : c + 1], CHUNK), over(cols[:, c + 1 : c + 2], CHUNK)], axis=1)


def both(ref, q, lo, hi):
    return jnp.concatenate([ref[q * PAIR, lo:hi, :], ref[q * PAIR + 1, lo:hi, :]], axis=1)


def put(ref, q, lo, hi, value):
    for h in range(PAIR):
        ref[q * PAIR + h, lo:hi, :] = value[:, h * PC : (h + 1) * PC]


def pair_sums(a):
    return [jnp.sum(a[:, h * PC : (h + 1) * PC], axis=1, keepdims=True) for h in range(PAIR)]


def two_lanes(q):
    return slice(q * PAIR * WIDE, (q + 1) * PAIR * WIDE)


def lanes(q):
    return slice(q * WIDE, (q + 1) * WIDE)


def own_state_body(
    x_hbm, b_hbm, dt_hbm, bias_hbm, alog_hbm, skip_hbm, send, tok, x, b, dt_t, bias, alog, skip, sem
):
    copies = [
        pltpu.make_async_copy(src, dst, sem.at[i])
        for i, (src, dst) in enumerate(
            [(dt_hbm, dt_t), (bias_hbm, bias), (alog_hbm, alog), (skip_hbm, skip), (b_hbm, b), (x_hbm, x)]
        )
    ]
    for copy in copies:
        copy.start()
    for copy in copies:
        copy.wait()
    raw = dt_t[...] + head_col(bias)
    step = softplus(raw)
    rate = -jnp.exp(head_col(alog))
    la = step * rate
    upper = (iota((CHUNK, CHUNK), 0) <= iota((CHUNK, CHUNK), 1)).astype(F32)
    logs = jnp.dot(la, upper, precision=lax.Precision.HIGHEST, preferred_element_type=F32)
    for at, value in (
        (T_RAW, raw), (T_STEP, step), (T_LA, la), (T_LOGS, logs), (T_RATE, rate), (T_SKIP, head_col(skip))
    ):
        tok[at : at + HD, :] = jnp.broadcast_to(value, (HD, CHUNK))
    cols = columns(jnp.exp(last(logs) - logs) * step)
    decay = lanes_of(jnp.exp(last(logs)))
    b_t = b[...].astype(F32).T.astype(BF16)
    for q in range(GROUP):
        send[q, :NS, :] = mm_right(b_t, x[:, lanes(q)].astype(F32) * head_cols(cols, q))
        send[q, NS:, :] = jnp.broadcast_to(decay[q], (8, WIDE))


def to_slices(out, at, state):
    rows = NS // out.shape[0]
    for n in range(0, NS, SUB):
        tile = at + n % rows // SUB
        out[n // rows, :, tile * PC : (tile + 1) * PC] = state[n : n + SUB, :]


def from_slices(ref, out):
    rows = NS // ref.shape[0]
    for n in range(0, NS, SUB):
        tile = n % rows // SUB
        out[n : n + SUB, :] = ref[n // rows, :, tile * PC : (tile + 1) * PC]


def group_state_body(got, part, send):
    state = got[0, :NS, :]
    whole = got[0, NS : NS + 1, :]
    part[0] = state
    for k in range(1, GROUP):
        decay = got[k, NS : NS + 1, :]
        state = decay * state + got[k, :NS, :]
        whole = whole * decay
        part[k] = state
    to_slices(send, 0, state)
    for lap in range(send.shape[0]):
        send[lap, :, send.shape[2] - PC :] = jnp.broadcast_to(whole, (SUB, PC))
def spread(row, count):
    return jnp.concatenate([row] * count, axis=1)


def scan_body(got, state_in, out, decay, flat, first):
    laps, _, width = out.shape
    tiles = width // PC
    flat[...] = state_in[lax.axis_index("y")].T
    for j in range(tiles):
        for r in range(SUB):
            row = lax.axis_index("z") * (tiles * SUB) + (j * SUB + r)
            first[r : r + 1, j * PC : (j + 1) * PC] = flat[pl.ds(row, 1), :]
    state = first[...]
    for lap in range(laps):
        out[lap] = state
        factor = got[lap, :, width:]
        decay[lap] = factor
        state = spread(factor, tiles) * state + got[lap, :, :width]


def scan_back_body(got, decay, out, done):
    laps = got.shape[0]
    width = out.shape[2] - PC
    tiles = width // PC
    state = jnp.zeros((SUB, width), F32)
    cross = jnp.zeros((SUB, width), F32)
    total = jnp.zeros((SUB, PC), F32)
    for lap in reversed(range(laps)):
        out[lap, :, :width] = state
        cross = cross + state * got[lap, :, width : 2 * width]
        state = spread(decay[lap], tiles) * state + got[lap, :, :width]
        total = total + got[lap, :, 2 * width :]
    done[...] = total
    extra = cross[:, :PC]
    for j in range(1, tiles):
        extra = extra + cross[:, j * PC : (j + 1) * PC]
    for lap in range(laps):
        out[lap, :, width:] = extra


def enter_body(got, own, part, send, flat):
    from_slices(got, flat)
    state = flat[...]
    send[0] = state
    reach = own[0, NS : NS + 1, :]
    for k in range(1, GROUP):
        send[k] = part[k - 1] + reach * state
        reach = reach * own[k, NS : NS + 1, :]


def decays(logs, cols, r, lower):
    diff = cols[:, r : r + 1] - logs[r : r + 1]
    return jnp.where(lower, jnp.exp(jnp.where(lower, diff, 0.0)), 0.0)


def output_body(block_len, x, b, c, z, grad_full, keep, gain, tok, enter, y_out, up, stats):
    blocks, kept = keep.shape
    for i in range(blocks):
        pick = (iota((kept, block_len), 1) == keep[i : i + 1, :].T).astype(BF16)
        up[i * kept : (i + 1) * kept, :] = mm(pick, grad_full[i * block_len : (i + 1) * block_len, :])
    logs, step = table(tok, T_LOGS), table(tok, T_STEP)
    cols = columns(logs, jnp.exp(logs))
    lower = iota((CHUNK, CHUNK), 0) >= iota((CHUNK, CHUNK), 1)
    d = pairs_of(last(table(tok, T_SKIP)))
    scores = mm(c[...], b[...], NT)
    squares = jnp.zeros((CHUNK, 1), F32)
    crosses = jnp.zeros((CHUNK, 1), F32)
    for q in range(HD // PAIR):
        inner = []
        for h in range(PAIR):
            r = q * PAIR + h
            mixed = decays(logs, cols, r, lower) * scores * step[r : r + 1]
            inner.append(mm_left(mixed, x[:, r * PC : (r + 1) * PC]))
        carried = mm_right(c[...], both(enter, q, 0, NS)) * both_cols(cols, q, HD)
        y = jnp.concatenate(inner, axis=1) + carried + d[q] * x[:, two_lanes(q)].astype(F32)
        y_out[:, two_lanes(q)] = y
        zq = z[:, two_lanes(q)].astype(F32)
        gated = y * zq * sigmoid(zq)
        squares = squares + jnp.sum(gated * gated, axis=1, keepdims=True)
        crosses = crosses + jnp.sum(up[:, two_lanes(q)] * gated * gain[:, two_lanes(q)], axis=1, keepdims=True)
    stats[...] = jnp.broadcast_to(rows_of([squares, crosses])[None], stats.shape)


def output_back_body(
    total_width, stats, x, b, c, z, up, gain, router, tok, enter, own, y_in,
    gz, gx_out, send, small, maps, router_grad,
):
    sums = stats[0]
    for i in range(1, stats.shape[0]):
        sums = sums + stats[i]
    rstd = lax.rsqrt(sums[:1] / total_width + EPS)
    cross = sums[1:]
    router_grad[...] = rstd * cross
    logs, step, la = table(tok, T_LOGS), table(tok, T_STEP), table(tok, T_LA)
    total = last(logs)
    tail = jnp.exp(total - logs)
    cols = columns(
        logs, jnp.exp(logs), step, tail * step * logs,
        rstd * router[...], rstd * rstd * rstd * (router[...] * cross / total_width),
    )
    at_a = 4 * HD
    lower = iota((CHUNK, CHUNK), 0) >= iota((CHUNK, CHUNK), 1)
    upper = iota((CHUNK, CHUNK), 0) <= iota((CHUNK, CHUNK), 1)
    d = pairs_of(last(table(tok, T_SKIP)))
    decay = pairs_of(jnp.exp(total))
    near = pairs_of(total)
    scores_t = mm(b[...], c[...], NT)
    b_t = b[...].astype(F32).T.astype(BF16)
    c_t = c[...].astype(F32).T.astype(BF16)
    dscores = jnp.zeros((CHUNK, CHUNK), F32)
    dc = jnp.zeros((CHUNK, NS), F32)
    dots, xv, shared, skips = [], [], [], []
    for q in range(HD // PAIR):
        xb = x[:, two_lanes(q)]
        xq, zq, u, y = xb.astype(F32), z[:, two_lanes(q)].astype(F32), up[:, two_lanes(q)], y_in[:, two_lanes(q)]
        sig = sigmoid(zq)
        gate = zq * sig
        gated = y * gate
        scaled = cols[:, at_a : at_a + 1] * u
        gg = scaled * gain[:, two_lanes(q)] - gated * cols[:, at_a + 1 : at_a + 2]
        gz[:, two_lanes(q)] = (gg * y * sig * (1.0 + zq * (1.0 - sig))).astype(BF16)
        gy = gg * gate
        shared.append(jnp.sum(scaled * gated, axis=0, keepdims=True))
        skips += whole_sums(gy * xq)
        dots += pair_sums(gy * (y - d[q] * xq))
        gh, gl = split(gy)
        inner = []
        for h in range(PAIR):
            r = q * PAIR + h
            sl = slice(h * PC, (h + 1) * PC)
            dmixed = mm(stack([gh[:, sl], gl[:, sl]], 1), stack([xb[:, sl], xb[:, sl]], 1), NT)
            dscores = dscores + decays(logs, cols, r, lower) * dmixed * step[r : r + 1]
            diff = logs[r : r + 1] - cols[:, r : r + 1]
            mixed_t = jnp.where(upper, jnp.exp(jnp.where(upper, diff, 0.0)), 0.0) * scores_t
            inner.append(mm_halves(split(mixed_t), (gh[:, sl], gl[:, sl])))
        v = jnp.concatenate(inner, axis=1)
        gx_out[:, two_lanes(q)] = both_cols(cols, q, 2 * HD) * v + d[q] * gy
        xv += pair_sums(xq * v)
        eg = both_cols(cols, q, HD) * gy
        dc = dc + mm_both(eg, both(enter, q, 0, NS), NT)
        put(send, q, 0, NS, mm_right(c_t, eg))
        leaving = decay[q] * both(enter, q, 0, NS) + both(own, q, 0, NS)
        put(send, q, NS, 2 * NS, near[q] * leaving - mm_right(b_t, xq * both_cols(cols, q, 3 * HD)))
    maps[0] = mm_left(dscores.T, c[...])
    maps[1] = dc + mm_left(dscores, b[...])
    xv = rows_of(xv)
    after = (iota((CHUNK, CHUNK), 0) >= iota((CHUNK, CHUNK), 1)).astype(F32)
    dla = jnp.dot(rows_of(dots) - step * xv, after, precision=lax.Precision.HIGHEST, preferred_element_type=F32)
    small[:HD] = dla
    small[HD:] = xv
    alogs = jnp.sum(dla * la, axis=1, keepdims=True)
    for r in range(HD):
        gain_row = shared[r // PAIR][:, r % PAIR * PC : (r % PAIR + 1) * PC]
        row = halved(over(skips[r]), over(alogs[r : r + 1]))
        send[r, 2 * NS :, :] = jnp.concatenate([gain_row, row, jnp.zeros((6, WIDE), F32)], axis=0)


def group_back_body(got, own, back, send):
    grad = got[GROUP - 1, :NS, :]
    tangent = got[GROUP - 1, NS : 2 * NS, :]
    reach = own[GROUP - 1, NS : NS + 1, :]
    back[GROUP - 1] = jnp.zeros((NS, WIDE), F32)
    extra = got[GROUP - 1, 2 * NS : 2 * NS + 2, :]
    cross = jnp.zeros((1, WIDE), F32)
    for k in reversed(range(GROUP - 1)):
        q = got[k, NS : 2 * NS, :]
        back[k] = grad
        cross = cross + jnp.sum(grad * q, axis=0, keepdims=True)
        tangent = tangent + reach * q
        extra = extra + got[k, 2 * NS : 2 * NS + 2, :]
        decay = own[k, NS : NS + 1, :]
        reach = reach * decay
        grad = decay * grad + got[k, :NS, :]
    laps = send.shape[0]
    tiles = NS // laps // SUB
    to_slices(send, 0, grad)
    to_slices(send, tiles, tangent)
    scalars = extra[1:] + halved(jnp.zeros((1, WIDE), F32), over(head_sums(cross)[0]))
    tail = jnp.concatenate([extra[:1], scalars], axis=0)
    for lap in range(laps):
        send[lap, :, 2 * tiles * PC :] = tail


def leave_body(late, done, back, own, send, flat):
    from_slices(late, flat)
    grad = flat[...]
    at = late.shape[2] - PC
    alog = late[0, :, at:]
    for lap in range(1, late.shape[0]):
        alog = alog + late[lap, :, at:]
    alog = jnp.sum(jnp.sum(alog, axis=0, keepdims=True), axis=1, keepdims=True) + done[1:, PC - 1 :]
    extra = jnp.concatenate([done[:1], over(done[1:, :1]), over(alog), jnp.zeros((5, WIDE), F32)], axis=0)
    reach = jnp.ones((1, WIDE), F32)
    for k in reversed(range(GROUP)):
        send[k, :NS, :] = back[k] + reach * grad
        send[k, NS:, :] = extra
        reach = reach * own[k, NS : NS + 1, :]


def input_back_body(x, b, tok, gx_in, small, maps, enter, own, late, gx, ddt, gain, alog, skip, send):
    raw, step, rate = table(tok, T_RAW), table(tok, T_STEP), table(tok, T_RATE)
    logs = table(tok, T_LOGS)
    total = last(logs)
    cols = columns(jnp.exp(total - logs), step)
    decay = pairs_of(jnp.exp(total))
    db = maps[0]
    ends, xv = [], []
    lane = iota((1, HD), 1)
    a = jnp.zeros((1, HD), F32)
    s = jnp.zeros((1, HD), F32)
    for q in range(HD // PAIR):
        grad = both(late, q, 0, NS)
        xq = x[:, two_lanes(q)].astype(F32)
        tail = both_cols(cols, q)
        stepc = both_cols(cols, q, HD)
        v = tail * mm_right(b[...], grad)
        gx[:, two_lanes(q)] = (gx_in[:, two_lanes(q)] + stepc * v).astype(BF16)
        db = db + mm_both(tail * stepc * xq, grad, NT)
        xv += pair_sums(xq * v)
        leaving = decay[q] * both(enter, q, 0, NS) + both(own, q, 0, NS)
        ends += whole_sums(grad * leaving)
        gain[:, two_lanes(q)] = both(late, q, NS, NS + 1)
        for h in range(PAIR):
            r = q * PAIR + h
            s = jnp.where(lane == r, late[r, NS + 1 : NS + 2, :1], s)
            a = jnp.where(lane == r, late[r, NS + 2 : NS + 3, :1], a)
    alog[...] = a
    skip[...] = s
    xv = rows_of(xv)
    after = (iota((CHUNK, CHUNK), 0) >= iota((CHUNK, CHUNK), 1)).astype(F32)
    dla = jnp.dot(-step * xv, after, precision=lax.Precision.HIGHEST, preferred_element_type=F32)
    dla = small[:HD] + dla + jnp.concatenate(ends, axis=0)
    ddt[...] = (dla * rate + small[HD:] + xv) * sigmoid(raw)
    ranks = send.shape[0]
    rows = CHUNK // ranks
    for j in range(ranks):
        send[j, :rows, :] = db[j * rows : (j + 1) * rows]
        send[j, rows:, :] = maps[1, j * rows : (j + 1) * rows, :]


def sum_body(got, out):
    total = got[0]
    for q in range(1, got.shape[0]):
        total = total + got[q]
    out[...] = jnp.broadcast_to(total[None], out.shape)


def maps_body(got, db, dc):
    ranks = got.shape[0]
    rows = CHUNK // ranks
    for i in range(ranks):
        db[i * rows : (i + 1) * rows, :] = got[i, :rows, :]
        dc[i * rows : (i + 1) * rows, :] = got[i, rows:, :]


def call(body, ins, outs, scratch=(), limit=LIMIT):
    out = pl.pallas_call(
        body,
        in_specs=ins,
        out_specs=[VMEM] * len(outs),
        out_shape=[jax.ShapeDtypeStruct(s, t) for s, t in outs],
        scratch_shapes=scratch,
        compiler_params=pltpu.CompilerParams(vmem_limit_bytes=limit),
    )
    return out


def swap(a, axis):
    return lax.all_to_all(a, axis, 0, 0, tiled=True)


def shards(
    grad_full, keep, router_score, x_in, z_in, b_in, c_in, dt_raw, dt_bias, a_log, d_skip, norm_gain, state_in,
):
    laps = lax.axis_size("z")
    ranks = lax.axis_size("head")
    heads = dt_raw.shape[1]
    width = x_in.shape[1]
    total_width = width * ranks
    block_len = grad_full.shape[0] // keep.shape[0]
    states = ((GROUP, NS, WIDE), F32)
    slab = ((CHUNK, width), F32)
    tile = NS // laps // SUB * PC
    bind = functools.partial
    dma = pltpu.SemaphoreType.DMA
    router = router_score.reshape(1, CHUNK)
    gain = norm_gain.reshape(1, width)
    flat = pltpu.VMEM((NS, WIDE), F32)

    own, tok = call(
        own_state_body, [ANY] * 6, [((GROUP, ROWS_S, WIDE), F32), ((ROWS_T, CHUNK), F32)],
        [
            pltpu.VMEM((CHUNK, width), BF16), pltpu.VMEM((CHUNK, NS), BF16), pltpu.VMEM((heads, CHUNK), F32),
            pltpu.SMEM((heads,), F32), pltpu.SMEM((heads,), F32), pltpu.SMEM((heads,), F32),
            dma((6,)),
        ], FULL,
    )(x_in, b_in, dt_raw.T, dt_bias, a_log, d_skip)
    group = swap(own, "y")
    part, send = call(group_state_body, [VMEM], [states, ((laps, SUB, tile + PC), F32)])(group)
    send, decay = call(
        scan_body, [VMEM] * 2, [((laps, SUB, tile), F32), ((laps, SUB, PC), F32)],
        [pltpu.VMEM((NS, PC), F32), pltpu.VMEM((SUB, tile), F32)],
    )(swap(send, "z"), state_in)
    (enter,) = call(enter_body, [VMEM] * 3, [states], [flat])(swap(send, "z"), group, part)
    enter = swap(enter, "y")

    y, up, stats = call(bind(output_body, block_len), [VMEM] * 9, [slab, slab, ((ranks, 2, CHUNK), F32)])(
        x_in, b_in, c_in, z_in, grad_full, keep, gain, tok, enter
    )
    grad_z, gx, send, small, maps, router_grad = call(
        bind(output_back_body, total_width), [VMEM] * 12,
        [
            ((CHUNK, width), BF16), slab, ((GROUP, ROWS_G, WIDE), F32), ((2 * HD, CHUNK), F32),
            ((2, CHUNK, NS), F32), ((1, CHUNK), F32),
        ],
    )(swap(stats, "head"), x_in, b_in, c_in, z_in, up, gain, router, tok, enter, own, y)
    back, send = call(group_back_body, [VMEM] * 2, [states, ((laps, SUB, 2 * tile + PC), F32)])(
        swap(send, "y"), group
    )
    send, done = call(scan_back_body, [VMEM] * 2, [((laps, SUB, tile + PC), F32), ((SUB, PC), F32)])(
        swap(send, "z"), decay
    )
    (late,) = call(leave_body, [VMEM] * 4, [((GROUP, ROWS_S, WIDE), F32)], [flat])(
        swap(send, "z"), done, back, group
    )
    piece = ((ranks, 2 * CHUNK // ranks, NS), F32)
    grad_x, ddt, grad_gain, grad_alog, grad_skip, send = call(
        input_back_body, [VMEM] * 9,
        [
            ((CHUNK, width), BF16), ((heads, CHUNK), F32), ((1, width), F32), ((1, heads), F32),
            ((1, heads), F32), piece,
        ],
    )(x_in, b_in, tok, gx, small, maps, enter, own, swap(late, "y"))
    (send,) = call(sum_body, [VMEM], [piece])(swap(send, "head"))
    grad_b, grad_c = call(maps_body, [VMEM], [((CHUNK, NS), F32)] * 2)(swap(send, "head"))
    return (
        grad_x,
        grad_z,
        grad_b,
        grad_c,
        ddt.T,
        router_grad.reshape(CHUNK),
        grad_gain.reshape(width),
        grad_alog.reshape(heads),
        grad_skip.reshape(heads),
    )


def solution(mesh):
    count, heads = mesh.devices.shape
    inner = Mesh(mesh.devices.reshape(count // GROUP, GROUP, heads), ("z", "y", "head"))
    seq = ("z", "y")
    in_specs = (
        P(seq, "head"),
        P(seq, None),
        P(seq),
        P(seq, "head"),
        P(seq, "head"),
        P(seq, None),
        P(seq, None),
        P(seq, "head"),
        P("head"),
        P("head"),
        P("head"),
        P("head"),
        P("head", None, None),
    )
    out_specs = (
        P(seq, "head"),
        P(seq, "head"),
        P(seq, None),
        P(seq, None),
        P(seq, "head"),
        P(seq),
        P("head"),
        P("head"),
        P("head"),
    )
    return jax.shard_map(shards, mesh=inner, in_specs=in_specs, out_specs=out_specs, check_vma=False)
```

```python
import functools

import jax
import jax.numpy as jnp
import numpy as np
from jax import lax
from jax.experimental import pallas as pl
from jax.experimental.pallas import tpu as pltpu
from jax.sharding import Mesh
from jax.sharding import PartitionSpec as P

EPS = 1e-05
GROUP = 8
CHUNK = 128
HP = 1
PAIR = 2
SUB = 2
PC = 128
NS = 128
WIDE = HP * PC
F32 = jnp.float32
BF16 = jnp.bfloat16
NN = ((1,), (0,))
NT = ((1,), (1,))

HD = GROUP * HP
ROWS_S = NS + 8
ROWS_G = 2 * NS + 8

VMEM = pl.BlockSpec(memory_space=pltpu.VMEM)
SMEM = pl.BlockSpec(memory_space=pltpu.SMEM)
ANY = pl.BlockSpec(memory_space=pl.ANY)
LIMIT = 24 * 2**20
FULL = 56 * 2**20


def mm(a, b, dims=NN):
    return lax.dot_general(a, b, (dims, ((), ())), preferred_element_type=F32)


def split(a):
    high = a.astype(BF16)
    return high, (a - high.astype(F32)).astype(BF16)


def stack(parts, dim):
    return jnp.concatenate(parts, axis=dim)


def mm_left(a, exact, dims=NN):
    return mm(stack(split(a), 1), stack([exact, exact], dims[1][0]), dims)


def mm_right(exact, b, dims=NN):
    return mm(stack([exact, exact], 1), stack(split(b), dims[1][0]), dims)


def mm_halves(a, b, dims=NN):
    (ah, al), (bh, bl) = a, b
    return mm(stack([ah, al], 1), stack([bh, bh], dims[1][0]), dims) + mm(ah, bl, dims)


def mm_both(a, b, dims=NN):
    return mm_halves(split(a), split(b), dims)


def iota(shape, dim):
    return lax.broadcasted_iota(jnp.int32, shape, dim)


def softplus(v):
    return jnp.maximum(v, 0.0) + jnp.log1p(jnp.exp(-jnp.abs(v)))


def sigmoid(v):
    return 1.0 / (1.0 + jnp.exp(-v))


def head_col(ref):
    row = iota((HD, 1), 0)
    out = jnp.zeros((HD, 1), F32)
    for h in range(HD):
        out = jnp.where(row == h, ref[h], out)
    return out


T_RAW, T_STEP, T_LA, T_LOGS, T_RATE, T_SKIP, ROWS_T = (HD * i for i in range(7))


def table(tok, at):
    return tok[at : at + HD, :]


def last(rows):
    return rows[:, CHUNK - 1 :]


def columns(*rows):
    count = sum(r.shape[0] for r in rows)
    return jnp.concatenate(rows + (jnp.zeros((CHUNK - count, CHUNK), F32),), axis=0).T


def rows_of(cols):
    pad = jnp.zeros((CHUNK, CHUNK - len(cols)), F32)
    return jnp.concatenate(list(cols) + [pad], axis=1).T[: len(cols)]


def over(value, rows=1):
    return jnp.broadcast_to(value, (rows, WIDE))


def lanes_of(values):
    return [over(values[q : q + 1]) for q in range(GROUP)]


def head_cols(cols, q, at=0):
    return over(cols[:, at + q : at + q + 1], CHUNK)


def head_sums(a):
    return [jnp.sum(a[:, h * PC : (h + 1) * PC], axis=1, keepdims=True) for h in range(HP)]


def whole_sums(a):
    return pair_sums(jnp.sum(a, axis=0, keepdims=True))


def halved(a, b):
    return jnp.where(iota((1, WIDE), 1) % PC < PC // 2, a, b)


def pairs_of(values):
    return [jnp.concatenate([over(values[r : r + 1]), over(values[r + 1 : r + 2])], axis=1) for r in range(0, HD, PAIR)]


def both_cols(cols, q, at=0):
    c = at + q * PAIR
    return jnp.concatenate([over(cols[:, c : c + 1], CHUNK), over(cols[:, c + 1 : c + 2], CHUNK)], axis=1)


def both(ref, q, lo, hi):
    return jnp.concatenate([ref[q * PAIR, lo:hi, :], ref[q * PAIR + 1, lo:hi, :]], axis=1)


def put(ref, q, lo, hi, value):
    for h in range(PAIR):
        ref[q * PAIR + h, lo:hi, :] = value[:, h * PC : (h + 1) * PC]


def pair_sums(a):
    return [jnp.sum(a[:, h * PC : (h + 1) * PC], axis=1, keepdims=True) for h in range(PAIR)]


def token_sums(a, q):
    shape = (HD, 2 * PAIR * PC)
    ones = (iota(shape, 0) == q * PAIR + iota(shape, 1) // PC % PAIR).astype(BF16)
    return mm(ones, stack(split(a), 1), NT)


def two_lanes(q):
    return slice(q * PAIR * WIDE, (q + 1) * PAIR * WIDE)


def lanes(q):
    return slice(q * WIDE, (q + 1) * WIDE)


def own_state_body(
    x_hbm, b_hbm, dt_hbm, bias_hbm, alog_hbm, skip_hbm, send, tok, x, b, dt_t, bias, alog, skip, sem
):
    copies = [
        pltpu.make_async_copy(src, dst, sem.at[i])
        for i, (src, dst) in enumerate(
            [(dt_hbm, dt_t), (bias_hbm, bias), (alog_hbm, alog), (skip_hbm, skip), (b_hbm, b), (x_hbm, x)]
        )
    ]
    for copy in copies:
        copy.start()
    for copy in copies:
        copy.wait()
    raw = dt_t[...] + head_col(bias)
    step = softplus(raw)
    rate = -jnp.exp(head_col(alog))
    la = step * rate
    upper = (iota((CHUNK, CHUNK), 0) <= iota((CHUNK, CHUNK), 1)).astype(F32)
    logs = jnp.dot(la, upper, precision=lax.Precision.HIGHEST, preferred_element_type=F32)
    for at, value in (
        (T_RAW, raw), (T_STEP, step), (T_LA, la), (T_LOGS, logs), (T_RATE, rate), (T_SKIP, head_col(skip))
    ):
        tok[at : at + HD, :] = jnp.broadcast_to(value, (HD, CHUNK))
    cols = columns(jnp.exp(last(logs) - logs) * step)
    decay = lanes_of(jnp.exp(last(logs)))
    b_t = b[...].astype(F32).T.astype(BF16)
    for q in range(GROUP):
        send[q, :NS, :] = mm_right(b_t, x[:, lanes(q)].astype(F32) * head_cols(cols, q))
        send[q, NS:, :] = jnp.broadcast_to(decay[q], (8, WIDE))


def to_slices(out, at, state):
    rows = NS // out.shape[0]
    for n in range(0, NS, SUB):
        tile = at + n % rows // SUB
        out[n // rows, :, tile * PC : (tile + 1) * PC] = state[n : n + SUB, :]


def from_slices(ref, out):
    rows = NS // ref.shape[0]
    for n in range(0, NS, SUB):
        tile = n % rows // SUB
        out[n : n + SUB, :] = ref[n // rows, :, tile * PC : (tile + 1) * PC]


def group_state_body(got, part, send):
    state = got[0, :NS, :]
    whole = got[0, NS : NS + 1, :]
    part[0] = state
    for k in range(1, GROUP):
        decay = got[k, NS : NS + 1, :]
        state = decay * state + got[k, :NS, :]
        whole = whole * decay
        part[k] = state
    to_slices(send, 0, state)
    for lap in range(send.shape[0]):
        send[lap, :, send.shape[2] - PC :] = jnp.broadcast_to(whole, (SUB, PC))
def spread(row, count):
    return jnp.concatenate([row] * count, axis=1)


def scan_body(got, state_in, out, decay, flat, first):
    laps, _, width = out.shape
    tiles = width // PC
    flat[...] = state_in[lax.axis_index("y")].T
    for j in range(tiles):
        for r in range(SUB):
            row = lax.axis_index("z") * (tiles * SUB) + (j * SUB + r)
            first[r : r + 1, j * PC : (j + 1) * PC] = flat[pl.ds(row, 1), :]
    state = first[...]
    for lap in range(laps):
        out[lap] = state
        factor = got[lap, :, width:]
        decay[lap] = factor
        state = spread(factor, tiles) * state + got[lap, :, :width]


def scan_back_body(got, decay, out, done):
    laps = got.shape[0]
    width = out.shape[2] - PC
    tiles = width // PC
    state = jnp.zeros((SUB, width), F32)
    cross = jnp.zeros((SUB, width), F32)
    total = jnp.zeros((SUB, PC), F32)
    for lap in reversed(range(laps)):
        out[lap, :, :width] = state
        cross = cross + state * got[lap, :, width : 2 * width]
        state = spread(decay[lap], tiles) * state + got[lap, :, :width]
        total = total + got[lap, :, 2 * width :]
    done[...] = total
    extra = cross[:, :PC]
    for j in range(1, tiles):
        extra = extra + cross[:, j * PC : (j + 1) * PC]
    for lap in range(laps):
        out[lap, :, width:] = extra


def enter_body(got, own, part, send, flat):
    from_slices(got, flat)
    state = flat[...]
    send[0] = state
    reach = own[0, NS : NS + 1, :]
    for k in range(1, GROUP):
        send[k] = part[k - 1] + reach * state
        reach = reach * own[k, NS : NS + 1, :]


def decays(logs, cols, r, lower):
    diff = cols[:, r : r + 1] - logs[r : r + 1]
    return jnp.where(lower, jnp.exp(jnp.where(lower, diff, 0.0)), 0.0)


def output_body(block_len, x, b, c, z, grad_full, keep, gain, tok, enter, y_out, up, stats):
    blocks, kept = keep.shape
    for i in range(blocks):
        pick = (iota((kept, block_len), 1) == keep[i : i + 1, :].T).astype(BF16)
        up[i * kept : (i + 1) * kept, :] = mm(pick, grad_full[i * block_len : (i + 1) * block_len, :])
    logs, step = table(tok, T_LOGS), table(tok, T_STEP)
    cols = columns(logs, jnp.exp(logs))
    lower = iota((CHUNK, CHUNK), 0) >= iota((CHUNK, CHUNK), 1)
    d = pairs_of(last(table(tok, T_SKIP)))
    scores = mm(c[...], b[...], NT)
    squares = jnp.zeros((CHUNK, PC), F32)
    crosses = jnp.zeros((CHUNK, PC), F32)
    for q in range(HD // PAIR):
        inner = []
        for h in range(PAIR):
            r = q * PAIR + h
            mixed = decays(logs, cols, r, lower) * scores * step[r : r + 1]
            inner.append(mm_left(mixed, x[:, r * PC : (r + 1) * PC]))
        carried = mm_right(c[...], both(enter, q, 0, NS)) * both_cols(cols, q, HD)
        y = jnp.concatenate(inner, axis=1) + carried + d[q] * x[:, two_lanes(q)].astype(F32)
        y_out[:, two_lanes(q)] = y
        zq = z[:, two_lanes(q)].astype(F32)
        gated = y * zq * sigmoid(zq)
        cross = up[:, two_lanes(q)] * gated * gain[:, two_lanes(q)]
        square = gated * gated
        squares = squares + (square[:, :PC] + square[:, PC:])
        crosses = crosses + (cross[:, :PC] + cross[:, PC:])
    squares = jnp.sum(squares, axis=1, keepdims=True)
    crosses = jnp.sum(crosses, axis=1, keepdims=True)
    stats[...] = jnp.broadcast_to(rows_of([squares, crosses])[None], stats.shape)


def output_back_body(
    total_width, stats, x, b, c, z, up, gain, router, tok, enter, own, y_in,
    gz, gx_out, send, small, maps, router_grad,
):
    sums = stats[0]
    for i in range(1, stats.shape[0]):
        sums = sums + stats[i]
    rstd = lax.rsqrt(sums[:1] / total_width + EPS)
    cross = sums[1:]
    router_grad[...] = rstd * cross
    logs, step, la = table(tok, T_LOGS), table(tok, T_STEP), table(tok, T_LA)
    total = last(logs)
    tail = jnp.exp(total - logs)
    cols = columns(
        logs, jnp.exp(logs), step, tail * step * logs,
        rstd * router[...], rstd * rstd * rstd * (router[...] * cross / total_width),
    )
    at_a = 4 * HD
    lower = iota((CHUNK, CHUNK), 0) >= iota((CHUNK, CHUNK), 1)
    upper = iota((CHUNK, CHUNK), 0) <= iota((CHUNK, CHUNK), 1)
    d = pairs_of(last(table(tok, T_SKIP)))
    decay = pairs_of(jnp.exp(total))
    near = pairs_of(total)
    scores_t = mm(b[...], c[...], NT)
    b_t = b[...].astype(F32).T.astype(BF16)
    c_t = c[...].astype(F32).T.astype(BF16)
    dscores = jnp.zeros((CHUNK, CHUNK), F32)
    dc = jnp.zeros((CHUNK, NS), F32)
    shared, skips = [], []
    dots = jnp.zeros((HD, CHUNK), F32)
    xv = jnp.zeros((HD, CHUNK), F32)
    for q in range(HD // PAIR):
        xb = x[:, two_lanes(q)]
        xq, zq, u, y = xb.astype(F32), z[:, two_lanes(q)].astype(F32), up[:, two_lanes(q)], y_in[:, two_lanes(q)]
        sig = sigmoid(zq)
        gate = zq * sig
        gated = y * gate
        scaled = cols[:, at_a : at_a + 1] * u
        gg = scaled * gain[:, two_lanes(q)] - gated * cols[:, at_a + 1 : at_a + 2]
        gz[:, two_lanes(q)] = (gg * y * sig * (1.0 + zq * (1.0 - sig))).astype(BF16)
        gy = gg * gate
        shared.append(jnp.sum(scaled * gated, axis=0, keepdims=True))
        skips += whole_sums(gy * xq)
        dots = dots + token_sums(gy * (y - d[q] * xq), q)
        gh, gl = split(gy)
        inner = []
        for h in range(PAIR):
            r = q * PAIR + h
            sl = slice(h * PC, (h + 1) * PC)
            dmixed = mm(stack([gh[:, sl], gl[:, sl]], 1), stack([xb[:, sl], xb[:, sl]], 1), NT)
            dscores = dscores + decays(logs, cols, r, lower) * dmixed * step[r : r + 1]
            diff = logs[r : r + 1] - cols[:, r : r + 1]
            mixed_t = jnp.where(upper, jnp.exp(jnp.where(upper, diff, 0.0)), 0.0) * scores_t
            inner.append(mm_halves(split(mixed_t), (gh[:, sl], gl[:, sl])))
        v = jnp.concatenate(inner, axis=1)
        gx_out[:, two_lanes(q)] = both_cols(cols, q, 2 * HD) * v + d[q] * gy
        xv = xv + token_sums(xq * v, q)
        eg = both_cols(cols, q, HD) * gy
        dc = dc + mm_both(eg, both(enter, q, 0, NS), NT)
        put(send, q, 0, NS, mm_right(c_t, eg))
        leaving = decay[q] * both(enter, q, 0, NS) + both(own, q, 0, NS)
        put(send, q, NS, 2 * NS, near[q] * leaving - mm_right(b_t, xq * both_cols(cols, q, 3 * HD)))
    maps[0] = mm_left(dscores.T, c[...])
    maps[1] = dc + mm_left(dscores, b[...])
    after = (iota((CHUNK, CHUNK), 0) >= iota((CHUNK, CHUNK), 1)).astype(F32)
    dla = jnp.dot(dots - step * xv, after, precision=lax.Precision.HIGHEST, preferred_element_type=F32)
    small[:HD] = dla
    small[HD:] = xv
    alogs = jnp.sum(dla * la, axis=1, keepdims=True)
    for r in range(HD):
        gain_row = shared[r // PAIR][:, r % PAIR * PC : (r % PAIR + 1) * PC]
        row = halved(over(skips[r]), over(alogs[r : r + 1]))
        send[r, 2 * NS :, :] = jnp.concatenate([gain_row, row, jnp.zeros((6, WIDE), F32)], axis=0)


def group_back_body(got, own, back, send):
    grad = got[GROUP - 1, :NS, :]
    tangent = got[GROUP - 1, NS : 2 * NS, :]
    reach = own[GROUP - 1, NS : NS + 1, :]
    back[GROUP - 1] = jnp.zeros((NS, WIDE), F32)
    extra = got[GROUP - 1, 2 * NS : 2 * NS + 2, :]
    cross = jnp.zeros((1, WIDE), F32)
    for k in reversed(range(GROUP - 1)):
        q = got[k, NS : 2 * NS, :]
        back[k] = grad
        cross = cross + jnp.sum(grad * q, axis=0, keepdims=True)
        tangent = tangent + reach * q
        extra = extra + got[k, 2 * NS : 2 * NS + 2, :]
        decay = own[k, NS : NS + 1, :]
        reach = reach * decay
        grad = decay * grad + got[k, :NS, :]
    laps = send.shape[0]
    tiles = NS // laps // SUB
    to_slices(send, 0, grad)
    to_slices(send, tiles, tangent)
    scalars = extra[1:] + halved(jnp.zeros((1, WIDE), F32), over(head_sums(cross)[0]))
    tail = jnp.concatenate([extra[:1], scalars], axis=0)
    for lap in range(laps):
        send[lap, :, 2 * tiles * PC :] = tail


def leave_body(late, done, back, own, send, flat):
    from_slices(late, flat)
    grad = flat[...]
    at = late.shape[2] - PC
    alog = late[0, :, at:]
    for lap in range(1, late.shape[0]):
        alog = alog + late[lap, :, at:]
    alog = jnp.sum(jnp.sum(alog, axis=0, keepdims=True), axis=1, keepdims=True) + done[1:, PC - 1 :]
    extra = jnp.concatenate([done[:1], over(done[1:, :1]), over(alog), jnp.zeros((5, WIDE), F32)], axis=0)
    reach = jnp.ones((1, WIDE), F32)
    for k in reversed(range(GROUP)):
        send[k, :NS, :] = back[k] + reach * grad
        send[k, NS:, :] = extra
        reach = reach * own[k, NS : NS + 1, :]


def input_back_body(x, b, tok, gx_in, small, maps, enter, own, late, gx, ddt, gain, alog, skip, send):
    raw, step, rate = table(tok, T_RAW), table(tok, T_STEP), table(tok, T_RATE)
    logs = table(tok, T_LOGS)
    total = last(logs)
    cols = columns(jnp.exp(total - logs), step)
    decay = pairs_of(jnp.exp(total))
    db = maps[0]
    ends = []
    xv = jnp.zeros((HD, CHUNK), F32)
    lane = iota((1, HD), 1)
    a = jnp.zeros((1, HD), F32)
    s = jnp.zeros((1, HD), F32)
    for q in range(HD // PAIR):
        grad = both(late, q, 0, NS)
        xq = x[:, two_lanes(q)].astype(F32)
        tail = both_cols(cols, q)
        stepc = both_cols(cols, q, HD)
        v = tail * mm_right(b[...], grad)
        gx[:, two_lanes(q)] = (gx_in[:, two_lanes(q)] + stepc * v).astype(BF16)
        db = db + mm_both(tail * stepc * xq, grad, NT)
        xv = xv + token_sums(xq * v, q)
        leaving = decay[q] * both(enter, q, 0, NS) + both(own, q, 0, NS)
        ends += whole_sums(grad * leaving)
        gain[:, two_lanes(q)] = both(late, q, NS, NS + 1)
        for h in range(PAIR):
            r = q * PAIR + h
            s = jnp.where(lane == r, late[r, NS + 1 : NS + 2, :1], s)
            a = jnp.where(lane == r, late[r, NS + 2 : NS + 3, :1], a)
    alog[...] = a
    skip[...] = s
    after = (iota((CHUNK, CHUNK), 0) >= iota((CHUNK, CHUNK), 1)).astype(F32)
    dla = jnp.dot(-step * xv, after, precision=lax.Precision.HIGHEST, preferred_element_type=F32)
    dla = small[:HD] + dla + jnp.concatenate(ends, axis=0)
    ddt[...] = (dla * rate + small[HD:] + xv) * sigmoid(raw)
    ranks = send.shape[0]
    rows = CHUNK // ranks
    for j in range(ranks):
        send[j, :rows, :] = db[j * rows : (j + 1) * rows]
        send[j, rows:, :] = maps[1, j * rows : (j + 1) * rows, :]


def sum_body(got, out):
    total = got[0]
    for q in range(1, got.shape[0]):
        total = total + got[q]
    out[...] = jnp.broadcast_to(total[None], out.shape)


def maps_body(got, db, dc):
    ranks = got.shape[0]
    rows = CHUNK // ranks
    for i in range(ranks):
        db[i * rows : (i + 1) * rows, :] = got[i, :rows, :]
        dc[i * rows : (i + 1) * rows, :] = got[i, rows:, :]


def call(body, ins, outs, scratch=(), limit=LIMIT):
    out = pl.pallas_call(
        body,
        in_specs=ins,
        out_specs=[VMEM] * len(outs),
        out_shape=[jax.ShapeDtypeStruct(s, t) for s, t in outs],
        scratch_shapes=scratch,
        compiler_params=pltpu.CompilerParams(vmem_limit_bytes=limit),
    )
    return out


def swap(a, axis):
    return lax.all_to_all(a, axis, 0, 0, tiled=True)


def shards(
    grad_full, keep, router_score, x_in, z_in, b_in, c_in, dt_raw, dt_bias, a_log, d_skip, norm_gain, state_in,
):
    laps = lax.axis_size("z")
    ranks = lax.axis_size("head")
    heads = dt_raw.shape[1]
    width = x_in.shape[1]
    total_width = width * ranks
    block_len = grad_full.shape[0] // keep.shape[0]
    states = ((GROUP, NS, WIDE), F32)
    slab = ((CHUNK, width), F32)
    tile = NS // laps // SUB * PC
    bind = functools.partial
    dma = pltpu.SemaphoreType.DMA
    router = router_score.reshape(1, CHUNK)
    gain = norm_gain.reshape(1, width)
    flat = pltpu.VMEM((NS, WIDE), F32)

    own, tok = call(
        own_state_body, [ANY] * 6, [((GROUP, ROWS_S, WIDE), F32), ((ROWS_T, CHUNK), F32)],
        [
            pltpu.VMEM((CHUNK, width), BF16), pltpu.VMEM((CHUNK, NS), BF16), pltpu.VMEM((heads, CHUNK), F32),
            pltpu.SMEM((heads,), F32), pltpu.SMEM((heads,), F32), pltpu.SMEM((heads,), F32),
            dma((6,)),
        ], FULL,
    )(x_in, b_in, dt_raw.T, dt_bias, a_log, d_skip)
    group = swap(own, "y")
    part, send = call(group_state_body, [VMEM], [states, ((laps, SUB, tile + PC), F32)])(group)
    send, decay = call(
        scan_body, [VMEM] * 2, [((laps, SUB, tile), F32), ((laps, SUB, PC), F32)],
        [pltpu.VMEM((NS, PC), F32), pltpu.VMEM((SUB, tile), F32)],
    )(swap(send, "z"), state_in)
    (enter,) = call(enter_body, [VMEM] * 3, [states], [flat])(swap(send, "z"), group, part)
    enter = swap(enter, "y")

    y, up, stats = call(bind(output_body, block_len), [VMEM] * 9, [slab, slab, ((ranks, 2, CHUNK), F32)])(
        x_in, b_in, c_in, z_in, grad_full, keep, gain, tok, enter
    )
    grad_z, gx, send, small, maps, router_grad = call(
        bind(output_back_body, total_width), [VMEM] * 12,
        [
            ((CHUNK, width), BF16), slab, ((GROUP, ROWS_G, WIDE), F32), ((2 * HD, CHUNK), F32),
            ((2, CHUNK, NS), F32), ((1, CHUNK), F32),
        ],
    )(swap(stats, "head"), x_in, b_in, c_in, z_in, up, gain, router, tok, enter, own, y)
    back, send = call(group_back_body, [VMEM] * 2, [states, ((laps, SUB, 2 * tile + PC), F32)])(
        swap(send, "y"), group
    )
    send, done = call(scan_back_body, [VMEM] * 2, [((laps, SUB, tile + PC), F32), ((SUB, PC), F32)])(
        swap(send, "z"), decay
    )
    (late,) = call(leave_body, [VMEM] * 4, [((GROUP, ROWS_S, WIDE), F32)], [flat])(
        swap(send, "z"), done, back, group
    )
    piece = ((ranks, 2 * CHUNK // ranks, NS), F32)
    grad_x, ddt, grad_gain, grad_alog, grad_skip, send = call(
        input_back_body, [VMEM] * 9,
        [
            ((CHUNK, width), BF16), ((heads, CHUNK), F32), ((1, width), F32), ((1, heads), F32),
            ((1, heads), F32), piece,
        ],
    )(x_in, b_in, tok, gx, small, maps, enter, own, swap(late, "y"))
    (send,) = call(sum_body, [VMEM], [piece])(swap(send, "head"))
    grad_b, grad_c = call(maps_body, [VMEM], [((CHUNK, NS), F32)] * 2)(swap(send, "head"))
    return (
        grad_x,
        grad_z,
        grad_b,
        grad_c,
        ddt.T,
        router_grad.reshape(CHUNK),
        grad_gain.reshape(width),
        grad_alog.reshape(heads),
        grad_skip.reshape(heads),
    )


def solution(mesh):
    count, heads = mesh.devices.shape
    inner = Mesh(mesh.devices.reshape(count // GROUP, GROUP, heads), ("z", "y", "head"))
    seq = ("z", "y")
    in_specs = (
        P(seq, "head"),
        P(seq, None),
        P(seq),
        P(seq, "head"),
        P(seq, "head"),
        P(seq, None),
        P(seq, None),
        P(seq, "head"),
        P("head"),
        P("head"),
        P("head"),
        P("head"),
        P("head", None, None),
    )
    out_specs = (
        P(seq, "head"),
        P(seq, "head"),
        P(seq, None),
        P(seq, None),
        P(seq, "head"),
        P(seq),
        P("head"),
        P("head"),
        P("head"),
    )
    return jax.shard_map(shards, mesh=inner, in_specs=in_specs, out_specs=out_specs, check_vma=False)
```
